256 devices in a mesh: row: 8 (over z), col: 32 (over x, y, core).
Axes of the slice: x: 4, y: 4, z: 8, core: 2. Of those that a mesh axis runs over, the one named last changes fastest.
Arguments:
- feats: bfloat16 [65536, 256], P(('row', 'col')), may hold values from -6 to 6
- rel_embed: float32 [201, 256], replicated, may hold values from -6 to 6
- weights: float32 [3, 256, 256], replicated, may hold values from -0.046875 to 0.046875
- cot: bfloat16 [65536, 256], P(('col', 'row')), may hold values from -6 to 6
- tile_row: int32 [16384], P(('row', 'col')), may hold values from 0 to 511, as said below
- tile_col: int32 [16384], P(('row', 'col')), may hold values from 0 to 511, as said below
- tile_live: int32 [256], P(('row', 'col')), may hold values from 1 to 64, as said below
- edge_ends: int32 [16384, 256], P(('row', 'col')), may hold values from 0 to 16383
- edge_relation: int32 [16384, 256], P(('row', 'col')), may hold values from 0 to 199
- edge_dir: int32 [16384, 256], P(('row', 'col')), may hold values 0 or 1
- edge_count: int32 [16384], P(('row', 'col')), may hold values from 1 to 256, as said below
Outputs:
- mixed: float32 [65536, 256], P(('col', 'row'))
- grad_feats: float32 [65536, 256], P(('row', 'col'))
- grad_rel: float32 [201, 256], replicated
- grad_weights: float32 [3, 256, 256], replicated
The draws below stay inside these ranges and needn't reach their ends.
Inputs may be any that keep to these rules, and one draw needn't show every extreme that they name: `tile_row`: the slots of group k = i * 32 + j (j below 32) have block rows from j * 16 up to (j + 1) * 16 - 1. `tile_col`: the slots of group k = i * 32 + j have block columns from i * 64 up to (i + 1) * 64 - 1. `tile_live`: slots at or past the count are padding; some group is full in every draw. `edge_count`: edge slots at or past the count are padding; some tile slot is full in every draw.
All inputs are finite; a program needn't handle non-finite values. No bound on the sum of `edge_dir` on one device may be relied on, other than what follows from the above.
Results may differ from the reference program's by a relative error of at most 0.0003.
Values may be sent and summed in bfloat16 or wider, within the bound.
A program may use at most 128 MiB of HBM per device.

```python
import jax
import jax.numpy as jnp
from jax import lax

D = 256
RELS = 200
TILE = 128
EDGE_TILE = 256
TILE_DEV = 64
ENT_DEV = 256
ENTITIES = 65536
DST_DEV = 2048
SRC_DEV = 8192
RELS_ALL = 201
DEVICES = 256


def draw_tile_row(key, part):
    key = jax.random.fold_in(key, 11)
    slot_ids = jnp.arange(DEVICES * TILE_DEV, dtype=jnp.int32)
    columns = SRC_DEV // ENT_DEV
    column_index = slot_ids // TILE_DEV % columns
    blocks = DST_DEV // TILE
    return column_index * blocks + jax.random.randint(key, (DEVICES * TILE_DEV,), 0, blocks, dtype=jnp.int32)


def draw_tile_col(key, part):
    key = jax.random.fold_in(key, 12)
    slot_ids = jnp.arange(DEVICES * TILE_DEV, dtype=jnp.int32)
    columns = SRC_DEV // ENT_DEV
    row_index = slot_ids // TILE_DEV // columns
    blocks = SRC_DEV // TILE
    return row_index * blocks + jax.random.randint(key, (DEVICES * TILE_DEV,), 0, blocks, dtype=jnp.int32)


def draw_tile_live(key, part):
    key = jax.random.fold_in(key, 13)
    key_counts, key_full = jax.random.split(key)
    counts = jax.random.randint(key_counts, (DEVICES,), 1, TILE_DEV + 1, dtype=jnp.int32)
    busiest = jax.random.randint(key_full, (), 0, DEVICES, dtype=jnp.int32)
    return counts.at[busiest].set(TILE_DEV)


def draw_edge_count(key, part):
    key = jax.random.fold_in(key, 14)
    key_counts, key_full = jax.random.split(key)
    counts = jax.random.randint(key_counts, (DEVICES * TILE_DEV,), 1, EDGE_TILE + 1, dtype=jnp.int32)
    fullest = jax.random.randint(key_full, (), 0, DEVICES * TILE_DEV, dtype=jnp.int32)
    return counts.at[fullest].set(EDGE_TILE)


def set_ends(entries, stream_key, least, top_value):
    place = [jax.random.randint(jax.random.fold_in(stream_key, axis), (), 0, length) for axis, length in enumerate(entries.shape)]
    longest = entries.shape.index(max(entries.shape))
    next_to = place[:longest] + [(place[longest] + 1) % entries.shape[longest]] + place[longest + 1:]
    return entries.at[tuple(place)].set(least).at[tuple(next_to)].set(top_value)


def shard_levels(key, shape, pieces, smallest, top_value):
    factor_of, own = 1.0, jax.random.fold_in(key, 6)
    for axis_at, parts in pieces:
        draws = jnp.exp(jax.random.uniform(jax.random.fold_in(own, axis_at), (parts,), jnp.float32, smallest / len(pieces), top_value / len(pieces)))
        factor_of = factor_of * jnp.repeat(draws, shape[axis_at] // parts).reshape([-1 if axis == axis_at else 1 for axis in range(len(shape))])
    return factor_of


def noise(own_key, extent, deviation, reach, cuts=(), kind=jnp.bfloat16):
    factor_of = shard_levels(own_key, extent, cuts, -0.22, 0.18) if cuts else 1.0
    result = jax.random.normal(own_key, extent, jnp.float32) * deviation * factor_of
    return jnp.minimum(jnp.maximum(result, -reach), reach).astype(kind)


def setup_inputs(seed: int = 0) -> dict:
    splits = jax.random.split(jax.random.key(seed), 12)
    return {
        "feats": noise(splits[0], (ENTITIES, D), 1.0, 6.0, ((0, 256),)),
        "rel_embed": noise(splits[1], (RELS_ALL, D), 1.0, 6.0, (), jnp.float32),
        "weights": noise(splits[2], (3, D, D), (D * 64) ** -0.5, 0.046875, (), jnp.float32),
        "cot": noise(splits[3], (ENTITIES, D), 1.0, 6.0, ((0, 256),)),
        "tile_row": draw_tile_row(jax.random.fold_in(splits[11], 71), 0),
        "tile_col": draw_tile_col(jax.random.fold_in(splits[11], 71), 0),
        "tile_live": draw_tile_live(jax.random.fold_in(splits[11], 71), 0),
        "edge_ends": set_ends(jax.random.randint(splits[7], (DEVICES * TILE_DEV, EDGE_TILE), 0, TILE * TILE), jax.random.fold_in(splits[7], 1), 0, (TILE * TILE) - 1).astype(jnp.int32),
        "edge_relation": set_ends(jax.random.randint(splits[8], (DEVICES * TILE_DEV, EDGE_TILE), 0, RELS), jax.random.fold_in(splits[8], 1), 0, RELS - 1).astype(jnp.int32),
        "edge_dir": set_ends((jax.random.randint(splits[9], (DEVICES * TILE_DEV, EDGE_TILE), 0, 2) < 1).astype(jnp.int32), jax.random.fold_in(splits[9], 1), 0, 1),
        "edge_count": draw_edge_count(jax.random.fold_in(splits[11], 71), 0),
    }


def product(left, right):
    return jnp.dot(left, right, precision=lax.Precision.HIGHEST, preferred_element_type=jnp.float32)


def reference(feats, rel_embed, weights, cot, tile_row, tile_col, tile_live, edge_ends, edge_relation, edge_dir, edge_count):
    entities = feats.shape[0]
    feats_f = feats.astype(jnp.float32)
    rows_b = tile_row.reshape(DEVICES, TILE_DEV)
    cols_b = tile_col.reshape(DEVICES, TILE_DEV)
    counts_b = edge_count.reshape(DEVICES, TILE_DEV)
    ends_b = edge_ends.reshape(DEVICES, TILE_DEV, EDGE_TILE)
    rels_b = edge_relation.reshape(DEVICES, TILE_DEV, EDGE_TILE)
    dirs_b = edge_dir.reshape(DEVICES, TILE_DEV, EDGE_TILE)

    def device_edges(index):
        live_slot = jnp.arange(TILE_DEV, dtype=jnp.int32) < tile_live[index]
        live_edge = (jnp.arange(EDGE_TILE, dtype=jnp.int32)[None, :] < counts_b[index][:, None]) & live_slot[:, None]
        ends = ends_b[index]
        target = (rows_b[index][:, None] * TILE + ends // TILE).reshape(-1).astype(jnp.int32)
        source = (cols_b[index][:, None] * TILE + ends % TILE).reshape(-1).astype(jnp.int32)
        relation = rels_b[index].reshape(-1).astype(jnp.int32)
        direction = dirs_b[index].reshape(-1).astype(jnp.int32)
        return target, source, relation, direction, live_edge.reshape(-1).astype(jnp.float32)

    def forward_step(carry, index):
        target, source, relation, direction, valid = device_edges(index)
        message = (feats_f[source] - rel_embed[relation]) * valid[:, None]
        return carry.at[direction * entities + target].add(message), None

    totals, _ = lax.scan(forward_step, jnp.zeros((2 * entities, D), jnp.float32), jnp.arange(DEVICES, dtype=jnp.int32))
    totals = totals.reshape(2, entities, D)
    self_term = feats_f - rel_embed[RELS]
    mixed = product(totals[0], weights[0]) + product(totals[1], weights[1]) + product(self_term, weights[2])
    cot_f = cot.astype(jnp.float32)
    images = jnp.stack([product(cot_f, weights[which].T) for which in range(3)])
    images_flat = images[:2].reshape(2 * entities, D)

    def backward_step(carry, index):
        grad_in, grad_edges = carry
        target, source, relation, direction, valid = device_edges(index)
        selected_rows = images_flat[direction * entities + target] * valid[:, None]
        return (grad_in.at[source].add(selected_rows), grad_edges.at[relation].add(-selected_rows)), None

    start_rel = jnp.zeros((RELS_ALL, D), jnp.float32).at[RELS].set(-jnp.sum(images[2], axis=0))
    (grad_feats, grad_rel), _ = lax.scan(backward_step, (images[2], start_rel), jnp.arange(DEVICES, dtype=jnp.int32))
    grad_weights = jnp.stack([product(totals[0].T, cot_f), product(totals[1].T, cot_f), product(self_term.T, cot_f)])
    return mixed, grad_feats, grad_rel, grad_weights
```

```python
import functools

import jax
import jax.numpy as jnp
from jax import lax
from jax.experimental import pallas as pl
from jax.experimental.pallas import tpu as pltpu
from jax.sharding import PartitionSpec as P

D = 256
TILE = 128
EDGE_TILE = 256
PAIR = 2 * TILE
RELS_PAD = 256
NONE = 1024
F32 = jnp.float32
BF16 = jnp.bfloat16
NN = (((1,), (0,)), ((), ()))
NT = (((1,), (1,)), ((), ()))
TN = (((0,), (0,)), ((), ()))


def dot(left, right, dims=NN):
    return lax.dot_general(left, right, dims, preferred_element_type=F32)


def split(value):
    high = value.astype(BF16)
    return high, (value - high.astype(F32)).astype(BF16)


def dot_exact_left(left, right, dims=NN):
    high, low = right
    return dot(left, high, dims) + dot(left, low, dims)


def dot_exact_right(left, right, dims=NN):
    high, low = left
    return dot(high, right, dims) + dot(low, right, dims)


def dot_split(left, right, dims=NN):
    return dot(left[0], right[0], dims) + (dot(left[0], right[1], dims) + dot(left[1], right[0], dims))


def rows_at(index, size):
    return pl.ds(pl.multiple_of(index * size, size), size)


def tiles_kernel(
    meta_ref,
    row_ref,
    col_ref,
    count_ref,
    ends_ref,
    relation_ref,
    dir_ref,
    feats_ref,
    cot_ref,
    rel_ref,
    weights_ref,
    grad_ref,
    mixed_ref,
    grad_weights_ref,
    grad_rel_ref,
    key_ref,
    src_ref,
    totals_ref,
    counts_ref,
    high_ref,
    low_ref,
):
    slots = ends_ref.shape[0]
    blocks = cot_ref.shape[0] // TILE
    rels_all = meta_ref[3]
    slot_iota = lax.broadcasted_iota(jnp.int32, (slots, EDGE_TILE), 0)
    edge_iota = lax.broadcasted_iota(jnp.int32, (slots, EDGE_TILE), 1)
    valid = (edge_iota < count_ref[...]) & (slot_iota < meta_ref[0])
    ends = ends_ref[...]
    key_ref[...] = jnp.where(valid, dir_ref[...] * TILE + lax.shift_right_logical(ends, 7), NONE)
    src_ref[...] = ends & (TILE - 1)

    weight = [split(weights_ref[which]) for which in range(3)]

    def image_block(block, _):
        cot = cot_ref[rows_at(block, TILE), :]
        pair = [dot_exact_left(cot, weight[which], NT) for which in range(2)]
        high, low = split(jnp.concatenate(pair, axis=0))
        at = rows_at(block, PAIR)
        high_ref[at, :] = high
        low_ref[at, :] = low
        totals_ref[at, :] = jnp.zeros((PAIR, D), F32)
        counts_ref[at, :] = jnp.zeros((PAIR, RELS_PAD), F32)
        return 0

    lax.fori_loop(0, blocks, image_block, 0)

    def clear_block(block, _):
        grad_ref[rows_at(block, PAIR), :] = jnp.zeros((PAIR, D), F32)
        return 0

    lax.fori_loop(0, grad_ref.shape[0] // PAIR, clear_block, 0)

    pair_iota = lax.broadcasted_iota(jnp.int32, (PAIR, EDGE_TILE), 0)
    tile_iota = lax.broadcasted_iota(jnp.int32, (TILE, EDGE_TILE), 0)

    def hot(iota, entries):
        return jnp.where(iota == entries, 1.0, 0.0).astype(BF16)

    def tile(slot, _):
        at = pl.ds(slot, 1)
        hot_dst = hot(pair_iota, key_ref[at, :])
        hot_src = hot(tile_iota, src_ref[at, :])
        hot_rel = hot(pair_iota, relation_ref[at, :])
        forward = dot(hot_dst, hot_src, NT).astype(BF16)
        backward = dot(hot_src, hot_dst, NT).astype(BF16)
        counted = dot(hot_dst, hot_rel, NT)
        row = rows_at(row_ref[slot], PAIR)
        col = rows_at(col_ref[slot], TILE)
        counts_ref[row, :] += counted
        totals_ref[row, :] += dot(forward, feats_ref[col, :])
        grad_ref[col, :] += dot(backward, high_ref[row, :]) + dot(backward, low_ref[row, :])
        return 0

    lax.fori_loop(0, slots, tile, 0, unroll=2)

    relations = split(rel_ref[...])
    grad_weights_ref[...] = jnp.zeros_like(grad_weights_ref)
    grad_rel_ref[...] = jnp.zeros_like(grad_rel_ref)

    def finish_block(block, _):
        at = rows_at(block, PAIR)
        counts = split(counts_ref[at, :])
        high, low = high_ref[at, :], low_ref[at, :]
        rel_part = dot(counts[0], high, TN) + (dot(counts[0], low, TN) + dot(counts[1], high, TN))
        grad_rel_ref[...] -= rel_part
        totals = totals_ref[at, :] - dot_split(counts, relations)
        total_in = split(totals[:TILE])
        total_out = split(totals[TILE:])
        here = rows_at(block, TILE)
        mixed_ref[here, :] = dot_split(total_in, weight[0]) + dot_split(total_out, weight[1])
        cot = cot_ref[here, :]
        grad_weights_ref[0] += dot_exact_right(total_in, cot, TN)
        grad_weights_ref[1] += dot_exact_right(total_out, cot, TN)
        return 0

    lax.fori_loop(0, blocks, finish_block, 0)

    @pl.when(meta_ref[1] == 1)
    def _():
        own_rel = rel_ref[pl.ds(rels_all - 1, 1), :]

        def self_block(block, total):
            here = rows_at(block, TILE)
            there = rows_at(meta_ref[2] + block, TILE)
            self_term = split(feats_ref[there, :].astype(F32) - own_rel)
            cot = cot_ref[here, :]
            mixed_ref[here, :] += dot_split(self_term, weight[2])
            grad_weights_ref[2] += dot_exact_right(self_term, cot, TN)
            image = dot_exact_left(cot, weight[2], NT)
            grad_ref[there, :] += image
            return total + jnp.sum(image, axis=0, keepdims=True)

        total = lax.fori_loop(0, blocks, self_block, jnp.zeros((1, D), F32))
        grad_rel_ref[pl.ds(rels_all - 1, 1), :] -= total


def tiles_call(meta, rows, cols, counts, ends, relation, direction, sources, cot, rel, weights):
    dst_dev, src_dev = cot.shape[0], sources.shape[0]
    slots = ends.shape[0]
    smem = pl.BlockSpec(memory_space=pltpu.SMEM)
    vmem = pl.BlockSpec(memory_space=pltpu.VMEM)
    return pl.pallas_call(
        tiles_kernel,
        out_shape=[
            jax.ShapeDtypeStruct((src_dev, D), F32),
            jax.ShapeDtypeStruct((dst_dev, D), F32),
            jax.ShapeDtypeStruct((3, D, D), F32),
            jax.ShapeDtypeStruct((RELS_PAD, D), F32),
        ],
        in_specs=[smem] * 3 + [vmem] * 8,
        out_specs=[vmem] * 4,
        scratch_shapes=[
            pltpu.VMEM((slots, EDGE_TILE), jnp.int32),
            pltpu.VMEM((slots, EDGE_TILE), jnp.int32),
            pltpu.VMEM((2 * dst_dev, D), F32),
            pltpu.VMEM((2 * dst_dev, RELS_PAD), F32),
            pltpu.VMEM((2 * dst_dev, D), BF16),
            pltpu.VMEM((2 * dst_dev, D), BF16),
        ],
        compiler_params=pltpu.CompilerParams(vmem_limit_bytes=56 * 1024 * 1024),
        name="tiles",
    )(meta, rows, cols, counts, ends, relation, direction, sources, cot, rel, weights)


def shards(
    feats,
    rel_embed,
    weights,
    cot,
    tile_row,
    tile_col,
    tile_live,
    edge_ends,
    edge_relation,
    edge_dir,
    edge_count,
):
    rows_n = lax.axis_size("row")
    cols_n = lax.axis_size("col")
    row_index = lax.axis_index("row")
    col_index = lax.axis_index("col")
    ent_dev = feats.shape[0]
    src_dev = ent_dev * cols_n
    dst_dev = ent_dev * rows_n
    rels_all = rel_embed.shape[0]
    sources = lax.all_gather(feats, "col", axis=0, tiled=True)
    targets = lax.all_gather(cot, "row", axis=0, tiled=True)
    owner = (row_index == col_index * rows_n // cols_n).astype(jnp.int32)
    offset = jnp.clip(col_index * dst_dev - row_index * src_dev, 0, src_dev - dst_dev) // TILE
    meta = jnp.stack([tile_live[0], owner, offset.astype(jnp.int32), jnp.int32(rels_all)])
    grad, mixed, grad_weights, grad_rel = tiles_call(
        meta,
        tile_row - col_index * (dst_dev // TILE),
        tile_col - row_index * (src_dev // TILE),
        edge_count[:, None],
        edge_ends,
        edge_relation,
        edge_dir,
        sources,
        targets,
        jnp.pad(rel_embed, ((0, RELS_PAD - rels_all), (0, 0))),
        weights,
    )
    grad_feats = lax.psum_scatter(grad, "col", scatter_dimension=0, tiled=True)
    mixed = lax.psum_scatter(mixed, "row", scatter_dimension=0, tiled=True)
    grad_weights, grad_rel = lax.psum((grad_weights, grad_rel[:rels_all]), ("row", "col"))
    return (mixed, grad_feats, grad_rel, grad_weights)


def solution(mesh):
    return jax.shard_map(
        shards,
        mesh=mesh,
        in_specs=(
            P(("row", "col"), None),
            P(),
            P(),
            P(("col", "row"), None),
            P(("row", "col")),
            P(("row", "col")),
            P(("row", "col")),
            P(("row", "col"), None),
            P(("row", "col"), None),
            P(("row", "col"), None),
            P(("row", "col")),
        ),
        out_specs=(P(("col", "row"), None), P(("row", "col"), None), P(), P()),
        check_vma=False,
    )
```

```python
import functools

import jax
import jax.numpy as jnp
from jax import lax
from jax.experimental import pallas as pl
from jax.experimental.pallas import tpu as pltpu
from jax.sharding import PartitionSpec as P

D = 256
TILE = 128
EDGE_TILE = 256
PAIR = 2 * TILE
RELS_PAD = 256
NONE = 1024
F32 = jnp.float32
BF16 = jnp.bfloat16
NN = (((1,), (0,)), ((), ()))
NT = (((1,), (1,)), ((), ()))
TN = (((0,), (0,)), ((), ()))


def dot(left, right, dims=NN):
    return lax.dot_general(left, right, dims, preferred_element_type=F32)


def split(value):
    high = value.astype(BF16)
    return high, (value - high.astype(F32)).astype(BF16)


def dot_exact_left(left, right, dims=NN):
    high, low = right
    return dot(left, high, dims) + dot(left, low, dims)


def dot_exact_right(left, right, dims=NN):
    high, low = left
    return dot(high, right, dims) + dot(low, right, dims)


def dot_split(left, right, dims=NN):
    return dot(left[0], right[0], dims) + (dot(left[0], right[1], dims) + dot(left[1], right[0], dims))


def rows_at(index, size):
    return pl.ds(pl.multiple_of(index * size, size), size)


def tiles_kernel(
    meta_ref,
    row_ref,
    col_ref,
    count_ref,
    ends_ref,
    relation_ref,
    dir_ref,
    feats_ref,
    cot_ref,
    rel_ref,
    weights_ref,
    grad_ref,
    mixed_ref,
    sums_ref,
    key_ref,
    src_ref,
    totals_ref,
    counts_ref,
    high_ref,
    low_ref,
):
    slots = ends_ref.shape[0]
    blocks = cot_ref.shape[0] // TILE
    rels_all = meta_ref[3]
    slot_iota = lax.broadcasted_iota(jnp.int32, (slots, EDGE_TILE), 0)
    edge_iota = lax.broadcasted_iota(jnp.int32, (slots, EDGE_TILE), 1)
    valid = (edge_iota < count_ref[...]) & (slot_iota < meta_ref[0])
    ends = ends_ref[...]
    key_ref[...] = jnp.where(valid, dir_ref[...] * TILE + lax.shift_right_logical(ends, 7), NONE)
    src_ref[...] = ends & (TILE - 1)

    weight = [split(weights_ref[which]) for which in range(3)]

    def image_block(block, _):
        cot = cot_ref[rows_at(block, TILE), :]
        pair = [dot_exact_left(cot, weight[which], NT) for which in range(2)]
        high, low = split(jnp.concatenate(pair, axis=0))
        at = rows_at(block, PAIR)
        high_ref[at, :] = high
        low_ref[at, :] = low
        totals_ref[at, :] = jnp.zeros((PAIR, D), F32)
        counts_ref[at, :] = jnp.zeros((PAIR, RELS_PAD), F32)
        return 0

    lax.fori_loop(0, blocks, image_block, 0)

    def clear_block(block, _):
        grad_ref[rows_at(block, PAIR), :] = jnp.zeros((PAIR, D), F32)
        return 0

    lax.fori_loop(0, grad_ref.shape[0] // PAIR, clear_block, 0)

    pair_iota = lax.broadcasted_iota(jnp.int32, (PAIR, EDGE_TILE), 0)
    tile_iota = lax.broadcasted_iota(jnp.int32, (TILE, EDGE_TILE), 0)

    def hot(iota, entries):
        return jnp.where(iota == entries, 1.0, 0.0).astype(BF16)

    def tile(slot, _):
        at = pl.ds(slot, 1)
        hot_dst = hot(pair_iota, key_ref[at, :])
        hot_src = hot(tile_iota, src_ref[at, :])
        hot_rel = hot(pair_iota, relation_ref[at, :])
        forward = dot(hot_dst, hot_src, NT).astype(BF16)
        backward = dot(hot_src, hot_dst, NT).astype(BF16)
        counted = dot(hot_dst, hot_rel, NT)
        row = rows_at(row_ref[slot], PAIR)
        col = rows_at(col_ref[slot], TILE)
        counts_ref[row, :] += counted
        totals_ref[row, :] += dot(forward, feats_ref[col, :])
        grad_ref[col, :] += dot(backward, high_ref[row, :]) + dot(backward, low_ref[row, :])
        return 0

    lax.fori_loop(0, slots, tile, 0, unroll=2)

    relations = split(rel_ref[...])
    sums_ref[...] = jnp.zeros_like(sums_ref)
    weights_at = [pl.ds(which * D, D) for which in range(3)]
    rel_at = pl.ds(3 * D, RELS_PAD)

    def finish_block(block, _):
        at = rows_at(block, PAIR)
        counts = split(counts_ref[at, :])
        high, low = high_ref[at, :], low_ref[at, :]
        rel_part = dot(counts[0], high, TN) + (dot(counts[0], low, TN) + dot(counts[1], high, TN))
        sums_ref[rel_at, :] -= rel_part
        totals = totals_ref[at, :] - dot_split(counts, relations)
        total_in = split(totals[:TILE])
        total_out = split(totals[TILE:])
        here = rows_at(block, TILE)
        mixed_ref[here, :] = dot_split(total_in, weight[0]) + dot_split(total_out, weight[1])
        cot = cot_ref[here, :]
        sums_ref[weights_at[0], :] += dot_exact_right(total_in, cot, TN)
        sums_ref[weights_at[1], :] += dot_exact_right(total_out, cot, TN)
        return 0

    lax.fori_loop(0, blocks, finish_block, 0)

    @pl.when(meta_ref[1] == 1)
    def _():
        own_rel = rel_ref[pl.ds(rels_all - 1, 1), :]

        def self_block(block, total):
            here = rows_at(block, TILE)
            there = rows_at(meta_ref[2] + block, TILE)
            self_term = split(feats_ref[there, :].astype(F32) - own_rel)
            cot = cot_ref[here, :]
            mixed_ref[here, :] += dot_split(self_term, weight[2])
            sums_ref[weights_at[2], :] += dot_exact_right(self_term, cot, TN)
            image = dot_exact_left(cot, weight[2], NT)
            grad_ref[there, :] += image
            return total + jnp.sum(image, axis=0, keepdims=True)

        total = lax.fori_loop(0, blocks, self_block, jnp.zeros((1, D), F32))
        sums_ref[pl.ds(3 * D + rels_all - 1, 1), :] -= total


def tiles_call(meta, rows, cols, counts, ends, relation, direction, sources, cot, rel, weights):
    dst_dev, src_dev = cot.shape[0], sources.shape[0]
    slots = ends.shape[0]
    smem = pl.BlockSpec(memory_space=pltpu.SMEM)
    vmem = pl.BlockSpec(memory_space=pltpu.VMEM)
    return pl.pallas_call(
        tiles_kernel,
        out_shape=[
            jax.ShapeDtypeStruct((src_dev, D), F32),
            jax.ShapeDtypeStruct((dst_dev, D), F32),
            jax.ShapeDtypeStruct((3 * D + RELS_PAD, D), F32),
        ],
        in_specs=[smem] * 3 + [vmem] * 8,
        out_specs=[vmem] * 3,
        scratch_shapes=[
            pltpu.VMEM((slots, EDGE_TILE), jnp.int32),
            pltpu.VMEM((slots, EDGE_TILE), jnp.int32),
            pltpu.VMEM((2 * dst_dev, D), F32),
            pltpu.VMEM((2 * dst_dev, RELS_PAD), F32),
            pltpu.VMEM((2 * dst_dev, D), BF16),
            pltpu.VMEM((2 * dst_dev, D), BF16),
        ],
        compiler_params=pltpu.CompilerParams(vmem_limit_bytes=56 * 1024 * 1024),
        name="tiles",
    )(meta, rows, cols, counts, ends, relation, direction, sources, cot, rel, weights)


MESH = pl.DeviceIdType.MESH
RING = 4
HALF = TILE


class Copies:
    def __init__(self, send_sems):
        self.send_sems, self.started = send_sems, []

    def start(self, src, dst, recv, peer):
        copy = pltpu.make_async_remote_copy(
            src_ref=src,
            dst_ref=dst,
            send_sem=self.send_sems.at[len(self.started)],
            recv_sem=recv,
            device_id=peer,
            device_id_type=MESH,
        )
        copy.start()
        self.started.append(copy)

    def received(self, dst, recv):
        pltpu.make_async_remote_copy(
            src_ref=dst,
            dst_ref=dst,
            send_sem=self.send_sems.at[0],
            recv_sem=recv,
            device_id=self.any_peer,
            device_id_type=MESH,
        ).wait_recv()

    def finish(self):
        for copy in self.started:
            copy.wait_send()


class Place:
    def __init__(self):
        self.row = lax.axis_index("row")
        self.col = lax.axis_index("col")
        self.core = self.col % 2
        self.stride1 = 8 - 6 * self.core
        self.stride2 = 10 - self.stride1
        self.p1 = self.col // self.stride1 % RING
        self.p2 = self.col // self.stride2 % RING

    def col_at(self, k1, k2):
        return (self.p1 + k1) % RING * self.stride1 + (self.p2 + k2) % RING * self.stride2 + self.core

    def peer(self, k1, k2):
        return (self.row, self.col_at(k1, k2))

    def partner(self):
        return (self.row, self.col + 1 - 2 * self.core)

    def along_row(self, k, rows):
        return ((self.row + k) % rows, self.col)

    def greet(self, peers):
        barrier = pltpu.get_barrier_semaphore()
        for peer in peers:
            pl.semaphore_signal(barrier, inc=1, device_id=peer, device_id_type=MESH)
        pl.semaphore_wait(barrier, len(peers))


def run_in_order(pipes, order):
    for name in order:
        next(pipes[name], None)
    for pipe in pipes.values():
        for _ in pipe:
            pass


def gather_kernel(rows, feats_ref, cot_ref, sources_ref, targets_ref, send_sems, shard_sems, row_sems, own_sems):
    place = Place()
    copies = Copies(send_sems)
    copies.any_peer = place.partner()
    own_copies = [
        pltpu.make_async_copy(feats_ref, sources_ref.at[place.col], own_sems.at[0]),
        pltpu.make_async_copy(cot_ref, targets_ref.at[place.row], own_sems.at[1]),
    ]
    for copy in own_copies:
        copy.start()
    place.greet(
        [place.partner()]
        + [place.peer(k, 0) for k in (1, 3)]
        + [place.peer(0, k) for k in (1, 3)]
        + [place.along_row(k, rows) for k in (1, rows - 1)]
    )
    parts = [pl.ds(0, HALF), pl.ds(HALF, HALF)]

    def send_shard(b, which, peer, src=None):
        for half in which:
            here = sources_ref.at[b, parts[half]]
            copies.start(here if src is None else src.at[parts[half]], here, shard_sems.at[2 * b + half], peer)

    def got_shard(b, which):
        for half in which:
            copies.received(sources_ref.at[b, parts[half]], shard_sems.at[2 * b + half])

    def feats_pipe():
        for half in (0, 1):
            for peer in (place.peer(1, 0), place.peer(3, 0)):
                send_shard(place.col, [half], peer, feats_ref)
        for peer in (place.peer(0, 1), place.peer(0, 3), place.partner()):
            send_shard(place.col, [0, 1], peer, feats_ref)
        yield

        def spread(b, which):
            for peer in (place.peer(0, 1), place.peer(0, 3)):
                send_shard(b, which, peer)
            send_shard(b, which, place.partner())

        left, right, far = place.col_at(3, 0), place.col_at(1, 0), place.col_at(2, 0)
        got_shard(left, [0])
        send_shard(left, [0], place.peer(1, 0))
        spread(left, [0])
        got_shard(right, [0])
        spread(right, [0])
        got_shard(right, [1])
        send_shard(right, [1], place.peer(3, 0))
        spread(right, [1])
        got_shard(left, [1])
        spread(left, [1])
        yield

        def second(k1):
            below, above = place.col_at(k1, 3), place.col_at(k1, 1)
            got_shard(below, [0])
            send_shard(below, [0], place.peer(0, 1))
            got_shard(above, [0])
            got_shard(above, [1])
            send_shard(above, [1], place.peer(0, 3))
            got_shard(below, [1])
            send_shard(below, [0, 1], place.partner())
            send_shard(above, [0, 1], place.partner())

        second(0)
        yield
        got_shard(far, [0, 1])
        spread(far, [0, 1])
        yield
        second(3)
        yield
        second(1)
        yield
        second(2)
        yield
        for k1 in (0, 3, 1, 2):
            b = place.col_at(k1, 2)
            got_shard(b, [0, 1])
            send_shard(b, [0, 1], place.partner())
        yield
        for k1 in range(RING):
            for k2 in range(RING):
                got_shard(place.col_at(k1, k2) + 1 - 2 * place.core, [0, 1])

    def cot_pipe():
        after, before = place.along_row(1, rows), place.along_row(rows - 1, rows)

        def send_row(index, which, peer, src=None):
            for half in which:
                here = targets_ref.at[index, parts[half]]
                copies.start(here if src is None else src.at[parts[half]], here, row_sems.at[2 * index + half], peer)

        def got_row(index, which):
            for half in which:
                copies.received(targets_ref.at[index, parts[half]], row_sems.at[2 * index + half])

        send_row(place.row, [0, 1], after, cot_ref)
        send_row(place.row, [1, 0], before, cot_ref)
        yield
        for k in range(1, rows // 2):
            last = k == rows // 2 - 1
            low, high = (place.row + rows - k) % rows, (place.row + k) % rows
            got_row(low, [0])
            send_row(low, [0], after)
            got_row(high, [1])
            send_row(high, [1], before)
            got_row(low, [1])
            if not last:
                send_row(low, [1], after)
            got_row(high, [0])
            if not last:
                send_row(high, [0], before)
            yield
        got_row((place.row + rows // 2) % rows, [0, 1])

    run_in_order({"f": feats_pipe(), "c": cot_pipe()}, "fcfcffcffcff")
    for copy in own_copies:
        copy.wait()
    copies.finish()


def gather_call(feats, cot, rows, cols):
    anywhere = pl.BlockSpec(memory_space=pl.ANY)
    vmem = pl.BlockSpec(memory_space=pltpu.VMEM)
    sources, targets = pl.pallas_call(
        functools.partial(gather_kernel, rows),
        out_shape=[
            jax.ShapeDtypeStruct((cols,) + feats.shape, feats.dtype),
            jax.ShapeDtypeStruct((rows,) + cot.shape, cot.dtype),
        ],
        in_specs=[vmem, vmem],
        out_specs=[anywhere, anywhere],
        scratch_shapes=[
            pltpu.SemaphoreType.DMA((160,)),
            pltpu.SemaphoreType.DMA((2 * cols,)),
            pltpu.SemaphoreType.DMA((2 * rows,)),
            pltpu.SemaphoreType.DMA((2,)),
        ],
        compiler_params=pltpu.CompilerParams(
            collective_id=0, has_side_effects=True, vmem_limit_bytes=32 * 1024 * 1024
        ),
        name="gather",
    )(feats, cot)
    return sources.reshape(-1, D), targets.reshape(-1, D)


def reduce_kernel(
    rows,
    grad_any,
    mixed_in,
    sums_in,
    grad_out,
    mixed_out,
    sums_out,
    grad_acc,
    pair_in,
    relay1,
    ring1,
    relay2,
    ring2,
    row_up,
    row_down,
    sum_pair,
    sum_first,
    sum_second,
    sum_rows,
    sum_tiles,
    send_sems,
    own_sems,
    pair_sems,
    ring_sems,
    row_sems,
    sum_sems,
    spread_sems,
):
    place = Place()
    copies = Copies(send_sems)
    copies.any_peer = place.partner()
    partner = place.partner()
    core = place.core
    order1 = (2, 1, 3, 0)
    own_copies = {}
    for k in order1:
        for r in (2, 1, 3, 0):
            block = place.col_at(k, r) // 2
            copy = pltpu.make_async_copy(grad_any.at[block, core], grad_acc.at[k, r], own_sems.at[4 * k + r])
            copy.start()
            own_copies[k, r] = copy
    place.greet(
        [partner]
        + [place.peer(k1, k2) for k1 in range(RING) for k2 in range(RING) if k1 or k2]
        + [place.along_row(k, rows) for k in range(1, rows)]
    )
    low, high = pl.ds(0, HALF), pl.ds(HALF, HALF)

    def grad_pipe():
        for k in order1:
            for r in (2, 1, 3, 0):
                block = ((place.p2 + k) % RING * place.stride2 + (place.p1 + r) % RING * place.stride1) // 2
                copies.start(grad_any.at[block, 1 - core], pair_in.at[k, r], pair_sems.at[4 * k + r], partner)
        yield

        def pair_sum(k, r):
            own_copies[k, r].wait()
            copies.received(pair_in.at[k, r], pair_sems.at[4 * k + r])
            grad_acc[k, r] += pair_in[k, r]

        right, left = place.peer(1, 0), place.peer(3, 0)
        for r in range(RING):
            pair_sum(2, r)
        copies.start(grad_acc.at[2, pl.ds(0, 2)], relay1.at[0], ring_sems.at[0], right)
        copies.start(grad_acc.at[2, pl.ds(2, 2)], relay1.at[1], ring_sems.at[1], left)
        yield
        for r in (2, 3):
            pair_sum(1, r)
        copies.start(grad_acc.at[1, pl.ds(2, 2)], ring1.at[0, pl.ds(2, 2)], ring_sems.at[3], right)
        for r in (0, 1):
            pair_sum(3, r)
        copies.start(grad_acc.at[3, pl.ds(0, 2)], ring1.at[1, pl.ds(0, 2)], ring_sems.at[4], left)
        yield
        for r in (0, 1):
            pair_sum(1, r)
        for r in (2, 3):
            pair_sum(3, r)
        for r in range(RING):
            pair_sum(0, r)
        yield
        copies.received(relay1.at[0], ring_sems.at[0])
        for r in (0, 1):
            grad_acc[1, r] += relay1[0, r]
        copies.start(grad_acc.at[1, pl.ds(0, 2)], ring1.at[0, pl.ds(0, 2)], ring_sems.at[2], right)
        copies.received(relay1.at[1], ring_sems.at[1])
        for r in (0, 1):
            grad_acc[3, 2 + r] += relay1[1, r]
        copies.start(grad_acc.at[3, pl.ds(2, 2)], ring1.at[1, pl.ds(2, 2)], ring_sems.at[5], left)
        yield
        copies.received(ring1.at[0, pl.ds(2, 2)], ring_sems.at[3])
        copies.received(ring1.at[1, pl.ds(0, 2)], ring_sems.at[4])
        for r in (2, 3):
            grad_acc[0, r] += ring1[0, r]
        for r in (0, 1):
            grad_acc[0, r] += ring1[1, r]
        yield
        up, down = place.peer(0, 1), place.peer(0, 3)
        copies.received(ring1.at[1, pl.ds(2, 2)], ring_sems.at[5])
        grad_acc[0, 2] += ring1[1, 2]
        copies.start(grad_acc.at[0, 2, low], relay2.at[0], ring_sems.at[6], up)
        copies.start(grad_acc.at[0, 2, high], relay2.at[1], ring_sems.at[7], down)
        grad_acc[0, 3] += ring1[1, 3]
        copies.start(grad_acc.at[0, 3, low], ring2.at[1, low], ring_sems.at[10], down)
        copies.received(ring1.at[0, pl.ds(0, 2)], ring_sems.at[2])
        grad_acc[0, 1] += ring1[0, 1]
        copies.start(grad_acc.at[0, 1, high], ring2.at[0, high], ring_sems.at[9], up)
        grad_acc[0, 0] += ring1[0, 0]
        yield
        copies.received(relay2.at[0], ring_sems.at[6])
        grad_acc[0, 1, low] += relay2[0]
        copies.start(grad_acc.at[0, 1, low], ring2.at[0, low], ring_sems.at[8], up)
        copies.received(relay2.at[1], ring_sems.at[7])
        grad_acc[0, 3, high] += relay2[1]
        copies.start(grad_acc.at[0, 3, high], ring2.at[1, high], ring_sems.at[11], down)
        yield
        copies.received(ring2.at[0, high], ring_sems.at[9])
        copies.received(ring2.at[1, low], ring_sems.at[10])
        copies.received(ring2.at[0, low], ring_sems.at[8])
        copies.received(ring2.at[1, high], ring_sems.at[11])
        grad_out[...] = grad_acc[0, 0] + ring2[0] + ring2[1]

    def mixed_pipe():
        after, before = place.along_row(1, rows), place.along_row(rows - 1, rows)
        copies.start(mixed_in.at[(place.row + rows - 1) % rows, low], row_up.at[0], row_sems.at[0], after)
        copies.start(mixed_in.at[(place.row + 1) % rows, high], row_down.at[0], row_sems.at[rows], before)
        yield
        for step in range(1, rows):
            copies.received(row_up.at[step - 1], row_sems.at[step - 1])
            row_up[step - 1] += mixed_in[(place.row + 2 * rows - 1 - step) % rows, low]
            if step < rows - 1:
                copies.start(row_up.at[step - 1], row_up.at[step], row_sems.at[step], after)
            copies.received(row_down.at[step - 1], row_sems.at[rows + step - 1])
            row_down[step - 1] += mixed_in[(place.row + 1 + step) % rows, high]
            if step < rows - 1:
                copies.start(row_down.at[step - 1], row_down.at[step], row_sems.at[rows + step], before)
            yield
        mixed_out[low] = row_up[rows - 2]
        mixed_out[high] = row_down[rows - 2]

    def sums_pipe():
        copies.start(sums_in.at[1 - core], sum_pair, sum_sems.at[0], partner)
        yield
        copies.received(sum_pair, sum_sems.at[0])
        for q in range(RING):
            sum_pair[q] += sums_in[core, q]
        for k in (2, 1, 3):
            copies.start(sum_pair.at[(place.p1 + k) % RING], sum_first.at[k], sum_sems.at[k], place.peer(k, 0))
        sum_first[0] = sum_pair[place.p1]
        yield
        for k in (1, 3, 2):
            copies.received(sum_first.at[k], sum_sems.at[k])
            sum_first[0] += sum_first[k]
        for k in (2, 1, 3):
            copies.start(sum_first.at[0, (place.p2 + k) % RING], sum_second.at[k], sum_sems.at[3 + k], place.peer(0, k))
        sum_second[0] = sum_first[0, place.p2]
        yield
        for k in (1, 3, 2):
            copies.received(sum_second.at[k], sum_sems.at[3 + k])
            sum_second[0] += sum_second[k]
        for quarter in range(RING):
            for side in range(2):
                sum_tiles[2 * quarter + side] = sum_second[0, pl.ds(8 * quarter, 8), pl.ds(TILE * side, TILE)]
        for k in (4, 3, 5, 2, 6, 1, 7):
            copies.start(
                sum_tiles.at[(place.row + k) % rows], sum_rows.at[k], sum_sems.at[6 + k], place.along_row(k, rows)
            )
        sum_rows[0] = sum_tiles[place.row]
        yield
        for k in (1, 7, 2, 6, 3, 5, 4):
            copies.received(sum_rows.at[k], sum_sems.at[6 + k])
            sum_rows[0] += sum_rows[k]
        for k in (4, 3, 5, 2, 6, 1, 7):
            copies.start(
                sum_rows.at[0], sum_tiles.at[rows + place.row], sum_sems.at[13 + k], place.along_row(k, rows)
            )
        sum_tiles[rows + place.row] = sum_rows[0]
        yield
        for k in (1, 7, 2, 6, 3, 5, 4):
            copies.received(sum_tiles.at[rows + (place.row + rows - k) % rows], sum_sems.at[13 + k])
        own = sums_out.at[core, place.p1, place.p2]
        for quarter in range(RING):
            for side in range(2):
                own[pl.ds(8 * quarter, 8), pl.ds(TILE * side, TILE)] = sum_tiles[rows + 2 * quarter + side]
        others = [(k1, k2) for k1 in range(RING) for k2 in range(RING) if k1 or k2]
        for k1, k2 in others:
            copies.start(own, own, spread_sems.at[4 * k1 + k2], place.peer(k1, k2))
        yield
        for k1, k2 in others:
            there = sums_out.at[core, (place.p1 + RING - k1) % RING, (place.p2 + RING - k2) % RING]
            copies.received(there, spread_sems.at[4 * k1 + k2])
        copies.start(sums_out.at[core], sums_out.at[core], spread_sems.at[0], partner)
        yield
        copies.received(sums_out.at[1 - core], spread_sems.at[0])

    run_in_order(
        {"s": sums_pipe(), "m": mixed_pipe(), "g": grad_pipe()},
        "smg" + "s" + "g" + "m" + "s" + "g" + "m" + "s" + "g" + "s" + "m" + "g" + "s" + "m" + "g" + "m" + "s" + "g" + "m" + "g" + "m" + "s" + "g",
    )
    copies.finish()


def reduce_call(grad, mixed, sums, rows, cols):
    anywhere = pl.BlockSpec(memory_space=pl.ANY)
    vmem = pl.BlockSpec(memory_space=pltpu.VMEM)
    ent_dev = grad.shape[0] // cols
    block = (ent_dev, D)
    share = sums.shape[0] // cols
    grad_out, mixed_out, sums_out = pl.pallas_call(
        functools.partial(reduce_kernel, rows),
        out_shape=[
            jax.ShapeDtypeStruct(block, F32),
            jax.ShapeDtypeStruct(block, F32),
            jax.ShapeDtypeStruct((2, RING, RING, share, D), F32),
        ],
        in_specs=[anywhere, vmem, vmem],
        out_specs=[vmem] * 3,
        scratch_shapes=[
            pltpu.VMEM((RING, RING) + block, F32),
            pltpu.VMEM((RING, RING) + block, F32),
            pltpu.VMEM((2, 2) + block, F32),
            pltpu.VMEM((2, RING) + block, F32),
            pltpu.VMEM((2, HALF, D), F32),
            pltpu.VMEM((2,) + block, F32),
            pltpu.VMEM((rows - 1, HALF, D), F32),
            pltpu.VMEM((rows - 1, HALF, D), F32),
            pltpu.VMEM((RING, RING, share, D), F32),
            pltpu.VMEM((RING, RING, share, D), F32),
            pltpu.VMEM((RING, share, D), F32),
            pltpu.VMEM((rows, 8, TILE), F32),
            pltpu.VMEM((2 * rows, 8, TILE), F32),
            pltpu.SemaphoreType.DMA((96,)),
            pltpu.SemaphoreType.DMA((16,)),
            pltpu.SemaphoreType.DMA((16,)),
            pltpu.SemaphoreType.DMA((12,)),
            pltpu.SemaphoreType.DMA((2 * rows,)),
            pltpu.SemaphoreType.DMA((24,)),
            pltpu.SemaphoreType.DMA((16,)),
        ],
        compiler_params=pltpu.CompilerParams(
            collective_id=1, has_side_effects=True, vmem_limit_bytes=48 * 1024 * 1024
        ),
        name="reduce",
    )(
        grad.reshape((cols // 2, 2) + block),
        mixed.reshape((rows,) + block),
        sums.reshape(2, RING, RING, share, D),
    )
    return grad_out, mixed_out, sums_out.reshape(-1, D)


def shards(
    feats,
    rel_embed,
    weights,
    cot,
    tile_row,
    tile_col,
    tile_live,
    edge_ends,
    edge_relation,
    edge_dir,
    edge_count,
):
    rows_n = lax.axis_size("row")
    cols_n = lax.axis_size("col")
    row_index = lax.axis_index("row")
    col_index = lax.axis_index("col")
    ent_dev = feats.shape[0]
    src_dev = ent_dev * cols_n
    dst_dev = ent_dev * rows_n
    rels_all = rel_embed.shape[0]
    sources, targets = gather_call(feats, cot, rows_n, cols_n)
    owner = (row_index == col_index * rows_n // cols_n).astype(jnp.int32)
    offset = jnp.clip(col_index * dst_dev - row_index * src_dev, 0, src_dev - dst_dev) // TILE
    meta = jnp.stack([tile_live[0], owner, offset.astype(jnp.int32), jnp.int32(rels_all)])
    grad, mixed, sums = tiles_call(
        meta,
        tile_row - col_index * (dst_dev // TILE),
        tile_col - row_index * (src_dev // TILE),
        edge_count[:, None],
        edge_ends,
        edge_relation,
        edge_dir,
        sources,
        targets,
        jnp.pad(rel_embed, ((0, RELS_PAD - rels_all), (0, 0))),
        weights,
    )
    grad_feats, mixed, sums = reduce_call(grad, mixed, sums, rows_n, cols_n)
    grad_rel = sums[3 * D : 3 * D + rels_all]
    return (mixed, grad_feats, grad_rel, sums[: 3 * D].reshape(3, D, D))


def solution(mesh):
    return jax.shard_map(
        shards,
        mesh=mesh,
        in_specs=(
            P(("row", "col"), None),
            P(),
            P(),
            P(("col", "row"), None),
            P(("row", "col")),
            P(("row", "col")),
            P(("row", "col")),
            P(("row", "col"), None),
            P(("row", "col"), None),
            P(("row", "col"), None),
            P(("row", "col")),
        ),
        out_specs=(P(("col", "row"), None), P(("row", "col"), None), P(), P()),
        check_vma=False,
    )
```

```python
import functools

import jax
import jax.numpy as jnp
from jax import lax
from jax.experimental import pallas as pl
from jax.experimental.pallas import tpu as pltpu
from jax.sharding import PartitionSpec as P

D = 256
TILE = 128
EDGE_TILE = 256
PAIR = 2 * TILE
RELS_PAD = 256
NONE = 1024
UNROLL = 16
VMEM_LIMIT = 60 * 1024 * 1024
F32 = jnp.float32
BF16 = jnp.bfloat16
NN = (((1,), (0,)), ((), ()))
NT = (((1,), (1,)), ((), ()))
TN = (((0,), (0,)), ((), ()))


def dot(left, right, dims=NN):
    return lax.dot_general(left, right, dims, preferred_element_type=F32)


def split(value):
    high = value.astype(BF16)
    return high, (value - high.astype(F32)).astype(BF16)


def dot_exact_left(left, right, dims=NN):
    high, low = right
    return dot(left, high, dims) + dot(left, low, dims)


def dot_exact_right(left, right, dims=NN):
    high, low = left
    return dot(high, right, dims) + dot(low, right, dims)


def dot_split(left, right, dims=NN):
    return dot(left[0], right[0], dims) + (dot(left[0], right[1], dims) + dot(left[1], right[0], dims))


def rows_at(index, size):
    return pl.ds(pl.multiple_of(index * size, size), size)


def tiles_kernel(
    row_ref,
    col_ref,
    live_ref,
    count_ref,
    ends_ref,
    relation_ref,
    dir_ref,
    rel_ref,
    weights_ref,
    feats_any,
    cot_any,
    grad_any,
    mixed_ref,
    sums_ref,
    key_ref,
    src_ref,
    feats_ref,
    cot_ref,
    turned_ref,
    rel_pad_ref,
    totals_ref,
    counts_ref,
    high_ref,
    low_ref,
    total_high_ref,
    total_low_ref,
    count_high_ref,
    grad_ref,
    self_rel_ref,
    sems,
):
    slots = ends_ref.shape[0]
    dst_dev, src_dev = cot_ref.shape[0], feats_ref.shape[0]
    blocks, source_blocks = dst_dev // TILE, src_dev // TILE
    rels_all = rel_ref.shape[0]
    col_index = row_ref[0] // blocks
    row_index = col_ref[0] // source_blocks
    ahead = col_index * blocks - row_index * source_blocks
    owner = (ahead >= 0) & (ahead < source_blocks)
    load_cot = pltpu.make_async_copy(cot_any, cot_ref, sems.at[0])
    load_feats = pltpu.make_async_copy(feats_any, feats_ref, sems.at[1])
    load_cot.start()
    load_feats.start()

    ends = ends_ref[...]
    key_ref[...] = dir_ref[...] * TILE + lax.shift_right_logical(ends, 7)
    src_ref[...] = ends & (TILE - 1)
    rel_pad_ref[...] = jnp.zeros_like(rel_pad_ref)
    rel_pad_ref[pl.ds(0, rels_all), :] = rel_ref[...]
    weight = [split(weights_ref[which]) for which in range(3)]

    def clear_block(block, _):
        grad_ref[rows_at(block, PAIR), :] = jnp.zeros((PAIR, D), F32)
        return 0

    lax.fori_loop(0, src_dev // PAIR, clear_block, 0)
    sums_ref[pl.ds(2 * D, D), :] = jnp.zeros((D, D), F32)
    self_rel_ref[...] = jnp.zeros_like(self_rel_ref)
    load_cot.wait()

    def image_block(block, _):
        cot = cot_ref[rows_at(block, TILE), :]
        turned_ref[:, rows_at(block, TILE)] = cot.T
        at = rows_at(block, PAIR)
        for which in range(2):
            high, low = split(dot_exact_left(cot, weight[which], NT))
            part = pl.ds(pl.multiple_of(block * PAIR + which * TILE, TILE), TILE)
            high_ref[part, :] = high
            low_ref[part, :] = low
        totals_ref[at, :] = jnp.zeros((PAIR, D), F32)
        counts_ref[at, :] = jnp.zeros((PAIR, RELS_PAD), F32)
        return 0

    lax.fori_loop(0, blocks, image_block, 0, unroll=2)

    @pl.when(owner)
    def _():
        def self_image(block, total):
            image = dot_exact_left(cot_ref[rows_at(block, PAIR), :], weight[2], NT)
            grad_ref[pl.ds(pl.multiple_of((ahead + 2 * block) * TILE, TILE), PAIR), :] = image
            return total + jnp.sum(image.reshape(PAIR // 8, 8, D), axis=0)

        self_rel_ref[...] = lax.fori_loop(0, blocks // 2, self_image, jnp.zeros((8, D), F32), unroll=2)

    load_feats.wait()

    pair_iota = lax.broadcasted_iota(jnp.int32, (PAIR, EDGE_TILE), 0)
    tile_iota = lax.broadcasted_iota(jnp.int32, (TILE, EDGE_TILE), 0)
    edge_iota = lax.broadcasted_iota(jnp.int32, (1, EDGE_TILE), 1)

    def hot(iota, entries):
        return jnp.where(iota == entries, 1.0, 0.0).astype(BF16)

    def tile(slot, _):
        at = pl.ds(slot, 1)
        edges = jnp.where(slot < live_ref[0], count_ref[slot], 0)
        hot_dst = hot(pair_iota, jnp.where(edge_iota < edges, key_ref[at, :], NONE))
        hot_src = hot(tile_iota, src_ref[at, :])
        hot_rel = hot(pair_iota, relation_ref[at, :])
        forward = dot(hot_dst, hot_src, NT).astype(BF16)
        backward = dot(hot_src, hot_dst, NT).astype(BF16)
        counted = dot(hot_dst, hot_rel, NT)
        row = rows_at(row_ref[slot] % blocks, PAIR)
        col = rows_at(col_ref[slot] % source_blocks, TILE)
        totals_ref[row, :] += dot(forward, feats_ref[col, :])
        counts_ref[row, :] += counted
        grad_ref[col, :] += dot(backward, high_ref[row, :]) + dot(backward, low_ref[row, :])
        return 0

    lax.fori_loop(0, slots, tile, 0, unroll=UNROLL)

    stores = []
    for part in range(4):
        here = pl.ds(part * (src_dev // 4), src_dev // 4)
        copy = pltpu.make_async_copy(grad_ref.at[here, :], grad_any.at[here, :], sems.at[2 + part])
        copy.start()
        stores.append(copy)

    relations = split(rel_pad_ref[...])

    def most(block, value):
        counts = counts_ref[rows_at(block, PAIR), :]
        return jnp.maximum(value, jnp.max(counts.reshape(PAIR // 8, 8, RELS_PAD), axis=0))

    largest = jnp.max(lax.fori_loop(0, blocks, most, jnp.zeros((8, RELS_PAD), F32)))
    large = largest > 256.0

    @pl.when(large)
    def _():
        def low_block(block, _):
            at = rows_at(block, PAIR)
            low = split(counts_ref[at, :])[1]
            totals_ref[at, :] -= dot(low, relations[0]) + dot(low, relations[1])
            return 0

        lax.fori_loop(0, blocks, low_block, 0)

    def finish_block(block, _):
        at = rows_at(block, PAIR)
        here = rows_at(block, TILE)
        counts = counts_ref[at, :].astype(BF16)
        totals = totals_ref[at, :] - (dot(counts, relations[0]) + dot(counts, relations[1]))
        pieces = [split(totals[:TILE]), split(totals[TILE:])]
        for which in range(2):
            total_high_ref[which, here, :] = pieces[which][0]
            total_low_ref[which, here, :] = pieces[which][1]
            count_high_ref[which, here, :] = counts[which * TILE : (which + 1) * TILE]
        mixed_ref[here, :] = dot_split(pieces[0], weight[0]) + dot_split(pieces[1], weight[1])
        return 0

    lax.fori_loop(0, blocks, finish_block, 0, unroll=4)

    turned = turned_ref[...]
    grad_rel = jnp.zeros((D, RELS_PAD), F32)
    met = [dot(turned, count_high_ref[which]) for which in range(2)]
    for which in range(2):
        product = dot(turned, total_high_ref[which]) + dot(turned, total_low_ref[which])
        sums_ref[pl.ds(which * D, D), :] = product.T
        grad_rel -= dot_split(weight[which], split(met[which]))
    sums_ref[pl.ds(3 * D, RELS_PAD), :] = grad_rel.T

    @pl.when(large)
    def _():
        def low_block(block, _):
            cot = cot_ref[rows_at(block, TILE), :]
            counts = counts_ref[rows_at(block, PAIR), :]
            for which in range(2):
                low = split(counts[which * TILE : (which + 1) * TILE])[1]
                part = split(dot(low, cot, TN))
                sums_ref[pl.ds(3 * D, RELS_PAD), :] -= dot_split(part, weight[which], NT)
            return 0

        lax.fori_loop(0, blocks, low_block, 0)

    sums_ref[pl.ds(3 * D + rels_all - 1, 1), :] -= jnp.sum(self_rel_ref[...], axis=0, keepdims=True)

    @pl.when(owner)
    def _():
        own_rel = rel_ref[pl.ds(rels_all - 1, 1), :]

        def self_block(block, _):
            here = rows_at(block, PAIR)
            there = pl.ds(pl.multiple_of((ahead + 2 * block) * TILE, TILE), PAIR)
            self_term = split(feats_ref[there, :].astype(F32) - own_rel)
            total_high_ref[0, here, :] = self_term[0]
            total_low_ref[0, here, :] = self_term[1]
            mixed_ref[here, :] += dot_split(self_term, weight[2])
            return 0

        lax.fori_loop(0, blocks // 2, self_block, 0, unroll=2)
        product = dot(turned, total_high_ref[0]) + dot(turned, total_low_ref[0])
        sums_ref[pl.ds(2 * D, D), :] = product.T

    for copy in stores:
        copy.wait()


def tiles_call(rows, cols, live, counts, ends, relation, direction, rel, weights, sources, cot):
    dst_dev, src_dev = cot.shape[0], sources.shape[0]
    slots = ends.shape[0]
    smem = pl.BlockSpec(memory_space=pltpu.SMEM)
    vmem = pl.BlockSpec(memory_space=pltpu.VMEM)
    anywhere = pl.BlockSpec(memory_space=pl.ANY)
    return pl.pallas_call(
        tiles_kernel,
        out_shape=[
            jax.ShapeDtypeStruct((src_dev, D), F32),
            jax.ShapeDtypeStruct((dst_dev, D), F32),
            jax.ShapeDtypeStruct((3 * D + RELS_PAD, D), F32),
        ],
        in_specs=[smem] * 4 + [vmem] * 5 + [anywhere] * 2,
        out_specs=[anywhere, vmem, vmem],
        scratch_shapes=[
            pltpu.VMEM((slots, EDGE_TILE), jnp.int32),
            pltpu.VMEM((slots, EDGE_TILE), jnp.int32),
            pltpu.VMEM((src_dev, D), BF16),
            pltpu.VMEM((dst_dev, D), BF16),
            pltpu.VMEM((D, dst_dev), BF16),
            pltpu.VMEM((RELS_PAD, D), F32),
            pltpu.VMEM((2 * dst_dev, D), F32),
            pltpu.VMEM((2 * dst_dev, RELS_PAD), F32),
            pltpu.VMEM((2 * dst_dev, D), BF16),
            pltpu.VMEM((2 * dst_dev, D), BF16),
            pltpu.VMEM((2, dst_dev, D), BF16),
            pltpu.VMEM((2, dst_dev, D), BF16),
            pltpu.VMEM((2, dst_dev, RELS_PAD), BF16),
            pltpu.VMEM((src_dev, D), F32),
            pltpu.VMEM((8, D), F32),
            pltpu.SemaphoreType.DMA((6,)),
        ],
        compiler_params=pltpu.CompilerParams(vmem_limit_bytes=VMEM_LIMIT),
        name="tiles",
    )(rows, cols, live, counts, ends, relation, direction, rel, weights, sources, cot)


MESH = pl.DeviceIdType.MESH
RING = 4
HALF = TILE


class Copies:
    def __init__(self, send_sems):
        self.send_sems, self.started = send_sems, []

    def start(self, src, dst, recv, peer):
        copy = pltpu.make_async_remote_copy(
            src_ref=src,
            dst_ref=dst,
            send_sem=self.send_sems.at[len(self.started)],
            recv_sem=recv,
            device_id=peer,
            device_id_type=MESH,
        )
        copy.start()
        self.started.append(copy)

    def received(self, dst, recv):
        pltpu.make_async_remote_copy(
            src_ref=dst,
            dst_ref=dst,
            send_sem=self.send_sems.at[0],
            recv_sem=recv,
            device_id=self.any_peer,
            device_id_type=MESH,
        ).wait_recv()

    def finish(self):
        for copy in self.started:
            copy.wait_send()


class Place:
    def __init__(self):
        self.row = lax.axis_index("row")
        self.col = lax.axis_index("col")
        self.core = self.col % 2
        self.stride1 = 8 - 6 * self.core
        self.stride2 = 10 - self.stride1
        self.p1 = self.col // self.stride1 % RING
        self.p2 = self.col // self.stride2 % RING

    def col_at(self, k1, k2):
        return (self.p1 + k1) % RING * self.stride1 + (self.p2 + k2) % RING * self.stride2 + self.core

    def peer(self, k1, k2):
        return (self.row, self.col_at(k1, k2))

    def partner(self):
        return (self.row, self.col + 1 - 2 * self.core)

    def along_row(self, k, rows):
        return ((self.row + k) % rows, self.col)

    def greet(self, peers):
        barrier = pltpu.get_barrier_semaphore()
        for peer in peers:
            pl.semaphore_signal(barrier, inc=1, device_id=peer, device_id_type=MESH)
        pl.semaphore_wait(barrier, len(peers))


def run_in_order(pipes, order):
    for name in order:
        next(pipes[name], None)
    for pipe in pipes.values():
        for _ in pipe:
            pass


def gather_kernel(
    rows,
    feats_ref,
    cot_ref,
    sources_ref,
    targets_ref,
    send_sems,
    shard_sems,
    row_sems,
    own_sems,
):
    place = Place()
    copies = Copies(send_sems)
    copies.any_peer = place.partner()
    own_copies = [
        pltpu.make_async_copy(feats_ref, sources_ref.at[place.col], own_sems.at[0]),
        pltpu.make_async_copy(cot_ref, targets_ref.at[place.row], own_sems.at[1]),
    ]
    for copy in own_copies:
        copy.start()
    place.greet(
        [place.partner()]
        + [place.peer(k, 0) for k in (1, 3)]
        + [place.peer(0, k) for k in (1, 3)]
        + [place.along_row(k, rows) for k in (1, rows - 1)]
    )
    parts = [pl.ds(0, HALF), pl.ds(HALF, HALF)]

    def send_shard(b, which, peer, src=None):
        for half in which:
            here = sources_ref.at[b, parts[half]]
            copies.start(here if src is None else src.at[parts[half]], here, shard_sems.at[2 * b + half], peer)

    def got_shard(b, which):
        for half in which:
            copies.received(sources_ref.at[b, parts[half]], shard_sems.at[2 * b + half])

    def feats_pipe():
        for half in (0, 1):
            for peer in (place.peer(1, 0), place.peer(3, 0)):
                send_shard(place.col, [half], peer, feats_ref)
        for peer in (place.peer(0, 1), place.peer(0, 3), place.partner()):
            send_shard(place.col, [0, 1], peer, feats_ref)
        yield

        def spread(b, which):
            for peer in (place.peer(0, 1), place.peer(0, 3)):
                send_shard(b, which, peer)
            send_shard(b, which, place.partner())

        left, right, far = place.col_at(3, 0), place.col_at(1, 0), place.col_at(2, 0)
        got_shard(left, [0])
        send_shard(left, [0], place.peer(1, 0))
        spread(left, [0])
        got_shard(right, [0])
        spread(right, [0])
        got_shard(right, [1])
        send_shard(right, [1], place.peer(3, 0))
        spread(right, [1])
        got_shard(left, [1])
        spread(left, [1])
        yield

        def second(k1):
            below, above = place.col_at(k1, 3), place.col_at(k1, 1)
            got_shard(below, [0])
            send_shard(below, [0], place.peer(0, 1))
            got_shard(above, [0])
            got_shard(above, [1])
            send_shard(above, [1], place.peer(0, 3))
            got_shard(below, [1])
            send_shard(below, [0, 1], place.partner())
            send_shard(above, [0, 1], place.partner())

        second(0)
        yield
        got_shard(far, [0, 1])
        spread(far, [0, 1])
        yield
        second(3)
        yield
        second(1)
        yield
        second(2)
        yield
        for k1 in (0, 3, 1, 2):
            b = place.col_at(k1, 2)
            got_shard(b, [0, 1])
            send_shard(b, [0, 1], place.partner())
        yield
        for k1 in range(RING):
            for k2 in range(RING):
                got_shard(place.col_at(k1, k2) + 1 - 2 * place.core, [0, 1])

    def cot_pipe():
        after, before = place.along_row(1, rows), place.along_row(rows - 1, rows)

        def send_row(index, which, peer, src=None):
            for half in which:
                here = targets_ref.at[index, parts[half]]
                copies.start(here if src is None else src.at[parts[half]], here, row_sems.at[2 * index + half], peer)

        def got_row(index, which):
            for half in which:
                copies.received(targets_ref.at[index, parts[half]], row_sems.at[2 * index + half])

        send_row(place.row, [0, 1], after, cot_ref)
        send_row(place.row, [1, 0], before, cot_ref)
        yield
        for k in range(1, rows // 2):
            last = k == rows // 2 - 1
            low, high = (place.row + rows - k) % rows, (place.row + k) % rows
            got_row(low, [0])
            send_row(low, [0], after)
            got_row(high, [1])
            send_row(high, [1], before)
            got_row(low, [1])
            if not last:
                send_row(low, [1], after)
            got_row(high, [0])
            if not last:
                send_row(high, [0], before)
            yield
        got_row((place.row + rows // 2) % rows, [0, 1])

    run_in_order({"f": feats_pipe(), "c": cot_pipe()}, "fcfcffcffcff")
    for copy in own_copies:
        copy.wait()
    copies.finish()


def gather_call(feats, cot, rows, cols):
    anywhere = pl.BlockSpec(memory_space=pl.ANY)
    sources, targets = pl.pallas_call(
        functools.partial(gather_kernel, rows),
        out_shape=[
            jax.ShapeDtypeStruct((cols,) + feats.shape, feats.dtype),
            jax.ShapeDtypeStruct((rows,) + cot.shape, cot.dtype),
        ],
        in_specs=[anywhere] * 2,
        out_specs=[anywhere] * 2,
        scratch_shapes=[
            pltpu.SemaphoreType.DMA((160,)),
            pltpu.SemaphoreType.DMA((2 * cols,)),
            pltpu.SemaphoreType.DMA((2 * rows,)),
            pltpu.SemaphoreType.DMA((2,)),
        ],
        compiler_params=pltpu.CompilerParams(
            collective_id=0, has_side_effects=True, vmem_limit_bytes=VMEM_LIMIT
        ),
        name="gather",
    )(feats, cot)
    return sources.reshape(-1, D), targets.reshape(-1, D)


def reduce_kernel(
    rows,
    grad_any,
    mixed_any,
    sums_any,
    grad_out,
    mixed_out,
    sums_out,
    grad_acc,
    mixed_in,
    sums_in,
    pair_in,
    relay1,
    ring1,
    relay2,
    ring2,
    row_up,
    row_down,
    sum_pair,
    sum_first,
    sum_second,
    sum_rows,
    sum_tiles,
    send_sems,
    own_sems,
    pair_sems,
    ring_sems,
    row_sems,
    sum_sems,
    spread_sems,
):
    place = Place()
    copies = Copies(send_sems)
    copies.any_peer = place.partner()
    partner = place.partner()
    core = place.core
    order1 = (2, 1, 3, 0)
    load_sums = pltpu.make_async_copy(sums_any.at[core], sums_in, own_sems.at[16])
    load_mixed = pltpu.make_async_copy(mixed_any, mixed_in, own_sems.at[17])
    load_sums.start()
    load_mixed.start()
    own_copies = {}
    for k in order1:
        for r in (2, 1, 3, 0):
            block = place.col_at(k, r) // 2
            copy = pltpu.make_async_copy(grad_any.at[block, core], grad_acc.at[k, r], own_sems.at[4 * k + r])
            copy.start()
            own_copies[k, r] = copy
    place.greet(
        [partner]
        + [place.peer(k1, k2) for k1 in range(RING) for k2 in range(RING) if k1 or k2]
        + [place.along_row(k, rows) for k in range(1, rows)]
    )
    low, high = pl.ds(0, HALF), pl.ds(HALF, HALF)

    def grad_pipe():
        for k in order1:
            for r in (2, 1, 3, 0):
                block = ((place.p2 + k) % RING * place.stride2 + (place.p1 + r) % RING * place.stride1) // 2
                copies.start(grad_any.at[block, 1 - core], pair_in.at[k, r], pair_sems.at[4 * k + r], partner)
        yield

        def pair_sum(k, r):
            own_copies[k, r].wait()
            copies.received(pair_in.at[k, r], pair_sems.at[4 * k + r])
            grad_acc[k, r] += pair_in[k, r]

        right, left = place.peer(1, 0), place.peer(3, 0)
        for r in range(RING):
            pair_sum(2, r)
        copies.start(grad_acc.at[2, pl.ds(0, 2)], relay1.at[0], ring_sems.at[0], right)
        copies.start(grad_acc.at[2, pl.ds(2, 2)], relay1.at[1], ring_sems.at[1], left)
        yield
        for r in (2, 3):
            pair_sum(1, r)
        copies.start(grad_acc.at[1, pl.ds(2, 2)], ring1.at[0, pl.ds(2, 2)], ring_sems.at[3], right)
        for r in (0, 1):
            pair_sum(3, r)
        copies.start(grad_acc.at[3, pl.ds(0, 2)], ring1.at[1, pl.ds(0, 2)], ring_sems.at[4], left)
        yield
        for r in (0, 1):
            pair_sum(1, r)
        for r in (2, 3):
            pair_sum(3, r)
        for r in range(RING):
            pair_sum(0, r)
        yield
        copies.received(relay1.at[0], ring_sems.at[0])
        for r in (0, 1):
            grad_acc[1, r] += relay1[0, r]
        copies.start(grad_acc.at[1, pl.ds(0, 2)], ring1.at[0, pl.ds(0, 2)], ring_sems.at[2], right)
        copies.received(relay1.at[1], ring_sems.at[1])
        for r in (0, 1):
            grad_acc[3, 2 + r] += relay1[1, r]
        copies.start(grad_acc.at[3, pl.ds(2, 2)], ring1.at[1, pl.ds(2, 2)], ring_sems.at[5], left)
        yield
        copies.received(ring1.at[0, pl.ds(2, 2)], ring_sems.at[3])
        copies.received(ring1.at[1, pl.ds(0, 2)], ring_sems.at[4])
        for r in (2, 3):
            grad_acc[0, r] += ring1[0, r]
        for r in (0, 1):
            grad_acc[0, r] += ring1[1, r]
        yield
        up, down = place.peer(0, 1), place.peer(0, 3)
        copies.received(ring1.at[1, pl.ds(2, 2)], ring_sems.at[5])
        grad_acc[0, 2] += ring1[1, 2]
        copies.start(grad_acc.at[0, 2, low], relay2.at[0], ring_sems.at[6], up)
        copies.start(grad_acc.at[0, 2, high], relay2.at[1], ring_sems.at[7], down)
        grad_acc[0, 3] += ring1[1, 3]
        copies.start(grad_acc.at[0, 3, low], ring2.at[1, low], ring_sems.at[10], down)
        copies.received(ring1.at[0, pl.ds(0, 2)], ring_sems.at[2])
        grad_acc[0, 1] += ring1[0, 1]
        copies.start(grad_acc.at[0, 1, high], ring2.at[0, high], ring_sems.at[9], up)
        grad_acc[0, 0] += ring1[0, 0]
        yield
        copies.received(relay2.at[0], ring_sems.at[6])
        grad_acc[0, 1, low] += relay2[0]
        copies.start(grad_acc.at[0, 1, low], ring2.at[0, low], ring_sems.at[8], up)
        copies.received(relay2.at[1], ring_sems.at[7])
        grad_acc[0, 3, high] += relay2[1]
        copies.start(grad_acc.at[0, 3, high], ring2.at[1, high], ring_sems.at[11], down)
        yield
        copies.received(ring2.at[0, high], ring_sems.at[9])
        copies.received(ring2.at[1, low], ring_sems.at[10])
        copies.received(ring2.at[0, low], ring_sems.at[8])
        copies.received(ring2.at[1, high], ring_sems.at[11])
        grad_out[...] = grad_acc[0, 0] + ring2[0] + ring2[1]

    def mixed_pipe():
        after, before = place.along_row(1, rows), place.along_row(rows - 1, rows)
        copies.start(mixed_any.at[(place.row + rows - 1) % rows, low], row_up.at[0], row_sems.at[0], after)
        copies.start(mixed_any.at[(place.row + 1) % rows, high], row_down.at[0], row_sems.at[rows], before)
        yield
        load_mixed.wait()
        for step in range(1, rows):
            copies.received(row_up.at[step - 1], row_sems.at[step - 1])
            row_up[step - 1] += mixed_in[(place.row + 2 * rows - 1 - step) % rows, low]
            if step < rows - 1:
                copies.start(row_up.at[step - 1], row_up.at[step], row_sems.at[step], after)
            copies.received(row_down.at[step - 1], row_sems.at[rows + step - 1])
            row_down[step - 1] += mixed_in[(place.row + 1 + step) % rows, high]
            if step < rows - 1:
                copies.start(row_down.at[step - 1], row_down.at[step], row_sems.at[rows + step], before)
            yield
        mixed_out[low] = row_up[rows - 2]
        mixed_out[high] = row_down[rows - 2]

    def sums_pipe():
        copies.start(sums_any.at[1 - core], sum_pair, sum_sems.at[0], partner)
        yield
        load_sums.wait()
        copies.received(sum_pair, sum_sems.at[0])
        for q in range(RING):
            sum_pair[q] += sums_in[q]
        for k in (2, 1, 3):
            copies.start(sum_pair.at[(place.p1 + k) % RING], sum_first.at[k], sum_sems.at[k], place.peer(k, 0))
        sum_first[0] = sum_pair[place.p1]
        yield
        for k in (1, 3, 2):
            copies.received(sum_first.at[k], sum_sems.at[k])
            sum_first[0] += sum_first[k]
        for k in (2, 1, 3):
            copies.start(sum_first.at[0, (place.p2 + k) % RING], sum_second.at[k], sum_sems.at[3 + k], place.peer(0, k))
        sum_second[0] = sum_first[0, place.p2]
        yield
        for k in (1, 3, 2):
            copies.received(sum_second.at[k], sum_sems.at[3 + k])
            sum_second[0] += sum_second[k]
        for quarter in range(RING):
            for side in range(2):
                sum_tiles[2 * quarter + side] = sum_second[0, pl.ds(8 * quarter, 8), pl.ds(TILE * side, TILE)]
        for k in (4, 3, 5, 2, 6, 1, 7):
            copies.start(
                sum_tiles.at[(place.row + k) % rows], sum_rows.at[k], sum_sems.at[6 + k], place.along_row(k, rows)
            )
        sum_rows[0] = sum_tiles[place.row]
        yield
        for k in (1, 7, 2, 6, 3, 5, 4):
            copies.received(sum_rows.at[k], sum_sems.at[6 + k])
            sum_rows[0] += sum_rows[k]
        for k in (4, 3, 5, 2, 6, 1, 7):
            copies.start(
                sum_rows.at[0], sum_tiles.at[rows + place.row], sum_sems.at[13 + k], place.along_row(k, rows)
            )
        sum_tiles[rows + place.row] = sum_rows[0]
        yield
        for k in (1, 7, 2, 6, 3, 5, 4):
            copies.received(sum_tiles.at[rows + (place.row + rows - k) % rows], sum_sems.at[13 + k])
        own = sums_out.at[core, place.p1, place.p2]
        for quarter in range(RING):
            for side in range(2):
                own[pl.ds(8 * quarter, 8), pl.ds(TILE * side, TILE)] = sum_tiles[rows + 2 * quarter + side]
        for k in (2, 1, 3):
            copies.start(own, own, spread_sems.at[k], place.peer(0, k))
        yield
        for k in (1, 3, 2):
            copies.received(sums_out.at[core, place.p1, (place.p2 + RING - k) % RING], spread_sems.at[k])
        line = sums_out.at[core, place.p1]
        for k in (2, 1, 3):
            copies.start(line, line, spread_sems.at[3 + k], place.peer(k, 0))
        yield
        copies.start(line, line, spread_sems.at[7], partner)
        for k in (1, 3, 2):
            there = sums_out.at[core, (place.p1 + RING - k) % RING]
            copies.received(there, spread_sems.at[3 + k])
            copies.start(there, there, spread_sems.at[7 + k], partner)
        yield
        copies.received(sums_out.at[1 - core, place.p2], spread_sems.at[7])
        for k in (1, 3, 2):
            copies.received(sums_out.at[1 - core, (place.p2 + RING - k) % RING], spread_sems.at[7 + k])

    run_in_order(
        {"s": sums_pipe(), "m": mixed_pipe(), "g": grad_pipe()},
        "smgsmgsmgsmgsmgsmgsmgsmgmg",
    )
    copies.finish()


def reduce_call(grad, mixed, sums, rows, cols):
    anywhere = pl.BlockSpec(memory_space=pl.ANY)
    vmem = pl.BlockSpec(memory_space=pltpu.VMEM)
    ent_dev = grad.shape[0] // cols
    block = (ent_dev, D)
    share = sums.shape[0] // cols
    grad_out, mixed_out, sums_out = pl.pallas_call(
        functools.partial(reduce_kernel, rows),
        out_shape=[
            jax.ShapeDtypeStruct(block, F32),
            jax.ShapeDtypeStruct(block, F32),
            jax.ShapeDtypeStruct((2, RING, RING, share, D), F32),
        ],
        in_specs=[anywhere] * 3,
        out_specs=[vmem] * 3,
        scratch_shapes=[
            pltpu.VMEM((RING, RING) + block, F32),
            pltpu.VMEM((rows,) + block, F32),
            pltpu.VMEM((RING, RING, share, D), F32),
            pltpu.VMEM((RING, RING) + block, F32),
            pltpu.VMEM((2, 2) + block, F32),
            pltpu.VMEM((2, RING) + block, F32),
            pltpu.VMEM((2, HALF, D), F32),
            pltpu.VMEM((2,) + block, F32),
            pltpu.VMEM((rows - 1, HALF, D), F32),
            pltpu.VMEM((rows - 1, HALF, D), F32),
            pltpu.VMEM((RING, RING, share, D), F32),
            pltpu.VMEM((RING, RING, share, D), F32),
            pltpu.VMEM((RING, share, D), F32),
            pltpu.VMEM((rows, 8, TILE), F32),
            pltpu.VMEM((2 * rows, 8, TILE), F32),
            pltpu.SemaphoreType.DMA((96,)),
            pltpu.SemaphoreType.DMA((18,)),
            pltpu.SemaphoreType.DMA((16,)),
            pltpu.SemaphoreType.DMA((12,)),
            pltpu.SemaphoreType.DMA((2 * rows,)),
            pltpu.SemaphoreType.DMA((24,)),
            pltpu.SemaphoreType.DMA((16,)),
        ],
        compiler_params=pltpu.CompilerParams(
            collective_id=1, has_side_effects=True, vmem_limit_bytes=48 * 1024 * 1024
        ),
        name="reduce",
    )(
        grad.reshape((cols // 2, 2) + block),
        mixed.reshape((rows,) + block),
        sums.reshape(2, RING, RING, share, D),
    )
    return grad_out, mixed_out, sums_out.reshape(-1, D)


def shards(
    feats,
    rel_embed,
    weights,
    cot,
    tile_row,
    tile_col,
    tile_live,
    edge_ends,
    edge_relation,
    edge_dir,
    edge_count,
):
    rows_n = lax.axis_size("row")
    cols_n = lax.axis_size("col")
    sources, targets = gather_call(feats, cot, rows_n, cols_n)
    grad, mixed, sums = tiles_call(
        tile_row,
        tile_col,
        tile_live,
        edge_count,
        edge_ends,
        edge_relation,
        edge_dir,
        rel_embed,
        weights,
        sources,
        targets,
    )
    rels_all = rel_embed.shape[0]
    grad_feats, mixed, sums = reduce_call(grad, mixed, sums, rows_n, cols_n)
    grad_rel = sums[3 * D : 3 * D + rels_all]
    return (mixed, grad_feats, grad_rel, sums[: 3 * D].reshape(3, D, D))


def solution(mesh):
    return jax.shard_map(
        shards,
        mesh=mesh,
        in_specs=(
            P(("row", "col"), None),
            P(),
            P(),
            P(("col", "row"), None),
            P(("row", "col")),
            P(("row", "col")),
            P(("row", "col")),
            P(("row", "col"), None),
            P(("row", "col"), None),
            P(("row", "col"), None),
            P(("row", "col")),
        ),
        out_specs=(P(("col", "row"), None), P(("row", "col"), None), P(), P()),
        check_vma=False,
    )
```

```python
import functools

import jax
import jax.numpy as jnp
from jax import lax
from jax.experimental import pallas as pl
from jax.experimental.pallas import tpu as pltpu
from jax.sharding import PartitionSpec as P

D = 256
TILE = 128
EDGE_TILE = 256
PAIR = 2 * TILE
RELS_PAD = 256
NONE = 1024
CHUNKS = 8
PREPARED = 16
GATHER_VMEM = 60 * 1024 * 1024
TILES_VMEM = 60 * 1024 * 1024
REDUCE_VMEM = 52 * 1024 * 1024
F32 = jnp.float32
BF16 = jnp.bfloat16
NN = (((1,), (0,)), ((), ()))
NT = (((1,), (1,)), ((), ()))
TN = (((0,), (0,)), ((), ()))


def dot(left, right, dims=NN):
    return lax.dot_general(left, right, dims, preferred_element_type=F32)


def split(value):
    high = value.astype(BF16)
    return high, (value - high.astype(F32)).astype(BF16)


def dot_exact_left(left, right, dims=NN):
    high, low = right
    return dot(left, high, dims) + dot(left, low, dims)


def dot_exact_right(left, right, dims=NN):
    high, low = left
    return dot(high, right, dims) + dot(low, right, dims)


def dot_split(left, right, dims=NN):
    return dot(left[0], right[0], dims) + (dot(left[0], right[1], dims) + dot(left[1], right[0], dims))


def rows_at(index, size):
    return pl.ds(pl.multiple_of(index * size, size), size)


def hot(iota, entries):
    return jnp.where(iota == entries, 1.0, 0.0).astype(BF16)


def tiles_kernel(
    row_ref,
    col_ref,
    rel_ref,
    weights_ref,
    feats_any,
    cot_any,
    forward_any,
    backward_any,
    counted_any,
    grad_any,
    mixed_ref,
    sums_ref,
    forward_ref,
    backward_ref,
    counted_ref,
    feats_ref,
    cot_ref,
    turned_ref,
    rel_pad_ref,
    totals_ref,
    counts_ref,
    high_ref,
    low_ref,
    count_high_ref,
    grad_ref,
    self_rel_ref,
    sems,
):
    slots = forward_ref.shape[0]
    dst_dev, src_dev = cot_ref.shape[0], feats_ref.shape[0]
    blocks, source_blocks = dst_dev // TILE, src_dev // TILE
    rels_all = rel_ref.shape[0]
    col_index = row_ref[0] // blocks
    row_index = col_ref[0] // source_blocks
    ahead = col_index * blocks - row_index * source_blocks
    owner = (ahead >= 0) & (ahead < source_blocks)
    load_cot = pltpu.make_async_copy(cot_any, cot_ref, sems.at[0])
    load_feats = pltpu.make_async_copy(feats_any, feats_ref, sems.at[1])
    load_cot.start()
    load_feats.start()

    chunk = slots // CHUNKS
    loads = []
    for part in range(CHUNKS):
        here = pl.ds(part * chunk, chunk)
        for which, (src, dst) in enumerate(
            ((forward_any, forward_ref), (backward_any, backward_ref), (counted_any, counted_ref))
        ):
            copy = pltpu.make_async_copy(src.at[here], dst.at[here], sems.at[6 + 3 * part + which])
            copy.start()
            loads.append(copy)
    rel_pad_ref[...] = jnp.zeros_like(rel_pad_ref)
    rel_pad_ref[pl.ds(0, rels_all), :] = rel_ref[...]
    weight = [split(weights_ref[which]) for which in range(3)]

    def clear_block(block, _):
        grad_ref[rows_at(block, PAIR), :] = jnp.zeros((PAIR, D), F32)
        return 0

    lax.fori_loop(0, src_dev // PAIR, clear_block, 0)
    sums_ref[pl.ds(2 * D, D), :] = jnp.zeros((D, D), F32)
    self_rel_ref[...] = jnp.zeros_like(self_rel_ref)
    load_cot.wait()

    def image_block(block, _):
        cot = cot_ref[rows_at(block, TILE), :]
        turned_ref[:, rows_at(block, TILE)] = cot.T
        at = rows_at(block, PAIR)
        for which in range(2):
            high, low = split(dot_exact_left(cot, weight[which], NT))
            part = pl.ds(pl.multiple_of(block * PAIR + which * TILE, TILE), TILE)
            high_ref[part, :] = high
            low_ref[part, :] = low
        totals_ref[at, :] = jnp.zeros((PAIR, D), F32)
        counts_ref[at, :] = jnp.zeros((PAIR, RELS_PAD), F32)
        mixed_ref[rows_at(block, TILE), :] = jnp.zeros((TILE, D), F32)
        return 0

    lax.fori_loop(0, blocks, image_block, 0, unroll=2)

    @pl.when(owner)
    def _():
        def self_image(block, total):
            image = dot_exact_left(cot_ref[rows_at(block, PAIR), :], weight[2], NT)
            grad_ref[pl.ds(pl.multiple_of((ahead + 2 * block) * TILE, TILE), PAIR), :] = image
            return total + jnp.sum(image.reshape(PAIR // 8, 8, D), axis=0)

        self_rel_ref[...] = lax.fori_loop(0, blocks // 2, self_image, jnp.zeros((8, D), F32), unroll=2)

    load_feats.wait()

    @pl.when(owner)
    def _():
        own_rel = rel_ref[pl.ds(rels_all - 1, 1), :]

        def self_block(block, _):
            here = rows_at(block, PAIR)
            there = pl.ds(pl.multiple_of((ahead + 2 * block) * TILE, TILE), PAIR)
            self_term = split(feats_ref[there, :].astype(F32) - own_rel)
            count_high_ref[0, here, :] = self_term[0]
            count_high_ref[1, here, :] = self_term[1]
            mixed_ref[here, :] = dot_split(self_term, weight[2])
            return 0

        lax.fori_loop(0, blocks // 2, self_block, 0, unroll=2)
        turned = turned_ref[...]
        product = dot(turned, count_high_ref[0]) + dot(turned, count_high_ref[1])
        sums_ref[pl.ds(2 * D, D), :] = product.T


    def tile(slot, _):
        row = rows_at(row_ref[slot] % blocks, PAIR)
        col = rows_at(col_ref[slot] % source_blocks, TILE)
        backward = backward_ref[slot]
        totals_ref[row, :] += dot(forward_ref[slot], feats_ref[col, :])
        counts_ref[row, :] += counted_ref[slot].astype(F32)
        grad_ref[col, :] += dot(backward, high_ref[row, :]) + dot(backward, low_ref[row, :])
        return 0

    for part in range(CHUNKS):
        for copy in loads[3 * part : 3 * part + 3]:
            copy.wait()
        lax.fori_loop(part * chunk, (part + 1) * chunk, tile, 0, unroll=True)

    stores = []
    for part in range(4):
        here = pl.ds(part * (src_dev // 4), src_dev // 4)
        copy = pltpu.make_async_copy(grad_ref.at[here, :], grad_any.at[here, :], sems.at[2 + part])
        copy.start()
        stores.append(copy)

    relations = split(rel_pad_ref[...])

    def most(block, value):
        counts = counts_ref[rows_at(block, PAIR), :]
        return jnp.maximum(value, jnp.max(counts.reshape(PAIR // 8, 8, RELS_PAD), axis=0))

    largest = jnp.max(lax.fori_loop(0, blocks, most, jnp.zeros((8, RELS_PAD), F32)))
    large = largest > 256.0

    @pl.when(large)
    def _():
        def low_block(block, _):
            at = rows_at(block, PAIR)
            low = split(counts_ref[at, :])[1]
            totals_ref[at, :] -= dot(low, relations[0]) + dot(low, relations[1])
            return 0

        lax.fori_loop(0, blocks, low_block, 0)

    def finish_block(block, _):
        at = rows_at(block, PAIR)
        here = rows_at(block, TILE)
        counts = counts_ref[at, :].astype(BF16)
        totals = totals_ref[at, :] - (dot(counts, relations[0]) + dot(counts, relations[1]))
        pieces = [split(totals[:TILE]), split(totals[TILE:])]
        for which in range(2):
            there = pl.ds(pl.multiple_of(which * dst_dev + block * TILE, TILE), TILE)
            high_ref[there, :] = pieces[which][0]
            low_ref[there, :] = pieces[which][1]
            count_high_ref[which, here, :] = counts[which * TILE : (which + 1) * TILE]
        mixed_ref[here, :] += dot_split(pieces[0], weight[0]) + dot_split(pieces[1], weight[1])
        return 0

    lax.fori_loop(0, blocks, finish_block, 0, unroll=4)

    turned = turned_ref[...]
    grad_rel = jnp.zeros((D, RELS_PAD), F32)
    met = [dot(turned, count_high_ref[which]) for which in range(2)]
    for which in range(2):
        there = pl.ds(which * dst_dev, dst_dev)
        product = dot(turned, high_ref[there, :]) + dot(turned, low_ref[there, :])
        sums_ref[pl.ds(which * D, D), :] = product.T
        grad_rel -= dot_split(weight[which], split(met[which]))
    sums_ref[pl.ds(3 * D, RELS_PAD), :] = grad_rel.T

    @pl.when(large)
    def _():
        def low_block(block, _):
            cot = cot_ref[rows_at(block, TILE), :]
            counts = counts_ref[rows_at(block, PAIR), :]
            for which in range(2):
                low = split(counts[which * TILE : (which + 1) * TILE])[1]
                part = split(dot(low, cot, TN))
                sums_ref[pl.ds(3 * D, RELS_PAD), :] -= dot_split(part, weight[which], NT)
            return 0

        lax.fori_loop(0, blocks, low_block, 0)

    sums_ref[pl.ds(3 * D + rels_all - 1, 1), :] -= jnp.sum(self_rel_ref[...], axis=0, keepdims=True)

    for copy in stores:
        copy.wait()


def tiles_call(rows, cols, rel, weights, sources, cot, forward, backward, counted):
    dst_dev, src_dev = cot.shape[0], sources.shape[0]
    smem = pl.BlockSpec(memory_space=pltpu.SMEM)
    vmem = pl.BlockSpec(memory_space=pltpu.VMEM)
    anywhere = pl.BlockSpec(memory_space=pl.ANY)
    return pl.pallas_call(
        tiles_kernel,
        out_shape=[
            jax.ShapeDtypeStruct((src_dev, D), F32),
            jax.ShapeDtypeStruct((dst_dev, D), F32),
            jax.ShapeDtypeStruct((3 * D + RELS_PAD, D), F32),
        ],
        in_specs=[smem] * 2 + [vmem] * 2 + [anywhere] * 5,
        out_specs=[anywhere, vmem, vmem],
        scratch_shapes=[
            pltpu.VMEM(forward.shape, BF16),
            pltpu.VMEM(backward.shape, BF16),
            pltpu.VMEM(counted.shape, BF16),
            pltpu.VMEM((src_dev, D), BF16),
            pltpu.VMEM((dst_dev, D), BF16),
            pltpu.VMEM((D, dst_dev), BF16),
            pltpu.VMEM((RELS_PAD, D), F32),
            pltpu.VMEM((2 * dst_dev, D), F32),
            pltpu.VMEM((2 * dst_dev, RELS_PAD), F32),
            pltpu.VMEM((2 * dst_dev, D), BF16),
            pltpu.VMEM((2 * dst_dev, D), BF16),
            pltpu.VMEM((2, dst_dev, RELS_PAD), BF16),
            pltpu.VMEM((src_dev, D), F32),
            pltpu.VMEM((8, D), F32),
            pltpu.SemaphoreType.DMA((6 + 3 * CHUNKS,)),
        ],
        compiler_params=pltpu.CompilerParams(vmem_limit_bytes=TILES_VMEM),
        name="tiles",
    )(rows, cols, rel, weights, sources, cot, forward, backward, counted)


MESH = pl.DeviceIdType.MESH
RING = 4
HALF = TILE


class Copies:
    def __init__(self, send_sems):
        self.send_sems, self.started = send_sems, []

    def start(self, src, dst, recv, peer):
        copy = pltpu.make_async_remote_copy(
            src_ref=src,
            dst_ref=dst,
            send_sem=self.send_sems.at[len(self.started)],
            recv_sem=recv,
            device_id=peer,
            device_id_type=MESH,
        )
        copy.start()
        self.started.append(copy)

    def received(self, dst, recv):
        pltpu.make_async_remote_copy(
            src_ref=dst,
            dst_ref=dst,
            send_sem=self.send_sems.at[0],
            recv_sem=recv,
            device_id=self.any_peer,
            device_id_type=MESH,
        ).wait_recv()

    def finish(self):
        for copy in self.started:
            copy.wait_send()


class Place:
    def __init__(self):
        self.row = lax.axis_index("row")
        self.col = lax.axis_index("col")
        self.core = self.col % 2
        self.stride1 = 8 - 6 * self.core
        self.stride2 = 10 - self.stride1
        self.p1 = self.col // self.stride1 % RING
        self.p2 = self.col // self.stride2 % RING

    def col_at(self, k1, k2):
        return (self.p1 + k1) % RING * self.stride1 + (self.p2 + k2) % RING * self.stride2 + self.core

    def peer(self, k1, k2):
        return (self.row, self.col_at(k1, k2))

    def partner(self):
        return (self.row, self.col + 1 - 2 * self.core)

    def along_row(self, k, rows):
        return ((self.row + k) % rows, self.col)

    def greet(self, peers):
        barrier = pltpu.get_barrier_semaphore()
        for peer in peers:
            pl.semaphore_signal(barrier, inc=1, device_id=peer, device_id_type=MESH)
        pl.semaphore_wait(barrier, len(peers))


def run_in_order(pipes, order):
    for name in order:
        next(pipes[name], None)
    for pipe in pipes.values():
        for _ in pipe:
            pass


def gather_kernel(
    rows,
    live_ref,
    count_ref,
    ends_ref,
    relation_ref,
    dir_ref,
    feats_ref,
    cot_ref,
    sources_ref,
    targets_ref,
    forward_any,
    backward_any,
    counted_any,
    forward_ref,
    backward_ref,
    counted_ref,
    send_sems,
    shard_sems,
    row_sems,
    own_sems,
    tile_sems,
):
    place = Place()
    copies = Copies(send_sems)
    copies.any_peer = place.partner()
    own_copies = [
        pltpu.make_async_copy(feats_ref, sources_ref.at[place.col], own_sems.at[0]),
        pltpu.make_async_copy(cot_ref, targets_ref.at[place.row], own_sems.at[1]),
    ]
    for copy in own_copies:
        copy.start()
    place.greet(
        [place.partner()]
        + [place.peer(k, 0) for k in (1, 3)]
        + [place.peer(0, k) for k in (1, 3)]
        + [place.along_row(k, rows) for k in (1, rows - 1)]
    )
    parts = [pl.ds(0, HALF), pl.ds(HALF, HALF)]

    def send(array, sems, count, index, peer, half=None, src=None):
        here = array.at[index] if half is None else array.at[index, parts[half]]
        sem = sems.at[2 * count + index] if half is None else sems.at[2 * index + half]
        copies.start(here if src is None else src, here, sem, peer)

    def got(array, sems, count, index, halves=False):
        if halves:
            for half in range(2):
                copies.received(array.at[index, parts[half]], sems.at[2 * index + half])
        else:
            copies.received(array.at[index], sems.at[2 * count + index])

    send_shard = functools.partial(send, sources_ref, shard_sems, 2 * RING * RING)
    got_shard = functools.partial(got, sources_ref, shard_sems, 2 * RING * RING)
    send_row = functools.partial(send, targets_ref, row_sems, rows)
    got_row = functools.partial(got, targets_ref, row_sems, rows)

    def feats_pipe():
        for peer in (place.peer(1, 0), place.peer(3, 0), place.peer(0, 1), place.peer(0, 3), place.partner()):
            send_shard(place.col, peer, src=feats_ref)
        yield

        def spread(b):
            for peer in (place.peer(0, 1), place.peer(0, 3), place.partner()):
                send_shard(b, peer)

        left, right, far = place.col_at(3, 0), place.col_at(1, 0), place.col_at(2, 0)
        got_shard(left)
        send_shard(left, place.peer(1, 0), 0)
        spread(left)
        got_shard(right)
        send_shard(right, place.peer(3, 0), 1)
        spread(right)
        yield

        def second(k1):
            below, above = place.col_at(k1, 3), place.col_at(k1, 1)
            got_shard(below)
            send_shard(below, place.peer(0, 1), 0)
            got_shard(above)
            send_shard(above, place.peer(0, 3), 1)
            send_shard(below, place.partner())
            send_shard(above, place.partner())

        second(0)
        yield
        got_shard(far, halves=True)
        spread(far)
        yield
        second(3)
        yield
        second(1)
        yield
        second(2)
        yield
        for k1 in (0, 3, 1, 2):
            b = place.col_at(k1, 2)
            got_shard(b, halves=True)
            send_shard(b, place.partner())
        yield
        for k1 in range(RING):
            for k2 in range(RING):
                got_shard(place.col_at(k1, k2) + 1 - 2 * place.core)

    def cot_pipe():
        after, before = place.along_row(1, rows), place.along_row(rows - 1, rows)
        send_row(place.row, after, src=cot_ref)
        send_row(place.row, before, src=cot_ref)
        yield
        for k in range(1, rows // 2):
            last = k == rows // 2 - 1
            low, high = (place.row + rows - k) % rows, (place.row + k) % rows
            got_row(low)
            send_row(low, after, 0 if last else None)
            got_row(high)
            send_row(high, before, 1 if last else None)
            yield
        got_row((place.row + rows // 2) % rows, halves=True)

    pair_iota = lax.broadcasted_iota(jnp.int32, (PAIR, EDGE_TILE), 0)
    tile_iota = lax.broadcasted_iota(jnp.int32, (TILE, EDGE_TILE), 0)
    edge_iota = lax.broadcasted_iota(jnp.int32, (1, EDGE_TILE), 1)
    tile_copies = []

    def tile(slot, _):
        at = pl.ds(slot, 1)
        edges = jnp.where(slot < live_ref[0], count_ref[slot], 0)
        ends = ends_ref[at, :]
        key = dir_ref[at, :] * TILE + lax.shift_right_logical(ends, 7)
        hot_dst = hot(pair_iota, jnp.where(edge_iota < edges, key, NONE))
        hot_src = hot(tile_iota, ends & (TILE - 1))
        hot_rel = hot(pair_iota, relation_ref[at, :])
        forward_ref[slot] = dot(hot_dst, hot_src, NT).astype(BF16)
        backward_ref[slot] = dot(hot_src, hot_dst, NT).astype(BF16)
        counted_ref[slot] = dot(hot_dst, hot_rel, NT).astype(BF16)
        return 0

    def tiles_pipe():
        chunk = ends_ref.shape[0] // PREPARED
        for part in range(PREPARED):
            lax.fori_loop(part * chunk, (part + 1) * chunk, tile, 0, unroll=2)
            here = pl.ds(part * chunk, chunk)
            for which, (src, dst) in enumerate(
                ((forward_ref, forward_any), (backward_ref, backward_any), (counted_ref, counted_any))
            ):
                copy = pltpu.make_async_copy(src.at[here], dst.at[here], tile_sems.at[3 * part + which])
                copy.start()
                tile_copies.append(copy)
            yield

    run_in_order({"f": feats_pipe(), "c": cot_pipe(), "p": tiles_pipe()}, "fcppppfpfcpfppcfppfpcfpppfppcff")
    for copy in tile_copies:
        copy.wait()
    for copy in own_copies:
        copy.wait()
    copies.finish()


def gather_call(live, counts, ends, relation, direction, feats, cot, rows, cols):
    anywhere = pl.BlockSpec(memory_space=pl.ANY)
    smem = pl.BlockSpec(memory_space=pltpu.SMEM)
    vmem = pl.BlockSpec(memory_space=pltpu.VMEM)
    slots = ends.shape[0]
    shapes = [(slots, PAIR, TILE), (slots, TILE, PAIR), (slots, PAIR, RELS_PAD)]
    sources, targets, *tiles = pl.pallas_call(
        functools.partial(gather_kernel, rows),
        out_shape=[
            jax.ShapeDtypeStruct((cols,) + feats.shape, feats.dtype),
            jax.ShapeDtypeStruct((rows,) + cot.shape, cot.dtype),
        ]
        + [jax.ShapeDtypeStruct(shape, BF16) for shape in shapes],
        in_specs=[smem] * 2 + [vmem] * 3 + [anywhere] * 2,
        out_specs=[anywhere] * 5,
        scratch_shapes=[pltpu.VMEM(shape, BF16) for shape in shapes]
        + [
            pltpu.SemaphoreType.DMA((64,)),
            pltpu.SemaphoreType.DMA((3 * cols,)),
            pltpu.SemaphoreType.DMA((3 * rows,)),
            pltpu.SemaphoreType.DMA((2,)),
            pltpu.SemaphoreType.DMA((3 * PREPARED,)),
        ],
        compiler_params=pltpu.CompilerParams(
            collective_id=0, has_side_effects=True, vmem_limit_bytes=GATHER_VMEM
        ),
        name="gather",
    )(live, counts, ends, relation, direction, feats, cot)
    return [sources.reshape(-1, D), targets.reshape(-1, D)] + tiles


def reduce_kernel(
    rows,
    grad_any,
    mixed_any,
    sums_any,
    grad_out,
    mixed_out,
    sums_out,
    grad_acc,
    mixed_in,
    sums_in,
    pair_in,
    relay1,
    ring1,
    relay2,
    ring2,
    row_up,
    row_down,
    sum_pair,
    sum_first,
    sum_second,
    sum_rows,
    sum_tiles,
    send_sems,
    own_sems,
    pair_sems,
    ring_sems,
    row_sems,
    sum_sems,
    spread_sems,
):
    place = Place()
    copies = Copies(send_sems)
    copies.any_peer = place.partner()
    partner = place.partner()
    core = place.core
    order1 = (2, 1, 3, 0)
    load_sums = pltpu.make_async_copy(sums_any.at[core], sums_in, own_sems.at[16])
    load_mixed = pltpu.make_async_copy(mixed_any, mixed_in, own_sems.at[17])
    load_sums.start()
    load_mixed.start()
    own_copies = {}
    for k in order1:
        for r in (2, 1, 3, 0):
            block = place.col_at(k, r) // 2
            copy = pltpu.make_async_copy(grad_any.at[block, core], grad_acc.at[k, r], own_sems.at[4 * k + r])
            copy.start()
            own_copies[k, r] = copy
    place.greet(
        [partner]
        + [place.peer(k1, k2) for k1 in range(RING) for k2 in range(RING) if k1 or k2]
        + [place.along_row(k, rows) for k in range(1, rows)]
    )
    low, high = pl.ds(0, HALF), pl.ds(HALF, HALF)

    def grad_pipe():
        for k in order1:
            for r in (2, 1, 3, 0):
                block = ((place.p2 + k) % RING * place.stride2 + (place.p1 + r) % RING * place.stride1) // 2
                copies.start(grad_any.at[block, 1 - core], pair_in.at[k, r], pair_sems.at[4 * k + r], partner)
        yield

        def pair_sum(k, r):
            own_copies[k, r].wait()
            copies.received(pair_in.at[k, r], pair_sems.at[4 * k + r])
            grad_acc[k, r] += pair_in[k, r]

        right, left = place.peer(1, 0), place.peer(3, 0)
        for r in range(RING):
            pair_sum(2, r)
        copies.start(grad_acc.at[2, pl.ds(0, 2)], relay1.at[0], ring_sems.at[0], right)
        copies.start(grad_acc.at[2, pl.ds(2, 2)], relay1.at[1], ring_sems.at[1], left)
        yield
        for r in (2, 3):
            pair_sum(1, r)
        copies.start(grad_acc.at[1, pl.ds(2, 2)], ring1.at[0, pl.ds(2, 2)], ring_sems.at[3], right)
        for r in (0, 1):
            pair_sum(3, r)
        copies.start(grad_acc.at[3, pl.ds(0, 2)], ring1.at[1, pl.ds(0, 2)], ring_sems.at[4], left)
        yield
        for r in (0, 1):
            pair_sum(1, r)
        for r in (2, 3):
            pair_sum(3, r)
        for r in range(RING):
            pair_sum(0, r)
        yield
        copies.received(relay1.at[0], ring_sems.at[0])
        for r in (0, 1):
            grad_acc[1, r] += relay1[0, r]
        copies.start(grad_acc.at[1, pl.ds(0, 2)], ring1.at[0, pl.ds(0, 2)], ring_sems.at[2], right)
        copies.received(relay1.at[1], ring_sems.at[1])
        for r in (0, 1):
            grad_acc[3, 2 + r] += relay1[1, r]
        copies.start(grad_acc.at[3, pl.ds(2, 2)], ring1.at[1, pl.ds(2, 2)], ring_sems.at[5], left)
        yield
        copies.received(ring1.at[0, pl.ds(2, 2)], ring_sems.at[3])
        copies.received(ring1.at[1, pl.ds(0, 2)], ring_sems.at[4])
        for r in (2, 3):
            grad_acc[0, r] += ring1[0, r]
        for r in (0, 1):
            grad_acc[0, r] += ring1[1, r]
        yield
        up, down = place.peer(0, 1), place.peer(0, 3)
        copies.received(ring1.at[1, pl.ds(2, 2)], ring_sems.at[5])
        grad_acc[0, 2] += ring1[1, 2]
        copies.start(grad_acc.at[0, 2, low], relay2.at[0], ring_sems.at[6], up)
        copies.start(grad_acc.at[0, 2, high], relay2.at[1], ring_sems.at[7], down)
        grad_acc[0, 3] += ring1[1, 3]
        copies.start(grad_acc.at[0, 3, low], ring2.at[1, low], ring_sems.at[10], down)
        copies.received(ring1.at[0, pl.ds(0, 2)], ring_sems.at[2])
        grad_acc[0, 1] += ring1[0, 1]
        copies.start(grad_acc.at[0, 1, high], ring2.at[0, high], ring_sems.at[9], up)
        grad_acc[0, 0] += ring1[0, 0]
        yield
        copies.received(relay2.at[0], ring_sems.at[6])
        grad_acc[0, 1, low] += relay2[0]
        copies.start(grad_acc.at[0, 1, low], ring2.at[0, low], ring_sems.at[8], up)
        copies.received(relay2.at[1], ring_sems.at[7])
        grad_acc[0, 3, high] += relay2[1]
        copies.start(grad_acc.at[0, 3, high], ring2.at[1, high], ring_sems.at[11], down)
        yield
        copies.received(ring2.at[0, high], ring_sems.at[9])
        copies.received(ring2.at[1, low], ring_sems.at[10])
        copies.received(ring2.at[0, low], ring_sems.at[8])
        copies.received(ring2.at[1, high], ring_sems.at[11])
        grad_out[...] = grad_acc[0, 0] + ring2[0] + ring2[1]

    def mixed_pipe():
        after, before = place.along_row(1, rows), place.along_row(rows - 1, rows)
        copies.start(mixed_any.at[(place.row + rows - 1) % rows, low], row_up.at[0], row_sems.at[0], after)
        copies.start(mixed_any.at[(place.row + 1) % rows, high], row_down.at[0], row_sems.at[rows], before)
        yield
        load_mixed.wait()
        for step in range(1, rows):
            copies.received(row_up.at[step - 1], row_sems.at[step - 1])
            row_up[step - 1] += mixed_in[(place.row + 2 * rows - 1 - step) % rows, low]
            if step < rows - 1:
                copies.start(row_up.at[step - 1], row_up.at[step], row_sems.at[step], after)
            copies.received(row_down.at[step - 1], row_sems.at[rows + step - 1])
            row_down[step - 1] += mixed_in[(place.row + 1 + step) % rows, high]
            if step < rows - 1:
                copies.start(row_down.at[step - 1], row_down.at[step], row_sems.at[rows + step], before)
            yield
        mixed_out[low] = row_up[rows - 2]
        mixed_out[high] = row_down[rows - 2]

    def sums_pipe():
        copies.start(sums_any.at[1 - core], sum_pair, sum_sems.at[0], partner)
        yield
        load_sums.wait()
        copies.received(sum_pair, sum_sems.at[0])
        for q in range(RING):
            sum_pair[q] += sums_in[q]
        for k in (2, 1, 3):
            copies.start(sum_pair.at[(place.p1 + k) % RING], sum_first.at[k], sum_sems.at[k], place.peer(k, 0))
        sum_first[0] = sum_pair[place.p1]
        yield
        for k in (1, 3, 2):
            copies.received(sum_first.at[k], sum_sems.at[k])
            sum_first[0] += sum_first[k]
        for k in (2, 1, 3):
            copies.start(sum_first.at[0, (place.p2 + k) % RING], sum_second.at[k], sum_sems.at[3 + k], place.peer(0, k))
        sum_second[0] = sum_first[0, place.p2]
        yield
        for k in (1, 3, 2):
            copies.received(sum_second.at[k], sum_sems.at[3 + k])
            sum_second[0] += sum_second[k]
        for quarter in range(RING):
            for side in range(2):
                sum_tiles[2 * quarter + side] = sum_second[0, pl.ds(8 * quarter, 8), pl.ds(TILE * side, TILE)]
        for k in (4, 3, 5, 2, 6, 1, 7):
            copies.start(
                sum_tiles.at[(place.row + k) % rows], sum_rows.at[k], sum_sems.at[6 + k], place.along_row(k, rows)
            )
        sum_rows[0] = sum_tiles[place.row]
        yield
        for k in (1, 7, 2, 6, 3, 5, 4):
            copies.received(sum_rows.at[k], sum_sems.at[6 + k])
            sum_rows[0] += sum_rows[k]
        for k in (4, 3, 5, 2, 6, 1, 7):
            copies.start(
                sum_rows.at[0], sum_tiles.at[rows + place.row], sum_sems.at[13 + k], place.along_row(k, rows)
            )
        sum_tiles[rows + place.row] = sum_rows[0]
        yield
        for k in (1, 7, 2, 6, 3, 5, 4):
            copies.received(sum_tiles.at[rows + (place.row + rows - k) % rows], sum_sems.at[13 + k])
        own = sums_out.at[core, place.p1, place.p2]
        for quarter in range(RING):
            for side in range(2):
                own[pl.ds(8 * quarter, 8), pl.ds(TILE * side, TILE)] = sum_tiles[rows + 2 * quarter + side]
        for k in (2, 1, 3):
            copies.start(own, own, spread_sems.at[k], place.peer(0, k))
        yield
        for k in (1, 3, 2):
            copies.received(sums_out.at[core, place.p1, (place.p2 + RING - k) % RING], spread_sems.at[k])
        line = sums_out.at[core, place.p1]
        for k in (2, 1, 3):
            copies.start(line, line, spread_sems.at[3 + k], place.peer(k, 0))
        yield
        copies.start(line, line, spread_sems.at[7], partner)
        for k in (1, 3, 2):
            there = sums_out.at[core, (place.p1 + RING - k) % RING]
            copies.received(there, spread_sems.at[3 + k])
            copies.start(there, there, spread_sems.at[7 + k], partner)
        yield
        copies.received(sums_out.at[1 - core, place.p2], spread_sems.at[7])
        for k in (1, 3, 2):
            copies.received(sums_out.at[1 - core, (place.p2 + RING - k) % RING], spread_sems.at[7 + k])

    run_in_order(
        {"s": sums_pipe(), "m": mixed_pipe(), "g": grad_pipe()},
        "smgsmgsmgsmgsmgsmgsmgsmgmg",
    )
    copies.finish()


def reduce_call(grad, mixed, sums, rows, cols):
    anywhere = pl.BlockSpec(memory_space=pl.ANY)
    vmem = pl.BlockSpec(memory_space=pltpu.VMEM)
    ent_dev = grad.shape[0] // cols
    block = (ent_dev, D)
    share = sums.shape[0] // cols
    grad_out, mixed_out, sums_out = pl.pallas_call(
        functools.partial(reduce_kernel, rows),
        out_shape=[
            jax.ShapeDtypeStruct(block, F32),
            jax.ShapeDtypeStruct(block, F32),
            jax.ShapeDtypeStruct((2, RING, RING, share, D), F32),
        ],
        in_specs=[anywhere] * 3,
        out_specs=[vmem] * 3,
        scratch_shapes=[
            pltpu.VMEM((RING, RING) + block, F32),
            pltpu.VMEM((rows,) + block, F32),
            pltpu.VMEM((RING, RING, share, D), F32),
            pltpu.VMEM((RING, RING) + block, F32),
            pltpu.VMEM((2, 2) + block, F32),
            pltpu.VMEM((2, RING) + block, F32),
            pltpu.VMEM((2, HALF, D), F32),
            pltpu.VMEM((2,) + block, F32),
            pltpu.VMEM((rows - 1, HALF, D), F32),
            pltpu.VMEM((rows - 1, HALF, D), F32),
            pltpu.VMEM((RING, RING, share, D), F32),
            pltpu.VMEM((RING, RING, share, D), F32),
            pltpu.VMEM((RING, share, D), F32),
            pltpu.VMEM((rows, 8, TILE), F32),
            pltpu.VMEM((2 * rows, 8, TILE), F32),
            pltpu.SemaphoreType.DMA((96,)),
            pltpu.SemaphoreType.DMA((18,)),
            pltpu.SemaphoreType.DMA((16,)),
            pltpu.SemaphoreType.DMA((12,)),
            pltpu.SemaphoreType.DMA((2 * rows,)),
            pltpu.SemaphoreType.DMA((24,)),
            pltpu.SemaphoreType.DMA((16,)),
        ],
        compiler_params=pltpu.CompilerParams(
            collective_id=1, has_side_effects=True, vmem_limit_bytes=REDUCE_VMEM
        ),
        name="reduce",
    )(
        grad.reshape((cols // 2, 2) + block),
        mixed.reshape((rows,) + block),
        sums.reshape(2, RING, RING, share, D),
    )
    return grad_out, mixed_out, sums_out.reshape(-1, D)


def shards(
    feats,
    rel_embed,
    weights,
    cot,
    tile_row,
    tile_col,
    tile_live,
    edge_ends,
    edge_relation,
    edge_dir,
    edge_count,
):
    rows_n, cols_n = lax.axis_size("row"), lax.axis_size("col")
    sources, targets, *tiles = gather_call(
        tile_live, edge_count, edge_ends, edge_relation, edge_dir, feats, cot, rows_n, cols_n
    )
    grad, mixed, sums = tiles_call(tile_row, tile_col, rel_embed, weights, sources, targets, *tiles)
    rels_all = rel_embed.shape[0]
    grad_feats, mixed, sums = reduce_call(grad, mixed, sums, rows_n, cols_n)
    grad_rel = sums[3 * D : 3 * D + rels_all]
    return (mixed, grad_feats, grad_rel, sums[: 3 * D].reshape(3, D, D))


def solution(mesh):
    return jax.shard_map(
        shards,
        mesh=mesh,
        in_specs=(
            P(("row", "col"), None),
            P(),
            P(),
            P(("col", "row"), None),
            P(("row", "col")),
            P(("row", "col")),
            P(("row", "col")),
            P(("row", "col"), None),
            P(("row", "col"), None),
            P(("row", "col"), None),
            P(("row", "col")),
        ),
        out_specs=(P(("col", "row"), None), P(("row", "col"), None), P(), P()),
        check_vma=False,
    )
```

```python
import functools

import jax
import jax.numpy as jnp
from jax import lax
from jax.experimental import pallas as pl
from jax.experimental.pallas import tpu as pltpu
from jax.sharding import PartitionSpec as P

D = 256
TILE = 128
EDGE_TILE = 256
PAIR = 2 * TILE
RELS_PAD = 256
NONE = 1024
CHUNKS = 8
PREPARED = 16
GATHER_VMEM = 60 * 1024 * 1024
TILES_VMEM = 60 * 1024 * 1024
REDUCE_VMEM = 52 * 1024 * 1024
F32 = jnp.float32
BF16 = jnp.bfloat16
NN = (((1,), (0,)), ((), ()))
NT = (((1,), (1,)), ((), ()))
TN = (((0,), (0,)), ((), ()))


def dot(left, right, dims=NN):
    return lax.dot_general(left, right, dims, preferred_element_type=F32)


def split(value):
    high = value.astype(BF16)
    return high, (value - high.astype(F32)).astype(BF16)


def dot_exact_left(left, right, dims=NN):
    high, low = right
    return dot(left, high, dims) + dot(left, low, dims)


def dot_exact_right(left, right, dims=NN):
    high, low = left
    return dot(high, right, dims) + dot(low, right, dims)


def dot_split(left, right, dims=NN):
    return dot(left[0], right[0], dims) + (dot(left[0], right[1], dims) + dot(left[1], right[0], dims))


def rows_at(index, size):
    return pl.ds(pl.multiple_of(index * size, size), size)


def hot(iota, entries):
    return jnp.where(iota == entries, 1.0, 0.0).astype(BF16)


def tiles_kernel(
    row_ref,
    col_ref,
    rel_ref,
    weights_ref,
    feats_any,
    cot_any,
    forward_any,
    backward_any,
    counted_any,
    grad_any,
    mixed_ref,
    sums_ref,
    forward_ref,
    backward_ref,
    counted_ref,
    feats_ref,
    cot_ref,
    turned_ref,
    rel_pad_ref,
    totals_ref,
    counts_ref,
    high_ref,
    low_ref,
    count_high_ref,
    grad_ref,
    self_rel_ref,
    self_sum_ref,
    sems,
):
    slots = forward_ref.shape[0]
    dst_dev, src_dev = cot_ref.shape[0], feats_ref.shape[0]
    blocks, source_blocks = dst_dev // TILE, src_dev // TILE
    rels_all = rel_ref.shape[0]
    col_index = row_ref[0] // blocks
    row_index = col_ref[0] // source_blocks
    ahead = col_index * blocks - row_index * source_blocks
    owner = (ahead >= 0) & (ahead < source_blocks)
    load_cot = pltpu.make_async_copy(cot_any, cot_ref, sems.at[0])
    load_feats = pltpu.make_async_copy(feats_any, feats_ref, sems.at[1])
    load_cot.start()
    load_feats.start()

    chunk = slots // CHUNKS
    loads = []
    for part in range(CHUNKS):
        here = pl.ds(part * chunk, chunk)
        for which, (src, dst) in enumerate(
            ((forward_any, forward_ref), (backward_any, backward_ref), (counted_any, counted_ref))
        ):
            copy = pltpu.make_async_copy(src.at[here], dst.at[here], sems.at[6 + 3 * part + which])
            copy.start()
            loads.append(copy)
    rel_pad_ref[...] = jnp.zeros_like(rel_pad_ref)
    rel_pad_ref[pl.ds(0, rels_all), :] = rel_ref[...]
    weight = [split(weights_ref[which]) for which in range(3)]

    def clear_block(block, _):
        grad_ref[rows_at(block, PAIR), :] = jnp.zeros((PAIR, D), F32)
        return 0

    lax.fori_loop(0, src_dev // PAIR, clear_block, 0)
    sums_ref[pl.ds(2 * D, D), :] = jnp.zeros((D, D), F32)
    self_rel_ref[...] = jnp.zeros_like(self_rel_ref)
    load_cot.wait()

    def image_block(block, _):
        cot = cot_ref[rows_at(block, TILE), :]
        turned_ref[:, rows_at(block, TILE)] = cot.T
        at = rows_at(block, PAIR)
        for which in range(2):
            high, low = split(dot_exact_left(cot, weight[which], NT))
            part = pl.ds(pl.multiple_of(block * PAIR + which * TILE, TILE), TILE)
            high_ref[part, :] = high
            low_ref[part, :] = low
        totals_ref[at, :] = jnp.zeros((PAIR, D), F32)
        counts_ref[at, :] = jnp.zeros((PAIR, RELS_PAD), F32)
        mixed_ref[rows_at(block, TILE), :] = jnp.zeros((TILE, D), F32)
        return 0

    lax.fori_loop(0, blocks, image_block, 0, unroll=2)

    @pl.when(owner)
    def _():
        def self_image(block, total):
            cot = cot_ref[rows_at(block, PAIR), :]
            grad_ref[pl.ds(pl.multiple_of((ahead + 2 * block) * TILE, TILE), PAIR), :] = dot_exact_left(
                cot, weight[2], NT
            )
            return total + jnp.sum(cot.astype(F32).reshape(PAIR // 8, 8, D), axis=0)

        self_sum_ref[...] = lax.fori_loop(0, blocks // 2, self_image, jnp.zeros((8, D), F32), unroll=2)

    load_feats.wait()

    @pl.when(owner)
    def _():
        own_rel = split(jnp.broadcast_to(rel_ref[pl.ds(rels_all - 1, 1), :], (8, D)))
        rel_image = dot_split(own_rel, weight[2])[:1]

        def self_block(block, _):
            there = pl.ds(pl.multiple_of((ahead + 2 * block) * TILE, TILE), PAIR)
            mixed_ref[rows_at(block, PAIR), :] = dot_exact_left(feats_ref[there, :], weight[2]) - rel_image
            return 0

        lax.fori_loop(0, blocks // 2, self_block, 0, unroll=2)
        there = pl.ds(pl.multiple_of(ahead * TILE, TILE), dst_dev)
        own_sum = split(self_sum_ref[...])
        sums_ref[pl.ds(2 * D, D), :] = dot(turned_ref[...], feats_ref[there, :]).T - dot_split(own_rel, own_sum, TN)
        self_rel_ref[...] = dot_split(own_sum, weight[2], NT)

    def tile(slot, _):
        row = rows_at(row_ref[slot] % blocks, PAIR)
        col = rows_at(col_ref[slot] % source_blocks, TILE)
        backward = backward_ref[slot]
        totals_ref[row, :] += dot(forward_ref[slot], feats_ref[col, :])
        counts_ref[row, :] += counted_ref[slot].astype(F32)
        grad_ref[col, :] += dot(backward, high_ref[row, :]) + dot(backward, low_ref[row, :])
        return 0

    for part in range(CHUNKS):
        for copy in loads[3 * part : 3 * part + 3]:
            copy.wait()
        lax.fori_loop(part * chunk, (part + 1) * chunk, tile, 0, unroll=True)

    stores = []
    for part in range(4):
        here = pl.ds(part * (src_dev // 4), src_dev // 4)
        copy = pltpu.make_async_copy(grad_ref.at[here, :], grad_any.at[here, :], sems.at[2 + part])
        copy.start()
        stores.append(copy)

    relations = split(rel_pad_ref[...])

    def most(block, value):
        counts = counts_ref[rows_at(block, PAIR), :]
        return jnp.maximum(value, jnp.max(counts.reshape(PAIR // 8, 8, RELS_PAD), axis=0))

    largest = jnp.max(lax.fori_loop(0, blocks, most, jnp.zeros((8, RELS_PAD), F32)))
    large = largest > 256.0

    @pl.when(large)
    def _():
        def low_block(block, _):
            at = rows_at(block, PAIR)
            low = split(counts_ref[at, :])[1]
            totals_ref[at, :] -= dot(low, relations[0]) + dot(low, relations[1])
            return 0

        lax.fori_loop(0, blocks, low_block, 0)

    def finish_block(block, _):
        at = rows_at(block, PAIR)
        here = rows_at(block, TILE)
        counts = counts_ref[at, :].astype(BF16)
        totals = totals_ref[at, :] - (dot(counts, relations[0]) + dot(counts, relations[1]))
        pieces = [split(totals[:TILE]), split(totals[TILE:])]
        for which in range(2):
            there = pl.ds(pl.multiple_of(which * dst_dev + block * TILE, TILE), TILE)
            high_ref[there, :] = pieces[which][0]
            low_ref[there, :] = pieces[which][1]
            count_high_ref[which, here, :] = counts[which * TILE : (which + 1) * TILE]
        mixed_ref[here, :] += dot_split(pieces[0], weight[0]) + dot_split(pieces[1], weight[1])
        return 0

    lax.fori_loop(0, blocks, finish_block, 0, unroll=4)

    turned = turned_ref[...]
    grad_rel = jnp.zeros((D, RELS_PAD), F32)
    met = [dot(turned, count_high_ref[which]) for which in range(2)]
    for which in range(2):
        there = pl.ds(which * dst_dev, dst_dev)
        product = dot(turned, high_ref[there, :]) + dot(turned, low_ref[there, :])
        sums_ref[pl.ds(which * D, D), :] = product.T
        grad_rel -= dot_split(weight[which], split(met[which]))
    sums_ref[pl.ds(3 * D, RELS_PAD), :] = grad_rel.T

    @pl.when(large)
    def _():
        def low_block(block, _):
            cot = cot_ref[rows_at(block, TILE), :]
            counts = counts_ref[rows_at(block, PAIR), :]
            for which in range(2):
                low = split(counts[which * TILE : (which + 1) * TILE])[1]
                part = split(dot(low, cot, TN))
                sums_ref[pl.ds(3 * D, RELS_PAD), :] -= dot_split(part, weight[which], NT)
            return 0

        lax.fori_loop(0, blocks, low_block, 0)

    sums_ref[pl.ds(3 * D + rels_all - 1, 1), :] -= jnp.sum(self_rel_ref[...], axis=0, keepdims=True)

    for copy in stores:
        copy.wait()


def tiles_call(rows, cols, rel, weights, sources, cot, forward, backward, counted):
    dst_dev, src_dev = cot.shape[0], sources.shape[0]
    smem = pl.BlockSpec(memory_space=pltpu.SMEM)
    vmem = pl.BlockSpec(memory_space=pltpu.VMEM)
    anywhere = pl.BlockSpec(memory_space=pl.ANY)
    return pl.pallas_call(
        tiles_kernel,
        out_shape=[
            jax.ShapeDtypeStruct((src_dev, D), F32),
            jax.ShapeDtypeStruct((dst_dev, D), F32),
            jax.ShapeDtypeStruct((3 * D + RELS_PAD, D), F32),
        ],
        in_specs=[smem] * 2 + [vmem] * 2 + [anywhere] * 5,
        out_specs=[anywhere, vmem, vmem],
        scratch_shapes=[
            pltpu.VMEM(forward.shape, BF16),
            pltpu.VMEM(backward.shape, BF16),
            pltpu.VMEM(counted.shape, BF16),
            pltpu.VMEM((src_dev, D), BF16),
            pltpu.VMEM((dst_dev, D), BF16),
            pltpu.VMEM((D, dst_dev), BF16),
            pltpu.VMEM((RELS_PAD, D), F32),
            pltpu.VMEM((2 * dst_dev, D), F32),
            pltpu.VMEM((2 * dst_dev, RELS_PAD), F32),
            pltpu.VMEM((2 * dst_dev, D), BF16),
            pltpu.VMEM((2 * dst_dev, D), BF16),
            pltpu.VMEM((2, dst_dev, RELS_PAD), BF16),
            pltpu.VMEM((src_dev, D), F32),
            pltpu.VMEM((8, D), F32),
            pltpu.VMEM((8, D), F32),
            pltpu.SemaphoreType.DMA((6 + 3 * CHUNKS,)),
        ],
        compiler_params=pltpu.CompilerParams(vmem_limit_bytes=TILES_VMEM),
        name="tiles",
    )(rows, cols, rel, weights, sources, cot, forward, backward, counted)


MESH = pl.DeviceIdType.MESH
RING = 4
HALF = TILE


class Copies:
    def __init__(self, send_sems):
        self.send_sems, self.started = send_sems, []

    def start(self, src, dst, recv, peer):
        copy = pltpu.make_async_remote_copy(
            src_ref=src,
            dst_ref=dst,
            send_sem=self.send_sems.at[len(self.started)],
            recv_sem=recv,
            device_id=peer,
            device_id_type=MESH,
        )
        copy.start()
        self.started.append(copy)

    def received(self, dst, recv):
        pltpu.make_async_remote_copy(
            src_ref=dst,
            dst_ref=dst,
            send_sem=self.send_sems.at[0],
            recv_sem=recv,
            device_id=self.any_peer,
            device_id_type=MESH,
        ).wait_recv()

    def finish(self):
        for copy in self.started:
            copy.wait_send()


class Place:
    def __init__(self):
        self.row = lax.axis_index("row")
        self.col = lax.axis_index("col")
        self.core = self.col % 2
        self.stride1 = 8 - 6 * self.core
        self.stride2 = 10 - self.stride1
        self.p1 = self.col // self.stride1 % RING
        self.p2 = self.col // self.stride2 % RING

    def col_at(self, k1, k2):
        return (self.p1 + k1) % RING * self.stride1 + (self.p2 + k2) % RING * self.stride2 + self.core

    def peer(self, k1, k2):
        return (self.row, self.col_at(k1, k2))

    def partner(self):
        return (self.row, self.col + 1 - 2 * self.core)

    def along_row(self, k, rows):
        return ((self.row + k) % rows, self.col)

    def greet(self, peers):
        barrier = pltpu.get_barrier_semaphore()
        for peer in peers:
            pl.semaphore_signal(barrier, inc=1, device_id=peer, device_id_type=MESH)
        pl.semaphore_wait(barrier, len(peers))


def run_in_order(pipes, order):
    for name in order:
        next(pipes[name], None)
    for pipe in pipes.values():
        for _ in pipe:
            pass


def gather_kernel(
    rows,
    live_ref,
    count_ref,
    ends_ref,
    relation_ref,
    dir_ref,
    feats_ref,
    cot_ref,
    sources_ref,
    targets_ref,
    forward_any,
    backward_any,
    counted_any,
    forward_ref,
    backward_ref,
    counted_ref,
    send_sems,
    shard_sems,
    row_sems,
    own_sems,
    tile_sems,
):
    place = Place()
    copies = Copies(send_sems)
    copies.any_peer = place.partner()
    own_copies = [
        pltpu.make_async_copy(feats_ref, sources_ref.at[place.col], own_sems.at[0]),
        pltpu.make_async_copy(cot_ref, targets_ref.at[place.row], own_sems.at[1]),
    ]
    for copy in own_copies:
        copy.start()
    place.greet(
        [place.partner()]
        + [place.peer(k, 0) for k in (1, 3)]
        + [place.peer(0, k) for k in (1, 3)]
        + [place.along_row(k, rows) for k in (1, rows - 1)]
    )
    parts = [pl.ds(0, HALF), pl.ds(HALF, HALF)]

    def send(array, sems, count, index, peer, half=None, src=None):
        here = array.at[index] if half is None else array.at[index, parts[half]]
        sem = sems.at[2 * count + index] if half is None else sems.at[2 * index + half]
        copies.start(here if src is None else src, here, sem, peer)

    def got(array, sems, count, index, halves=False):
        if halves:
            for half in range(2):
                copies.received(array.at[index, parts[half]], sems.at[2 * index + half])
        else:
            copies.received(array.at[index], sems.at[2 * count + index])

    send_shard = functools.partial(send, sources_ref, shard_sems, 2 * RING * RING)
    got_shard = functools.partial(got, sources_ref, shard_sems, 2 * RING * RING)
    send_row = functools.partial(send, targets_ref, row_sems, rows)
    got_row = functools.partial(got, targets_ref, row_sems, rows)

    def feats_pipe():
        for peer in (place.peer(1, 0), place.peer(3, 0), place.peer(0, 1), place.peer(0, 3), place.partner()):
            send_shard(place.col, peer, src=feats_ref)
        yield

        def spread(b):
            for peer in (place.peer(0, 1), place.peer(0, 3), place.partner()):
                send_shard(b, peer)

        left, right, far = place.col_at(3, 0), place.col_at(1, 0), place.col_at(2, 0)
        got_shard(left)
        send_shard(left, place.peer(1, 0), 0)
        spread(left)
        got_shard(right)
        send_shard(right, place.peer(3, 0), 1)
        spread(right)
        yield

        def second(k1):
            below, above = place.col_at(k1, 3), place.col_at(k1, 1)
            got_shard(below)
            send_shard(below, place.peer(0, 1), 0)
            got_shard(above)
            send_shard(above, place.peer(0, 3), 1)
            send_shard(below, place.partner())
            send_shard(above, place.partner())

        second(0)
        yield
        got_shard(far, halves=True)
        spread(far)
        yield
        second(3)
        yield
        second(1)
        yield
        second(2)
        yield
        for k1 in (0, 3, 1, 2):
            b = place.col_at(k1, 2)
            got_shard(b, halves=True)
            send_shard(b, place.partner())
        yield
        for k1 in range(RING):
            for k2 in range(RING):
                got_shard(place.col_at(k1, k2) + 1 - 2 * place.core)

    def cot_pipe():
        after, before = place.along_row(1, rows), place.along_row(rows - 1, rows)
        send_row(place.row, after, src=cot_ref)
        send_row(place.row, before, src=cot_ref)
        yield
        for k in range(1, rows // 2):
            last = k == rows // 2 - 1
            low, high = (place.row + rows - k) % rows, (place.row + k) % rows
            got_row(low)
            send_row(low, after, 0 if last else None)
            got_row(high)
            send_row(high, before, 1 if last else None)
            yield
        got_row((place.row + rows // 2) % rows, halves=True)

    pair_iota = lax.broadcasted_iota(jnp.int32, (PAIR, EDGE_TILE), 0)
    tile_iota = lax.broadcasted_iota(jnp.int32, (TILE, EDGE_TILE), 0)
    edge_iota = lax.broadcasted_iota(jnp.int32, (1, EDGE_TILE), 1)
    tile_copies = []

    def tile(slot, _):
        at = pl.ds(slot, 1)
        edges = jnp.where(slot < live_ref[0], count_ref[slot], 0)
        ends = ends_ref[at, :]
        key = dir_ref[at, :] * TILE + lax.shift_right_logical(ends, 7)
        hot_dst = hot(pair_iota, jnp.where(edge_iota < edges, key, NONE))
        hot_src = hot(tile_iota, ends & (TILE - 1))
        hot_rel = hot(pair_iota, relation_ref[at, :])
        forward_ref[slot] = dot(hot_dst, hot_src, NT).astype(BF16)
        backward_ref[slot] = dot(hot_src, hot_dst, NT).astype(BF16)
        counted_ref[slot] = dot(hot_dst, hot_rel, NT).astype(BF16)
        return 0

    def tiles_pipe():
        chunk = ends_ref.shape[0] // PREPARED
        for part in range(PREPARED):
            lax.fori_loop(part * chunk, (part + 1) * chunk, tile, 0, unroll=2)
            here = pl.ds(part * chunk, chunk)
            for which, (src, dst) in enumerate(
                ((forward_ref, forward_any), (backward_ref, backward_any), (counted_ref, counted_any))
            ):
                copy = pltpu.make_async_copy(src.at[here], dst.at[here], tile_sems.at[3 * part + which])
                copy.start()
                tile_copies.append(copy)
            yield

    run_in_order({"f": feats_pipe(), "c": cot_pipe(), "p": tiles_pipe()}, "fcppppfpfcpfppcfppfpcfpppfppcff")
    for copy in tile_copies:
        copy.wait()
    for copy in own_copies:
        copy.wait()
    copies.finish()


def gather_call(live, counts, ends, relation, direction, feats, cot, rows, cols):
    anywhere = pl.BlockSpec(memory_space=pl.ANY)
    smem = pl.BlockSpec(memory_space=pltpu.SMEM)
    vmem = pl.BlockSpec(memory_space=pltpu.VMEM)
    slots = ends.shape[0]
    shapes = [(slots, PAIR, TILE), (slots, TILE, PAIR), (slots, PAIR, RELS_PAD)]
    sources, targets, *tiles = pl.pallas_call(
        functools.partial(gather_kernel, rows),
        out_shape=[
            jax.ShapeDtypeStruct((cols,) + feats.shape, feats.dtype),
            jax.ShapeDtypeStruct((rows,) + cot.shape, cot.dtype),
        ]
        + [jax.ShapeDtypeStruct(shape, BF16) for shape in shapes],
        in_specs=[smem] * 2 + [vmem] * 3 + [anywhere] * 2,
        out_specs=[anywhere] * 5,
        scratch_shapes=[pltpu.VMEM(shape, BF16) for shape in shapes]
        + [
            pltpu.SemaphoreType.DMA((64,)),
            pltpu.SemaphoreType.DMA((3 * cols,)),
            pltpu.SemaphoreType.DMA((3 * rows,)),
            pltpu.SemaphoreType.DMA((2,)),
            pltpu.SemaphoreType.DMA((3 * PREPARED,)),
        ],
        compiler_params=pltpu.CompilerParams(
            collective_id=0, has_side_effects=True, vmem_limit_bytes=GATHER_VMEM
        ),
        name="gather",
    )(live, counts, ends, relation, direction, feats, cot)
    return [sources.reshape(-1, D), targets.reshape(-1, D)] + tiles


def reduce_kernel(
    rows,
    grad_any,
    mixed_any,
    sums_any,
    grad_out,
    mixed_out,
    sums_out,
    grad_acc,
    mixed_in,
    sums_in,
    pair_in,
    relay1,
    ring1,
    relay2,
    ring2,
    row_up,
    row_down,
    sum_pair,
    sum_first,
    sum_second,
    sum_rows,
    sum_tiles,
    send_sems,
    own_sems,
    pair_sems,
    ring_sems,
    row_sems,
    sum_sems,
    spread_sems,
):
    place = Place()
    copies = Copies(send_sems)
    copies.any_peer = place.partner()
    partner = place.partner()
    core = place.core
    order1 = (2, 1, 3, 0)
    load_sums = pltpu.make_async_copy(sums_any.at[core], sums_in, own_sems.at[16])
    load_mixed = pltpu.make_async_copy(mixed_any, mixed_in, own_sems.at[17])
    load_sums.start()
    load_mixed.start()
    own_copies = {}
    for k in order1:
        for r in (2, 1, 3, 0):
            block = place.col_at(k, r) // 2
            copy = pltpu.make_async_copy(grad_any.at[block, core], grad_acc.at[k, r], own_sems.at[4 * k + r])
            copy.start()
            own_copies[k, r] = copy
    place.greet(
        [partner]
        + [place.peer(k1, k2) for k1 in range(RING) for k2 in range(RING) if k1 or k2]
        + [place.along_row(k, rows) for k in range(1, rows)]
    )
    low, high = pl.ds(0, HALF), pl.ds(HALF, HALF)

    def grad_pipe():
        for k in order1:
            for r in (2, 1, 3, 0):
                block = ((place.p2 + k) % RING * place.stride2 + (place.p1 + r) % RING * place.stride1) // 2
                copies.start(grad_any.at[block, 1 - core], pair_in.at[k, r], pair_sems.at[4 * k + r], partner)
        yield

        def pair_sum(k, r):
            own_copies[k, r].wait()
            copies.received(pair_in.at[k, r], pair_sems.at[4 * k + r])
            grad_acc[k, r] += pair_in[k, r]

        right, left = place.peer(1, 0), place.peer(3, 0)
        for r in range(RING):
            pair_sum(2, r)
        copies.start(grad_acc.at[2, pl.ds(0, 2)], relay1.at[0], ring_sems.at[0], right)
        copies.start(grad_acc.at[2, pl.ds(2, 2)], relay1.at[1], ring_sems.at[1], left)
        yield
        for r in (2, 3):
            pair_sum(1, r)
        copies.start(grad_acc.at[1, pl.ds(2, 2)], ring1.at[0, pl.ds(2, 2)], ring_sems.at[3], right)
        for r in (0, 1):
            pair_sum(3, r)
        copies.start(grad_acc.at[3, pl.ds(0, 2)], ring1.at[1, pl.ds(0, 2)], ring_sems.at[4], left)
        yield
        for r in (0, 1):
            pair_sum(1, r)
        for r in (2, 3):
            pair_sum(3, r)
        for r in range(RING):
            pair_sum(0, r)
        yield
        copies.received(relay1.at[0], ring_sems.at[0])
        for r in (0, 1):
            grad_acc[1, r] += relay1[0, r]
        copies.start(grad_acc.at[1, pl.ds(0, 2)], ring1.at[0, pl.ds(0, 2)], ring_sems.at[2], right)
        copies.received(relay1.at[1], ring_sems.at[1])
        for r in (0, 1):
            grad_acc[3, 2 + r] += relay1[1, r]
        copies.start(grad_acc.at[3, pl.ds(2, 2)], ring1.at[1, pl.ds(2, 2)], ring_sems.at[5], left)
        yield
        copies.received(ring1.at[0, pl.ds(2, 2)], ring_sems.at[3])
        copies.received(ring1.at[1, pl.ds(0, 2)], ring_sems.at[4])
        for r in (2, 3):
            grad_acc[0, r] += ring1[0, r]
        for r in (0, 1):
            grad_acc[0, r] += ring1[1, r]
        yield
        up, down = place.peer(0, 1), place.peer(0, 3)
        copies.received(ring1.at[1, pl.ds(2, 2)], ring_sems.at[5])
        grad_acc[0, 2] += ring1[1, 2]
        copies.start(grad_acc.at[0, 2, low], relay2.at[0], ring_sems.at[6], up)
        copies.start(grad_acc.at[0, 2, high], relay2.at[1], ring_sems.at[7], down)
        grad_acc[0, 3] += ring1[1, 3]
        copies.start(grad_acc.at[0, 3, low], ring2.at[1, low], ring_sems.at[10], down)
        copies.received(ring1.at[0, pl.ds(0, 2)], ring_sems.at[2])
        grad_acc[0, 1] += ring1[0, 1]
        copies.start(grad_acc.at[0, 1, high], ring2.at[0, high], ring_sems.at[9], up)
        grad_acc[0, 0] += ring1[0, 0]
        yield
        copies.received(relay2.at[0], ring_sems.at[6])
        grad_acc[0, 1, low] += relay2[0]
        copies.start(grad_acc.at[0, 1, low], ring2.at[0, low], ring_sems.at[8], up)
        copies.received(relay2.at[1], ring_sems.at[7])
        grad_acc[0, 3, high] += relay2[1]
        copies.start(grad_acc.at[0, 3, high], ring2.at[1, high], ring_sems.at[11], down)
        yield
        copies.received(ring2.at[0, high], ring_sems.at[9])
        copies.received(ring2.at[1, low], ring_sems.at[10])
        copies.received(ring2.at[0, low], ring_sems.at[8])
        copies.received(ring2.at[1, high], ring_sems.at[11])
        grad_out[...] = grad_acc[0, 0] + ring2[0] + ring2[1]

    def mixed_pipe():
        after, before = place.along_row(1, rows), place.along_row(rows - 1, rows)
        copies.start(mixed_any.at[(place.row + rows - 1) % rows, low], row_up.at[0], row_sems.at[0], after)
        copies.start(mixed_any.at[(place.row + 1) % rows, high], row_down.at[0], row_sems.at[rows], before)
        yield
        load_mixed.wait()
        for step in range(1, rows):
            copies.received(row_up.at[step - 1], row_sems.at[step - 1])
            row_up[step - 1] += mixed_in[(place.row + 2 * rows - 1 - step) % rows, low]
            if step < rows - 1:
                copies.start(row_up.at[step - 1], row_up.at[step], row_sems.at[step], after)
            copies.received(row_down.at[step - 1], row_sems.at[rows + step - 1])
            row_down[step - 1] += mixed_in[(place.row + 1 + step) % rows, high]
            if step < rows - 1:
                copies.start(row_down.at[step - 1], row_down.at[step], row_sems.at[rows + step], before)
            yield
        mixed_out[low] = row_up[rows - 2]
        mixed_out[high] = row_down[rows - 2]

    def sums_pipe():
        copies.start(sums_any.at[1 - core], sum_pair, sum_sems.at[0], partner)
        yield
        load_sums.wait()
        copies.received(sum_pair, sum_sems.at[0])
        for q in range(RING):
            sum_pair[q] += sums_in[q]
        for k in (2, 1, 3):
            copies.start(sum_pair.at[(place.p1 + k) % RING], sum_first.at[k], sum_sems.at[k], place.peer(k, 0))
        sum_first[0] = sum_pair[place.p1]
        yield
        for k in (1, 3, 2):
            copies.received(sum_first.at[k], sum_sems.at[k])
            sum_first[0] += sum_first[k]
        for k in (2, 1, 3):
            copies.start(sum_first.at[0, (place.p2 + k) % RING], sum_second.at[k], sum_sems.at[3 + k], place.peer(0, k))
        sum_second[0] = sum_first[0, place.p2]
        yield
        for k in (1, 3, 2):
            copies.received(sum_second.at[k], sum_sems.at[3 + k])
            sum_second[0] += sum_second[k]
        for quarter in range(RING):
            for side in range(2):
                sum_tiles[2 * quarter + side] = sum_second[0, pl.ds(8 * quarter, 8), pl.ds(TILE * side, TILE)]
        for k in (4, 3, 5, 2, 6, 1, 7):
            copies.start(
                sum_tiles.at[(place.row + k) % rows], sum_rows.at[k], sum_sems.at[6 + k], place.along_row(k, rows)
            )
        sum_rows[0] = sum_tiles[place.row]
        yield
        for k in (1, 7, 2, 6, 3, 5, 4):
            copies.received(sum_rows.at[k], sum_sems.at[6 + k])
            sum_rows[0] += sum_rows[k]
        for k in (4, 3, 5, 2, 6, 1, 7):
            copies.start(
                sum_rows.at[0], sum_tiles.at[rows + place.row], sum_sems.at[13 + k], place.along_row(k, rows)
            )
        sum_tiles[rows + place.row] = sum_rows[0]
        yield
        for k in (1, 7, 2, 6, 3, 5, 4):
            copies.received(sum_tiles.at[rows + (place.row + rows - k) % rows], sum_sems.at[13 + k])
        own = sums_out.at[core, place.p1, place.p2]
        for quarter in range(RING):
            for side in range(2):
                own[pl.ds(8 * quarter, 8), pl.ds(TILE * side, TILE)] = sum_tiles[rows + 2 * quarter + side]
        for k in (2, 1, 3):
            copies.start(own, own, spread_sems.at[k], place.peer(0, k))
        yield
        for k in (1, 3, 2):
            copies.received(sums_out.at[core, place.p1, (place.p2 + RING - k) % RING], spread_sems.at[k])
        line = sums_out.at[core, place.p1]
        for k in (2, 1, 3):
            copies.start(line, line, spread_sems.at[3 + k], place.peer(k, 0))
        yield
        copies.start(line, line, spread_sems.at[7], partner)
        for k in (1, 3, 2):
            there = sums_out.at[core, (place.p1 + RING - k) % RING]
            copies.received(there, spread_sems.at[3 + k])
            copies.start(there, there, spread_sems.at[7 + k], partner)
        yield
        copies.received(sums_out.at[1 - core, place.p2], spread_sems.at[7])
        for k in (1, 3, 2):
            copies.received(sums_out.at[1 - core, (place.p2 + RING - k) % RING], spread_sems.at[7 + k])

    run_in_order(
        {"s": sums_pipe(), "m": mixed_pipe(), "g": grad_pipe()},
        "sgmsgmsgmsgmsgmsgmsgmsgmgg",
    )
    copies.finish()


def reduce_call(grad, mixed, sums, rows, cols):
    anywhere = pl.BlockSpec(memory_space=pl.ANY)
    vmem = pl.BlockSpec(memory_space=pltpu.VMEM)
    ent_dev = grad.shape[0] // cols
    block = (ent_dev, D)
    share = sums.shape[0] // cols
    grad_out, mixed_out, sums_out = pl.pallas_call(
        functools.partial(reduce_kernel, rows),
        out_shape=[
            jax.ShapeDtypeStruct(block, F32),
            jax.ShapeDtypeStruct(block, F32),
            jax.ShapeDtypeStruct((2, RING, RING, share, D), F32),
        ],
        in_specs=[anywhere] * 3,
        out_specs=[vmem] * 3,
        scratch_shapes=[
            pltpu.VMEM((RING, RING) + block, F32),
            pltpu.VMEM((rows,) + block, F32),
            pltpu.VMEM((RING, RING, share, D), F32),
            pltpu.VMEM((RING, RING) + block, F32),
            pltpu.VMEM((2, 2) + block, F32),
            pltpu.VMEM((2, RING) + block, F32),
            pltpu.VMEM((2, HALF, D), F32),
            pltpu.VMEM((2,) + block, F32),
            pltpu.VMEM((rows - 1, HALF, D), F32),
            pltpu.VMEM((rows - 1, HALF, D), F32),
            pltpu.VMEM((RING, RING, share, D), F32),
            pltpu.VMEM((RING, RING, share, D), F32),
            pltpu.VMEM((RING, share, D), F32),
            pltpu.VMEM((rows, 8, TILE), F32),
            pltpu.VMEM((2 * rows, 8, TILE), F32),
            pltpu.SemaphoreType.DMA((96,)),
            pltpu.SemaphoreType.DMA((18,)),
            pltpu.SemaphoreType.DMA((16,)),
            pltpu.SemaphoreType.DMA((12,)),
            pltpu.SemaphoreType.DMA((2 * rows,)),
            pltpu.SemaphoreType.DMA((24,)),
            pltpu.SemaphoreType.DMA((16,)),
        ],
        compiler_params=pltpu.CompilerParams(
            collective_id=1, has_side_effects=True, vmem_limit_bytes=REDUCE_VMEM
        ),
        name="reduce",
    )(
        grad.reshape((cols // 2, 2) + block),
        mixed.reshape((rows,) + block),
        sums.reshape(2, RING, RING, share, D),
    )
    return grad_out, mixed_out, sums_out.reshape(-1, D)


def place_kernel(grad_in, mixed_in, sums_in, mixed_out, grad_out, grad_rel_out, grad_weights_out, rel_ref, sems):
    rels_all = grad_rel_out.shape[0]
    pairs = [(sums_in.at[pl.ds(3 * D, RELS_PAD)], rel_ref), (mixed_in, mixed_out), (grad_in, grad_out)]
    pairs += [(sums_in.at[pl.ds(which * D, D)], grad_weights_out.at[which]) for which in range(3)]
    started = [pltpu.make_async_copy(src, dst, sems.at[index]) for index, (src, dst) in enumerate(pairs)]
    for copy in started:
        copy.start()
    started[0].wait()
    grad_rel_out[...] = rel_ref[pl.ds(0, rels_all), :]
    for copy in started[1:]:
        copy.wait()


def place_call(grad, mixed, sums, rels_all):
    anywhere = pl.BlockSpec(memory_space=pl.ANY)
    return pl.pallas_call(
        place_kernel,
        out_shape=[
            jax.ShapeDtypeStruct(mixed.shape, F32),
            jax.ShapeDtypeStruct(grad.shape, F32),
            jax.ShapeDtypeStruct((rels_all, D), F32),
            jax.ShapeDtypeStruct((3, D, D), F32),
        ],
        in_specs=[anywhere] * 3,
        out_specs=[anywhere, anywhere, pl.BlockSpec(memory_space=pltpu.VMEM), anywhere],
        scratch_shapes=[pltpu.VMEM((RELS_PAD, D), F32), pltpu.SemaphoreType.DMA((6,))],
        compiler_params=pltpu.CompilerParams(vmem_limit_bytes=REDUCE_VMEM),
        name="place",
    )(grad, mixed, sums)


def shards(
    feats,
    rel_embed,
    weights,
    cot,
    tile_row,
    tile_col,
    tile_live,
    edge_ends,
    edge_relation,
    edge_dir,
    edge_count,
):
    rows_n, cols_n = lax.axis_size("row"), lax.axis_size("col")
    sources, targets, *tiles = gather_call(
        tile_live, edge_count, edge_ends, edge_relation, edge_dir, feats, cot, rows_n, cols_n
    )
    grad, mixed, sums = tiles_call(tile_row, tile_col, rel_embed, weights, sources, targets, *tiles)
    grad_feats, mixed, sums = reduce_call(grad, mixed, sums, rows_n, cols_n)
    return place_call(grad_feats, mixed, sums, rel_embed.shape[0])


def solution(mesh):
    return jax.shard_map(
        shards,
        mesh=mesh,
        in_specs=(
            P(("row", "col"), None),
            P(),
            P(),
            P(("col", "row"), None),
            P(("row", "col")),
            P(("row", "col")),
            P(("row", "col")),
            P(("row", "col"), None),
            P(("row", "col"), None),
            P(("row", "col"), None),
            P(("row", "col")),
        ),
        out_specs=(P(("col", "row"), None), P(("row", "col"), None), P(), P()),
        check_vma=False,
    )
```

```python
import functools

import jax
import jax.numpy as jnp
from jax import lax
from jax.experimental import pallas as pl
from jax.experimental.pallas import tpu as pltpu
from jax.sharding import PartitionSpec as P

D = 256
TILE = 128
EDGE_TILE = 256
PAIR = 2 * TILE
RELS_PAD = 256
NONE = 1024
CHUNKS = 4
WIDE = 512
PREPARED = 16
GATHER_VMEM = 60 * 1024 * 1024
TILES_VMEM = 60 * 1024 * 1024
REDUCE_VMEM = 52 * 1024 * 1024
F32 = jnp.float32
BF16 = jnp.bfloat16
NN = (((1,), (0,)), ((), ()))
NT = (((1,), (1,)), ((), ()))
TN = (((0,), (0,)), ((), ()))


def dot(left, right, dims=NN):
    return lax.dot_general(left, right, dims, preferred_element_type=F32)


def split(value):
    high = value.astype(BF16)
    return high, (value - high.astype(F32)).astype(BF16)


def dot_exact_left(left, right, dims=NN):
    high, low = right
    return dot(left, high, dims) + dot(left, low, dims)


def dot_exact_right(left, right, dims=NN):
    high, low = left
    return dot(high, right, dims) + dot(low, right, dims)


def dot_split(left, right, dims=NN):
    return dot(left[0], right[0], dims) + (dot(left[0], right[1], dims) + dot(left[1], right[0], dims))


def rows_at(index, size):
    return pl.ds(pl.multiple_of(index * size, size), size)


def hot(iota, entries):
    return jnp.where(iota == entries, 1.0, 0.0).astype(BF16)


def tiles_kernel(
    row_ref,
    col_ref,
    rel_ref,
    weights_ref,
    feats_any,
    cot_any,
    forward_any,
    backward_any,
    counted_any,
    grad_any,
    mixed_ref,
    sums_ref,
    forward_ref,
    backward_ref,
    counted_ref,
    feats_ref,
    cot_ref,
    turned_ref,
    rel_pad_ref,
    totals_ref,
    counts_ref,
    high_ref,
    low_ref,
    count_high_ref,
    grad_ref,
    self_rel_ref,
    self_sum_ref,
    sems,
):
    slots = forward_ref.shape[0]
    dst_dev, src_dev = cot_ref.shape[0], feats_ref.shape[0]
    blocks, source_blocks = dst_dev // TILE, src_dev // TILE
    rels_all = rel_ref.shape[0]
    col_index = row_ref[0] // blocks
    row_index = col_ref[0] // source_blocks
    ahead = col_index * blocks - row_index * source_blocks
    owner = (ahead >= 0) & (ahead < source_blocks)
    load_cot = pltpu.make_async_copy(cot_any, cot_ref, sems.at[0])
    load_feats = pltpu.make_async_copy(feats_any, feats_ref, sems.at[1])
    load_cot.start()
    load_feats.start()

    chunk = slots // CHUNKS
    loads = []
    for part in range(CHUNKS):
        here = pl.ds(part * chunk, chunk)
        for which, (src, dst) in enumerate(
            ((forward_any, forward_ref), (backward_any, backward_ref), (counted_any, counted_ref))
        ):
            copy = pltpu.make_async_copy(src.at[here], dst.at[here], sems.at[6 + 3 * part + which])
            copy.start()
            loads.append(copy)
    rel_pad_ref[...] = jnp.zeros_like(rel_pad_ref)
    rel_pad_ref[pl.ds(0, rels_all), :] = rel_ref[...]
    weight = [split(weights_ref[which]) for which in range(3)]

    def clear_block(block, _):
        grad_ref[rows_at(block, PAIR), :] = jnp.zeros((PAIR, D), F32)
        return 0

    lax.fori_loop(0, src_dev // PAIR, clear_block, 0)
    sums_ref[pl.ds(2 * D, D), :] = jnp.zeros((D, D), F32)
    self_rel_ref[...] = jnp.zeros_like(self_rel_ref)
    load_cot.wait()

    def image_block(block, _):
        here = rows_at(block, WIDE)
        cot = cot_ref[here, :]
        turned_ref[:, here] = cot.T
        for which in range(2):
            high, low = split(dot_exact_left(cot, weight[which], NT))
            for sub in range(WIDE // TILE):
                first = (block * (WIDE // TILE) + sub) * PAIR + which * TILE
                part = pl.ds(pl.multiple_of(first, TILE), TILE)
                high_ref[part, :] = high[sub * TILE : (sub + 1) * TILE]
                low_ref[part, :] = low[sub * TILE : (sub + 1) * TILE]
        totals_ref[rows_at(block, 2 * WIDE), :] = jnp.zeros((2 * WIDE, D), F32)
        counts_ref[rows_at(block, 2 * WIDE), :] = jnp.zeros((2 * WIDE, RELS_PAD), F32)
        mixed_ref[here, :] = jnp.zeros((WIDE, D), F32)
        return 0

    lax.fori_loop(0, dst_dev // WIDE, image_block, 0, unroll=True)

    @pl.when(owner)
    def _():
        def self_image(block, total):
            cot = cot_ref[rows_at(block, WIDE), :]
            grad_ref[pl.ds(pl.multiple_of(ahead * TILE + block * WIDE, TILE), WIDE), :] = dot_exact_left(
                cot, weight[2], NT
            )
            return total + jnp.sum(cot.astype(F32).reshape(WIDE // 8, 8, D), axis=0)

        self_sum_ref[...] = lax.fori_loop(0, dst_dev // WIDE, self_image, jnp.zeros((8, D), F32), unroll=True)

    load_feats.wait()

    @pl.when(owner)
    def _():
        own_rel = split(jnp.broadcast_to(rel_ref[pl.ds(rels_all - 1, 1), :], (8, D)))
        rel_image = dot_split(own_rel, weight[2])[:1]

        def self_block(block, _):
            there = pl.ds(pl.multiple_of(ahead * TILE + block * WIDE, TILE), WIDE)
            mixed_ref[rows_at(block, WIDE), :] = dot_exact_left(feats_ref[there, :], weight[2]) - rel_image
            return 0

        lax.fori_loop(0, dst_dev // WIDE, self_block, 0, unroll=True)
        there = pl.ds(pl.multiple_of(ahead * TILE, TILE), dst_dev)
        own_sum = split(self_sum_ref[...])
        sums_ref[pl.ds(2 * D, D), :] = dot(turned_ref[...], feats_ref[there, :]).T - dot_split(own_rel, own_sum, TN)
        self_rel_ref[...] = dot_split(own_sum, weight[2], NT)

    def tile(slot, _):
        row = rows_at(row_ref[slot] % blocks, PAIR)
        col = rows_at(col_ref[slot] % source_blocks, TILE)
        backward = backward_ref[slot]
        totals_ref[row, :] += dot(forward_ref[slot], feats_ref[col, :])
        counts_ref[row, :] += counted_ref[slot].astype(F32)
        grad_ref[col, :] += dot(backward, high_ref[row, :]) + dot(backward, low_ref[row, :])
        return 0

    for part in range(CHUNKS):
        for copy in loads[3 * part : 3 * part + 3]:
            copy.wait()
        lax.fori_loop(part * chunk, (part + 1) * chunk, tile, 0, unroll=True)

    stores = []
    for part in range(4):
        here = pl.ds(part * (src_dev // 4), src_dev // 4)
        copy = pltpu.make_async_copy(grad_ref.at[here, :], grad_any.at[here, :], sems.at[2 + part])
        copy.start()
        stores.append(copy)

    relations = split(rel_pad_ref[...])

    def most(block, value):
        counts = counts_ref[rows_at(block, PAIR), :]
        return jnp.maximum(value, jnp.max(counts.reshape(PAIR // 8, 8, RELS_PAD), axis=0))

    largest = jnp.max(lax.fori_loop(0, blocks, most, jnp.zeros((8, RELS_PAD), F32)))
    large = largest > 256.0

    @pl.when(large)
    def _():
        def low_block(block, _):
            at = rows_at(block, PAIR)
            low = split(counts_ref[at, :])[1]
            totals_ref[at, :] -= dot(low, relations[0]) + dot(low, relations[1])
            return 0

        lax.fori_loop(0, blocks, low_block, 0)

    def relate_block(block, _):
        at = rows_at(block, WIDE)
        counts = counts_ref[at, :].astype(BF16)
        totals = totals_ref[at, :] - (dot(counts, relations[0]) + dot(counts, relations[1]))
        high, low = split(totals)
        for sub in range(WIDE // PAIR):
            here = rows_at(block * (WIDE // PAIR) + sub, TILE)
            for which in range(2):
                first = sub * PAIR + which * TILE
                there = pl.ds(
                    pl.multiple_of(which * dst_dev + (block * (WIDE // PAIR) + sub) * TILE, TILE), TILE
                )
                high_ref[there, :] = high[first : first + TILE]
                low_ref[there, :] = low[first : first + TILE]
                count_high_ref[which, here, :] = counts[first : first + TILE]
        return 0

    lax.fori_loop(0, 2 * dst_dev // WIDE, relate_block, 0, unroll=True)

    def mix_block(block, _):
        here = rows_at(block, WIDE)
        parts = []
        for which in range(2):
            there = pl.ds(pl.multiple_of(which * dst_dev + block * WIDE, WIDE), WIDE)
            parts.append(dot_split((high_ref[there, :], low_ref[there, :]), weight[which]))
        mixed_ref[here, :] += parts[0] + parts[1]
        return 0

    lax.fori_loop(0, dst_dev // WIDE, mix_block, 0, unroll=True)

    turned = turned_ref[...]
    grad_rel = jnp.zeros((D, RELS_PAD), F32)
    met = [dot(turned, count_high_ref[which]) for which in range(2)]
    for which in range(2):
        there = pl.ds(which * dst_dev, dst_dev)
        product = dot(turned, high_ref[there, :]) + dot(turned, low_ref[there, :])
        sums_ref[pl.ds(which * D, D), :] = product.T
        grad_rel -= dot_split(weight[which], split(met[which]))
    sums_ref[pl.ds(3 * D, RELS_PAD), :] = grad_rel.T

    @pl.when(large)
    def _():
        def low_block(block, _):
            cot = cot_ref[rows_at(block, TILE), :]
            counts = counts_ref[rows_at(block, PAIR), :]
            for which in range(2):
                low = split(counts[which * TILE : (which + 1) * TILE])[1]
                part = split(dot(low, cot, TN))
                sums_ref[pl.ds(3 * D, RELS_PAD), :] -= dot_split(part, weight[which], NT)
            return 0

        lax.fori_loop(0, blocks, low_block, 0)

    sums_ref[pl.ds(3 * D + rels_all - 1, 1), :] -= jnp.sum(self_rel_ref[...], axis=0, keepdims=True)

    for copy in stores:
        copy.wait()


def tiles_call(rows, cols, rel, weights, sources, cot, forward, backward, counted):
    dst_dev, src_dev = cot.shape[0], sources.shape[0]
    smem = pl.BlockSpec(memory_space=pltpu.SMEM)
    vmem = pl.BlockSpec(memory_space=pltpu.VMEM)
    anywhere = pl.BlockSpec(memory_space=pl.ANY)
    return pl.pallas_call(
        tiles_kernel,
        out_shape=[
            jax.ShapeDtypeStruct((src_dev, D), F32),
            jax.ShapeDtypeStruct((dst_dev, D), F32),
            jax.ShapeDtypeStruct((3 * D + RELS_PAD, D), F32),
        ],
        in_specs=[smem] * 2 + [vmem] * 2 + [anywhere] * 5,
        out_specs=[anywhere, vmem, vmem],
        scratch_shapes=[
            pltpu.VMEM(forward.shape, BF16),
            pltpu.VMEM(backward.shape, BF16),
            pltpu.VMEM(counted.shape, BF16),
            pltpu.VMEM((src_dev, D), BF16),
            pltpu.VMEM((dst_dev, D), BF16),
            pltpu.VMEM((D, dst_dev), BF16),
            pltpu.VMEM((RELS_PAD, D), F32),
            pltpu.VMEM((2 * dst_dev, D), F32),
            pltpu.VMEM((2 * dst_dev, RELS_PAD), F32),
            pltpu.VMEM((2 * dst_dev, D), BF16),
            pltpu.VMEM((2 * dst_dev, D), BF16),
            pltpu.VMEM((2, dst_dev, RELS_PAD), BF16),
            pltpu.VMEM((src_dev, D), F32),
            pltpu.VMEM((8, D), F32),
            pltpu.VMEM((8, D), F32),
            pltpu.SemaphoreType.DMA((6 + 3 * CHUNKS,)),
        ],
        compiler_params=pltpu.CompilerParams(vmem_limit_bytes=TILES_VMEM),
        name="tiles",
    )(rows, cols, rel, weights, sources, cot, forward, backward, counted)


MESH = pl.DeviceIdType.MESH
RING = 4
HALF = TILE


class Copies:
    def __init__(self, send_sems):
        self.send_sems, self.started = send_sems, []

    def start(self, src, dst, recv, peer):
        copy = pltpu.make_async_remote_copy(
            src_ref=src,
            dst_ref=dst,
            send_sem=self.send_sems.at[len(self.started)],
            recv_sem=recv,
            device_id=peer,
            device_id_type=MESH,
        )
        copy.start()
        self.started.append(copy)

    def received(self, dst, recv):
        pltpu.make_async_remote_copy(
            src_ref=dst,
            dst_ref=dst,
            send_sem=self.send_sems.at[0],
            recv_sem=recv,
            device_id=self.any_peer,
            device_id_type=MESH,
        ).wait_recv()

    def finish(self):
        for copy in self.started:
            copy.wait_send()


class Place:
    def __init__(self):
        self.row = lax.axis_index("row")
        self.col = lax.axis_index("col")
        self.core = self.col % 2
        self.stride1 = 8 - 6 * self.core
        self.stride2 = 10 - self.stride1
        self.p1 = self.col // self.stride1 % RING
        self.p2 = self.col // self.stride2 % RING

    def col_at(self, k1, k2):
        return (self.p1 + k1) % RING * self.stride1 + (self.p2 + k2) % RING * self.stride2 + self.core

    def peer(self, k1, k2):
        return (self.row, self.col_at(k1, k2))

    def partner(self):
        return (self.row, self.col + 1 - 2 * self.core)

    def along_row(self, k, rows):
        return ((self.row + k) % rows, self.col)

    def greet(self, peers):
        barrier = pltpu.get_barrier_semaphore()
        for peer in peers:
            pl.semaphore_signal(barrier, inc=1, device_id=peer, device_id_type=MESH)
        pl.semaphore_wait(barrier, len(peers))


def run_in_order(pipes, order):
    for name in order:
        next(pipes[name], None)
    for pipe in pipes.values():
        for _ in pipe:
            pass


def gather_kernel(
    rows,
    live_ref,
    count_ref,
    ends_ref,
    relation_ref,
    dir_ref,
    feats_ref,
    cot_ref,
    sources_ref,
    targets_ref,
    forward_any,
    backward_any,
    counted_any,
    forward_ref,
    backward_ref,
    counted_ref,
    send_sems,
    shard_sems,
    row_sems,
    own_sems,
    tile_sems,
):
    place = Place()
    copies = Copies(send_sems)
    copies.any_peer = place.partner()
    own_copies = [
        pltpu.make_async_copy(feats_ref, sources_ref.at[place.col], own_sems.at[0]),
        pltpu.make_async_copy(cot_ref, targets_ref.at[place.row], own_sems.at[1]),
    ]
    for copy in own_copies:
        copy.start()
    place.greet(
        [place.partner()]
        + [place.peer(k, 0) for k in (1, 3)]
        + [place.peer(0, k) for k in (1, 3)]
        + [place.along_row(k, rows) for k in (1, rows - 1)]
    )
    parts = [pl.ds(0, HALF), pl.ds(HALF, HALF)]

    def send(array, sems, count, index, peer, half=None, src=None):
        here = array.at[index] if half is None else array.at[index, parts[half]]
        sem = sems.at[2 * count + index] if half is None else sems.at[2 * index + half]
        copies.start(here if src is None else src, here, sem, peer)

    def got(array, sems, count, index, halves=False):
        if halves:
            for half in range(2):
                copies.received(array.at[index, parts[half]], sems.at[2 * index + half])
        else:
            copies.received(array.at[index], sems.at[2 * count + index])

    send_shard = functools.partial(send, sources_ref, shard_sems, 2 * RING * RING)
    got_shard = functools.partial(got, sources_ref, shard_sems, 2 * RING * RING)
    send_row = functools.partial(send, targets_ref, row_sems, rows)
    got_row = functools.partial(got, targets_ref, row_sems, rows)

    def feats_pipe():
        for peer in (place.peer(1, 0), place.peer(3, 0), place.peer(0, 1), place.peer(0, 3), place.partner()):
            send_shard(place.col, peer, src=feats_ref)
        yield

        def spread(b):
            for peer in (place.peer(0, 1), place.peer(0, 3), place.partner()):
                send_shard(b, peer)

        left, right, far = place.col_at(3, 0), place.col_at(1, 0), place.col_at(2, 0)
        got_shard(left)
        send_shard(left, place.peer(1, 0), 0)
        spread(left)
        got_shard(right)
        send_shard(right, place.peer(3, 0), 1)
        spread(right)
        yield

        def second(k1):
            below, above = place.col_at(k1, 3), place.col_at(k1, 1)
            got_shard(below)
            send_shard(below, place.peer(0, 1), 0)
            got_shard(above)
            send_shard(above, place.peer(0, 3), 1)
            send_shard(below, place.partner())
            send_shard(above, place.partner())

        second(0)
        yield
        got_shard(far, halves=True)
        spread(far)
        yield
        second(3)
        yield
        second(1)
        yield
        second(2)
        yield
        for k1 in (0, 3, 1, 2):
            b = place.col_at(k1, 2)
            got_shard(b, halves=True)
            send_shard(b, place.partner())
        yield
        for k1 in range(RING):
            for k2 in range(RING):
                got_shard(place.col_at(k1, k2) + 1 - 2 * place.core)

    def cot_pipe():
        after, before = place.along_row(1, rows), place.along_row(rows - 1, rows)
        send_row(place.row, after, src=cot_ref)
        send_row(place.row, before, src=cot_ref)
        yield
        for k in range(1, rows // 2):
            last = k == rows // 2 - 1
            low, high = (place.row + rows - k) % rows, (place.row + k) % rows
            got_row(low)
            send_row(low, after, 0 if last else None)
            got_row(high)
            send_row(high, before, 1 if last else None)
            yield
        got_row((place.row + rows // 2) % rows, halves=True)

    pair_iota = lax.broadcasted_iota(jnp.int32, (PAIR, EDGE_TILE), 0)
    tile_iota = lax.broadcasted_iota(jnp.int32, (TILE, EDGE_TILE), 0)
    edge_iota = lax.broadcasted_iota(jnp.int32, (1, EDGE_TILE), 1)
    tile_copies = []

    def tile(slot, _):
        at = pl.ds(slot, 1)
        edges = jnp.where(slot < live_ref[0], count_ref[slot], 0)
        ends = ends_ref[at, :]
        key = dir_ref[at, :] * TILE + lax.shift_right_logical(ends, 7)
        hot_dst = hot(pair_iota, jnp.where(edge_iota < edges, key, NONE))
        hot_src = hot(tile_iota, ends & (TILE - 1))
        hot_rel = hot(pair_iota, relation_ref[at, :])
        forward_ref[slot] = dot(hot_dst, hot_src, NT).astype(BF16)
        backward_ref[slot] = dot(hot_src, hot_dst, NT).astype(BF16)
        counted_ref[slot] = dot(hot_dst, hot_rel, NT).astype(BF16)
        return 0

    def tiles_pipe():
        chunk = ends_ref.shape[0] // PREPARED
        for part in range(PREPARED):
            lax.fori_loop(part * chunk, (part + 1) * chunk, tile, 0, unroll=2)
            here = pl.ds(part * chunk, chunk)
            for which, (src, dst) in enumerate(
                ((forward_ref, forward_any), (backward_ref, backward_any), (counted_ref, counted_any))
            ):
                copy = pltpu.make_async_copy(src.at[here], dst.at[here], tile_sems.at[3 * part + which])
                copy.start()
                tile_copies.append(copy)
            yield

    run_in_order({"f": feats_pipe(), "c": cot_pipe(), "p": tiles_pipe()}, "fcppppfpfcpfppcfppfpcfpppfppcff")
    for copy in tile_copies:
        copy.wait()
    for copy in own_copies:
        copy.wait()
    copies.finish()


def gather_call(live, counts, ends, relation, direction, feats, cot, rows, cols):
    anywhere = pl.BlockSpec(memory_space=pl.ANY)
    smem = pl.BlockSpec(memory_space=pltpu.SMEM)
    vmem = pl.BlockSpec(memory_space=pltpu.VMEM)
    slots = ends.shape[0]
    shapes = [(slots, PAIR, TILE), (slots, TILE, PAIR), (slots, PAIR, RELS_PAD)]
    sources, targets, *tiles = pl.pallas_call(
        functools.partial(gather_kernel, rows),
        out_shape=[
            jax.ShapeDtypeStruct((cols,) + feats.shape, feats.dtype),
            jax.ShapeDtypeStruct((rows,) + cot.shape, cot.dtype),
        ]
        + [jax.ShapeDtypeStruct(shape, BF16) for shape in shapes],
        in_specs=[smem] * 2 + [vmem] * 3 + [anywhere] * 2,
        out_specs=[anywhere] * 5,
        scratch_shapes=[pltpu.VMEM(shape, BF16) for shape in shapes]
        + [
            pltpu.SemaphoreType.DMA((64,)),
            pltpu.SemaphoreType.DMA((3 * cols,)),
            pltpu.SemaphoreType.DMA((3 * rows,)),
            pltpu.SemaphoreType.DMA((2,)),
            pltpu.SemaphoreType.DMA((3 * PREPARED,)),
        ],
        compiler_params=pltpu.CompilerParams(
            collective_id=0, has_side_effects=True, vmem_limit_bytes=GATHER_VMEM
        ),
        name="gather",
    )(live, counts, ends, relation, direction, feats, cot)
    return [sources.reshape(-1, D), targets.reshape(-1, D)] + tiles


def reduce_kernel(
    rows,
    grad_any,
    mixed_any,
    sums_any,
    grad_out,
    mixed_out,
    sums_out,
    grad_acc,
    mixed_in,
    sums_in,
    pair_in,
    relay1,
    ring1,
    relay2,
    ring2,
    row_up,
    row_down,
    sum_pair,
    sum_first,
    sum_second,
    sum_rows,
    sum_tiles,
    send_sems,
    own_sems,
    pair_sems,
    ring_sems,
    row_sems,
    sum_sems,
    spread_sems,
):
    place = Place()
    copies = Copies(send_sems)
    copies.any_peer = place.partner()
    partner = place.partner()
    core = place.core
    order1 = (2, 1, 3, 0)
    load_sums = pltpu.make_async_copy(sums_any.at[core], sums_in, own_sems.at[16])
    load_mixed = pltpu.make_async_copy(mixed_any, mixed_in, own_sems.at[17])
    load_sums.start()
    load_mixed.start()
    own_copies = {}
    for k in order1:
        for r in (2, 1, 3, 0):
            block = place.col_at(k, r) // 2
            copy = pltpu.make_async_copy(grad_any.at[block, core], grad_acc.at[k, r], own_sems.at[4 * k + r])
            copy.start()
            own_copies[k, r] = copy
    place.greet(
        [partner]
        + [place.peer(k1, k2) for k1 in range(RING) for k2 in range(RING) if k1 or k2]
        + [place.along_row(k, rows) for k in range(1, rows)]
    )
    low, high = pl.ds(0, HALF), pl.ds(HALF, HALF)

    def grad_pipe():
        for k in order1:
            for r in (2, 1, 3, 0):
                block = ((place.p2 + k) % RING * place.stride2 + (place.p1 + r) % RING * place.stride1) // 2
                copies.start(grad_any.at[block, 1 - core], pair_in.at[k, r], pair_sems.at[4 * k + r], partner)
        yield

        def pair_sum(k, r):
            own_copies[k, r].wait()
            copies.received(pair_in.at[k, r], pair_sems.at[4 * k + r])
            grad_acc[k, r] += pair_in[k, r]

        right, left = place.peer(1, 0), place.peer(3, 0)
        for r in range(RING):
            pair_sum(2, r)
        copies.start(grad_acc.at[2, pl.ds(0, 2)], relay1.at[0], ring_sems.at[0], right)
        copies.start(grad_acc.at[2, pl.ds(2, 2)], relay1.at[1], ring_sems.at[1], left)
        yield
        for r in (2, 3):
            pair_sum(1, r)
        copies.start(grad_acc.at[1, pl.ds(2, 2)], ring1.at[0, pl.ds(2, 2)], ring_sems.at[3], right)
        for r in (0, 1):
            pair_sum(3, r)
        copies.start(grad_acc.at[3, pl.ds(0, 2)], ring1.at[1, pl.ds(0, 2)], ring_sems.at[4], left)
        yield
        for r in (0, 1):
            pair_sum(1, r)
        for r in (2, 3):
            pair_sum(3, r)
        for r in range(RING):
            pair_sum(0, r)
        yield
        copies.received(relay1.at[0], ring_sems.at[0])
        for r in (0, 1):
            grad_acc[1, r] += relay1[0, r]
        copies.start(grad_acc.at[1, pl.ds(0, 2)], ring1.at[0, pl.ds(0, 2)], ring_sems.at[2], right)
        copies.received(relay1.at[1], ring_sems.at[1])
        for r in (0, 1):
            grad_acc[3, 2 + r] += relay1[1, r]
        copies.start(grad_acc.at[3, pl.ds(2, 2)], ring1.at[1, pl.ds(2, 2)], ring_sems.at[5], left)
        yield
        copies.received(ring1.at[0, pl.ds(2, 2)], ring_sems.at[3])
        copies.received(ring1.at[1, pl.ds(0, 2)], ring_sems.at[4])
        for r in (2, 3):
            grad_acc[0, r] += ring1[0, r]
        for r in (0, 1):
            grad_acc[0, r] += ring1[1, r]
        yield
        up, down = place.peer(0, 1), place.peer(0, 3)
        copies.received(ring1.at[1, pl.ds(2, 2)], ring_sems.at[5])
        grad_acc[0, 2] += ring1[1, 2]
        copies.start(grad_acc.at[0, 2, low], relay2.at[0], ring_sems.at[6], up)
        copies.start(grad_acc.at[0, 2, high], relay2.at[1], ring_sems.at[7], down)
        grad_acc[0, 3] += ring1[1, 3]
        copies.start(grad_acc.at[0, 3, low], ring2.at[1, low], ring_sems.at[10], down)
        copies.received(ring1.at[0, pl.ds(0, 2)], ring_sems.at[2])
        grad_acc[0, 1] += ring1[0, 1]
        copies.start(grad_acc.at[0, 1, high], ring2.at[0, high], ring_sems.at[9], up)
        grad_acc[0, 0] += ring1[0, 0]
        yield
        copies.received(relay2.at[0], ring_sems.at[6])
        grad_acc[0, 1, low] += relay2[0]
        copies.start(grad_acc.at[0, 1, low], ring2.at[0, low], ring_sems.at[8], up)
        copies.received(relay2.at[1], ring_sems.at[7])
        grad_acc[0, 3, high] += relay2[1]
        copies.start(grad_acc.at[0, 3, high], ring2.at[1, high], ring_sems.at[11], down)
        yield
        copies.received(ring2.at[0, high], ring_sems.at[9])
        copies.received(ring2.at[1, low], ring_sems.at[10])
        copies.received(ring2.at[0, low], ring_sems.at[8])
        copies.received(ring2.at[1, high], ring_sems.at[11])
        grad_out[...] = grad_acc[0, 0] + ring2[0] + ring2[1]

    def mixed_pipe():
        after, before = place.along_row(1, rows), place.along_row(rows - 1, rows)
        copies.start(mixed_any.at[(place.row + rows - 1) % rows, low], row_up.at[0], row_sems.at[0], after)
        copies.start(mixed_any.at[(place.row + 1) % rows, high], row_down.at[0], row_sems.at[rows], before)
        yield
        load_mixed.wait()
        for step in range(1, rows):
            copies.received(row_up.at[step - 1], row_sems.at[step - 1])
            row_up[step - 1] += mixed_in[(place.row + 2 * rows - 1 - step) % rows, low]
            if step < rows - 1:
                copies.start(row_up.at[step - 1], row_up.at[step], row_sems.at[step], after)
            copies.received(row_down.at[step - 1], row_sems.at[rows + step - 1])
            row_down[step - 1] += mixed_in[(place.row + 1 + step) % rows, high]
            if step < rows - 1:
                copies.start(row_down.at[step - 1], row_down.at[step], row_sems.at[rows + step], before)
            yield
        mixed_out[low] = row_up[rows - 2]
        mixed_out[high] = row_down[rows - 2]

    def sums_pipe():
        copies.start(sums_any.at[1 - core], sum_pair, sum_sems.at[0], partner)
        yield
        load_sums.wait()
        copies.received(sum_pair, sum_sems.at[0])
        for q in range(RING):
            sum_pair[q] += sums_in[q]
        for k in (2, 1, 3):
            copies.start(sum_pair.at[(place.p1 + k) % RING], sum_first.at[k], sum_sems.at[k], place.peer(k, 0))
        sum_first[0] = sum_pair[place.p1]
        yield
        for k in (1, 3, 2):
            copies.received(sum_first.at[k], sum_sems.at[k])
            sum_first[0] += sum_first[k]
        for k in (2, 1, 3):
            copies.start(sum_first.at[0, (place.p2 + k) % RING], sum_second.at[k], sum_sems.at[3 + k], place.peer(0, k))
        sum_second[0] = sum_first[0, place.p2]
        yield
        for k in (1, 3, 2):
            copies.received(sum_second.at[k], sum_sems.at[3 + k])
            sum_second[0] += sum_second[k]
        for quarter in range(RING):
            for side in range(2):
                sum_tiles[2 * quarter + side] = sum_second[0, pl.ds(8 * quarter, 8), pl.ds(TILE * side, TILE)]
        for k in (4, 3, 5, 2, 6, 1, 7):
            copies.start(
                sum_tiles.at[(place.row + k) % rows], sum_rows.at[k], sum_sems.at[6 + k], place.along_row(k, rows)
            )
        sum_rows[0] = sum_tiles[place.row]
        yield
        for k in (1, 7, 2, 6, 3, 5, 4):
            copies.received(sum_rows.at[k], sum_sems.at[6 + k])
            sum_rows[0] += sum_rows[k]
        for k in (4, 3, 5, 2, 6, 1, 7):
            copies.start(
                sum_rows.at[0], sum_tiles.at[rows + place.row], sum_sems.at[13 + k], place.along_row(k, rows)
            )
        sum_tiles[rows + place.row] = sum_rows[0]
        yield
        for k in (1, 7, 2, 6, 3, 5, 4):
            copies.received(sum_tiles.at[rows + (place.row + rows - k) % rows], sum_sems.at[13 + k])
        own = sums_out.at[core, place.p1, place.p2]
        for quarter in range(RING):
            for side in range(2):
                own[pl.ds(8 * quarter, 8), pl.ds(TILE * side, TILE)] = sum_tiles[rows + 2 * quarter + side]
        for k in (2, 1, 3):
            copies.start(own, own, spread_sems.at[k], place.peer(0, k))
        yield
        for k in (1, 3, 2):
            copies.received(sums_out.at[core, place.p1, (place.p2 + RING - k) % RING], spread_sems.at[k])
        line = sums_out.at[core, place.p1]
        for k in (2, 1, 3):
            copies.start(line, line, spread_sems.at[3 + k], place.peer(k, 0))
        yield
        copies.start(line, line, spread_sems.at[7], partner)
        for k in (1, 3, 2):
            there = sums_out.at[core, (place.p1 + RING - k) % RING]
            copies.received(there, spread_sems.at[3 + k])
            copies.start(there, there, spread_sems.at[7 + k], partner)
        yield
        copies.received(sums_out.at[1 - core, place.p2], spread_sems.at[7])
        for k in (1, 3, 2):
            copies.received(sums_out.at[1 - core, (place.p2 + RING - k) % RING], spread_sems.at[7 + k])

    run_in_order(
        {"s": sums_pipe(), "m": mixed_pipe(), "g": grad_pipe()},
        "sgmsgmsgmsgmsgmsgmsgmsgmgg",
    )
    copies.finish()


def reduce_call(grad, mixed, sums, rows, cols):
    anywhere = pl.BlockSpec(memory_space=pl.ANY)
    vmem = pl.BlockSpec(memory_space=pltpu.VMEM)
    ent_dev = grad.shape[0] // cols
    block = (ent_dev, D)
    share = sums.shape[0] // cols
    grad_out, mixed_out, sums_out = pl.pallas_call(
        functools.partial(reduce_kernel, rows),
        out_shape=[
            jax.ShapeDtypeStruct(block, F32),
            jax.ShapeDtypeStruct(block, F32),
            jax.ShapeDtypeStruct((2, RING, RING, share, D), F32),
        ],
        in_specs=[anywhere] * 3,
        out_specs=[vmem] * 3,
        scratch_shapes=[
            pltpu.VMEM((RING, RING) + block, F32),
            pltpu.VMEM((rows,) + block, F32),
            pltpu.VMEM((RING, RING, share, D), F32),
            pltpu.VMEM((RING, RING) + block, F32),
            pltpu.VMEM((2, 2) + block, F32),
            pltpu.VMEM((2, RING) + block, F32),
            pltpu.VMEM((2, HALF, D), F32),
            pltpu.VMEM((2,) + block, F32),
            pltpu.VMEM((rows - 1, HALF, D), F32),
            pltpu.VMEM((rows - 1, HALF, D), F32),
            pltpu.VMEM((RING, RING, share, D), F32),
            pltpu.VMEM((RING, RING, share, D), F32),
            pltpu.VMEM((RING, share, D), F32),
            pltpu.VMEM((rows, 8, TILE), F32),
            pltpu.VMEM((2 * rows, 8, TILE), F32),
            pltpu.SemaphoreType.DMA((96,)),
            pltpu.SemaphoreType.DMA((18,)),
            pltpu.SemaphoreType.DMA((16,)),
            pltpu.SemaphoreType.DMA((12,)),
            pltpu.SemaphoreType.DMA((2 * rows,)),
            pltpu.SemaphoreType.DMA((24,)),
            pltpu.SemaphoreType.DMA((16,)),
        ],
        compiler_params=pltpu.CompilerParams(
            collective_id=1, has_side_effects=True, vmem_limit_bytes=REDUCE_VMEM
        ),
        name="reduce",
    )(
        grad.reshape((cols // 2, 2) + block),
        mixed.reshape((rows,) + block),
        sums.reshape(2, RING, RING, share, D),
    )
    return grad_out, mixed_out, sums_out.reshape(-1, D)


def place_kernel(grad_in, mixed_in, sums_in, mixed_out, grad_out, grad_rel_out, grad_weights_out, rel_ref, sems):
    rels_all = grad_rel_out.shape[0]
    pairs = [(sums_in.at[pl.ds(3 * D, RELS_PAD)], rel_ref), (mixed_in, mixed_out), (grad_in, grad_out)]
    pairs += [(sums_in.at[pl.ds(which * D, D)], grad_weights_out.at[which]) for which in range(3)]
    started = [pltpu.make_async_copy(src, dst, sems.at[index]) for index, (src, dst) in enumerate(pairs)]
    for copy in started:
        copy.start()
    started[0].wait()
    grad_rel_out[...] = rel_ref[pl.ds(0, rels_all), :]
    for copy in started[1:]:
        copy.wait()


def place_call(grad, mixed, sums, rels_all):
    anywhere = pl.BlockSpec(memory_space=pl.ANY)
    return pl.pallas_call(
        place_kernel,
        out_shape=[
            jax.ShapeDtypeStruct(mixed.shape, F32),
            jax.ShapeDtypeStruct(grad.shape, F32),
            jax.ShapeDtypeStruct((rels_all, D), F32),
            jax.ShapeDtypeStruct((3, D, D), F32),
        ],
        in_specs=[anywhere] * 3,
        out_specs=[anywhere, anywhere, pl.BlockSpec(memory_space=pltpu.VMEM), anywhere],
        scratch_shapes=[pltpu.VMEM((RELS_PAD, D), F32), pltpu.SemaphoreType.DMA((6,))],
        compiler_params=pltpu.CompilerParams(vmem_limit_bytes=REDUCE_VMEM),
        name="place",
    )(grad, mixed, sums)


def shards(
    feats,
    rel_embed,
    weights,
    cot,
    tile_row,
    tile_col,
    tile_live,
    edge_ends,
    edge_relation,
    edge_dir,
    edge_count,
):
    rows_n, cols_n = lax.axis_size("row"), lax.axis_size("col")
    sources, targets, *tiles = gather_call(
        tile_live, edge_count, edge_ends, edge_relation, edge_dir, feats, cot, rows_n, cols_n
    )
    grad, mixed, sums = tiles_call(tile_row, tile_col, rel_embed, weights, sources, targets, *tiles)
    grad_feats, mixed, sums = reduce_call(grad, mixed, sums, rows_n, cols_n)
    return place_call(grad_feats, mixed, sums, rel_embed.shape[0])


def solution(mesh):
    return jax.shard_map(
        shards,
        mesh=mesh,
        in_specs=(
            P(("row", "col"), None),
            P(),
            P(),
            P(("col", "row"), None),
            P(("row", "col")),
            P(("row", "col")),
            P(("row", "col")),
            P(("row", "col"), None),
            P(("row", "col"), None),
            P(("row", "col"), None),
            P(("row", "col")),
        ),
        out_specs=(P(("col", "row"), None), P(("row", "col"), None), P(), P()),
        check_vma=False,
    )
```

```python
import functools

import jax
import jax.numpy as jnp
from jax import lax
from jax.experimental import pallas as pl
from jax.experimental.pallas import tpu as pltpu
from jax.sharding import PartitionSpec as P

D = 256
TILE = 128
EDGE_TILE = 256
PAIR = 2 * TILE
RELS_PAD = 256
NONE = 1024
CHUNKS = 4
WIDE = 512
PREPARED = 16
GATHER_VMEM = 60 * 1024 * 1024
TILES_VMEM = 60 * 1024 * 1024
REDUCE_VMEM = 52 * 1024 * 1024
F32 = jnp.float32
BF16 = jnp.bfloat16
NN = (((1,), (0,)), ((), ()))
NT = (((1,), (1,)), ((), ()))
TN = (((0,), (0,)), ((), ()))


def dot(left, right, dims=NN):
    return lax.dot_general(left, right, dims, preferred_element_type=F32)


def split(value):
    high = value.astype(BF16)
    return high, (value - high.astype(F32)).astype(BF16)


def dot_exact_left(left, right, dims=NN):
    high, low = right
    return dot(left, high, dims) + dot(left, low, dims)


def dot_exact_right(left, right, dims=NN):
    high, low = left
    return dot(high, right, dims) + dot(low, right, dims)


def dot_split(left, right, dims=NN):
    return dot(left[0], right[0], dims) + (dot(left[0], right[1], dims) + dot(left[1], right[0], dims))


def rows_at(index, size):
    return pl.ds(pl.multiple_of(index * size, size), size)


def hot(iota, entries):
    return jnp.where(iota == entries, 1.0, 0.0).astype(BF16)


def tiles_kernel(
    row_ref,
    col_ref,
    rel_ref,
    weights_ref,
    feats_any,
    cot_any,
    forward_any,
    backward_any,
    counted_any,
    grad_any,
    mixed_ref,
    sums_ref,
    forward_ref,
    backward_ref,
    counted_ref,
    feats_ref,
    cot_ref,
    turned_ref,
    rel_pad_ref,
    totals_ref,
    counts_ref,
    high_ref,
    low_ref,
    count_high_ref,
    grad_ref,
    self_rel_ref,
    self_sum_ref,
    sems,
):
    slots = forward_ref.shape[0]
    dst_dev, src_dev = cot_ref.shape[0], feats_ref.shape[0]
    blocks, source_blocks = dst_dev // TILE, src_dev // TILE
    rels_all = rel_ref.shape[0]
    col_index = row_ref[0] // blocks
    row_index = col_ref[0] // source_blocks
    ahead = col_index * blocks - row_index * source_blocks
    owner = (ahead >= 0) & (ahead < source_blocks)
    load_cot = pltpu.make_async_copy(cot_any, cot_ref, sems.at[0])
    load_feats = pltpu.make_async_copy(feats_any, feats_ref, sems.at[1])
    load_cot.start()
    load_feats.start()

    chunk = slots // CHUNKS
    loads = []
    for part in range(CHUNKS):
        here = pl.ds(part * chunk, chunk)
        for which, (src, dst) in enumerate(
            ((forward_any, forward_ref), (backward_any, backward_ref), (counted_any, counted_ref))
        ):
            copy = pltpu.make_async_copy(src.at[here], dst.at[here], sems.at[6 + 3 * part + which])
            copy.start()
            loads.append(copy)
    rel_pad_ref[...] = jnp.zeros_like(rel_pad_ref)
    rel_pad_ref[pl.ds(0, rels_all), :] = rel_ref[...]
    weight = [split(weights_ref[which]) for which in range(3)]

    def clear_block(block, _):
        grad_ref[rows_at(block, PAIR), :] = jnp.zeros((PAIR, D), F32)
        return 0

    lax.fori_loop(0, src_dev // PAIR, clear_block, 0)
    sums_ref[pl.ds(2 * D, D), :] = jnp.zeros((D, D), F32)
    self_rel_ref[...] = jnp.zeros_like(self_rel_ref)
    load_cot.wait()

    def image_block(block, _):
        here = rows_at(block, WIDE)
        cot = cot_ref[here, :]
        turned_ref[:, here] = cot.T
        for which in range(2):
            high, low = split(dot_exact_left(cot, weight[which], NT))
            for sub in range(WIDE // TILE):
                first = (block * (WIDE // TILE) + sub) * PAIR + which * TILE
                part = pl.ds(pl.multiple_of(first, TILE), TILE)
                high_ref[part, :] = high[sub * TILE : (sub + 1) * TILE]
                low_ref[part, :] = low[sub * TILE : (sub + 1) * TILE]
        totals_ref[rows_at(block, 2 * WIDE), :] = jnp.zeros((2 * WIDE, D), F32)
        counts_ref[rows_at(block, 2 * WIDE), :] = jnp.zeros((2 * WIDE, RELS_PAD), F32)
        mixed_ref[here, :] = jnp.zeros((WIDE, D), F32)
        return 0

    lax.fori_loop(0, dst_dev // WIDE, image_block, 0, unroll=True)

    @pl.when(owner)
    def _():
        def self_image(block, total):
            cot = cot_ref[rows_at(block, WIDE), :]
            grad_ref[pl.ds(pl.multiple_of(ahead * TILE + block * WIDE, TILE), WIDE), :] = dot_exact_left(
                cot, weight[2], NT
            )
            return total + jnp.sum(cot.astype(F32).reshape(WIDE // 8, 8, D), axis=0)

        self_sum_ref[...] = lax.fori_loop(0, dst_dev // WIDE, self_image, jnp.zeros((8, D), F32), unroll=True)

    load_feats.wait()

    @pl.when(owner)
    def _():
        own_rel = split(jnp.broadcast_to(rel_ref[pl.ds(rels_all - 1, 1), :], (8, D)))
        rel_image = dot_split(own_rel, weight[2])[:1]

        def self_block(block, _):
            there = pl.ds(pl.multiple_of(ahead * TILE + block * WIDE, TILE), WIDE)
            mixed_ref[rows_at(block, WIDE), :] = dot_exact_left(feats_ref[there, :], weight[2]) - rel_image
            return 0

        lax.fori_loop(0, dst_dev // WIDE, self_block, 0, unroll=True)
        there = pl.ds(pl.multiple_of(ahead * TILE, TILE), dst_dev)
        own_sum = split(self_sum_ref[...])
        sums_ref[pl.ds(2 * D, D), :] = dot(turned_ref[...], feats_ref[there, :]).T - dot_split(own_rel, own_sum, TN)
        self_rel_ref[...] = dot_split(own_sum, weight[2], NT)

    def tile(slot, _):
        row = rows_at(row_ref[slot] % blocks, PAIR)
        col = rows_at(col_ref[slot] % source_blocks, TILE)
        backward = backward_ref[slot]
        totals_ref[row, :] += dot(forward_ref[slot], feats_ref[col, :])
        counts_ref[row, :] += counted_ref[slot].astype(F32)
        grad_ref[col, :] += dot(backward, high_ref[row, :]) + dot(backward, low_ref[row, :])
        return 0

    for part in range(CHUNKS):
        for copy in loads[3 * part : 3 * part + 3]:
            copy.wait()
        lax.fori_loop(part * chunk, (part + 1) * chunk, tile, 0, unroll=True)

    stores = []
    for part in range(4):
        here = pl.ds(part * (src_dev // 4), src_dev // 4)
        copy = pltpu.make_async_copy(grad_ref.at[here, :], grad_any.at[here, :], sems.at[2 + part])
        copy.start()
        stores.append(copy)

    relations = split(rel_pad_ref[...])

    def most(block, value):
        counts = counts_ref[rows_at(block, PAIR), :]
        return jnp.maximum(value, jnp.max(counts.reshape(PAIR // 8, 8, RELS_PAD), axis=0))

    largest = jnp.max(lax.fori_loop(0, blocks, most, jnp.zeros((8, RELS_PAD), F32)))
    large = largest > 256.0

    @pl.when(large)
    def _():
        def low_block(block, _):
            at = rows_at(block, PAIR)
            low = split(counts_ref[at, :])[1]
            totals_ref[at, :] -= dot(low, relations[0]) + dot(low, relations[1])
            return 0

        lax.fori_loop(0, blocks, low_block, 0)

    def relate_block(block, _):
        at = rows_at(block, WIDE)
        counts = counts_ref[at, :].astype(BF16)
        totals = totals_ref[at, :] - (dot(counts, relations[0]) + dot(counts, relations[1]))
        high, low = split(totals)
        for sub in range(WIDE // PAIR):
            here = rows_at(block * (WIDE // PAIR) + sub, TILE)
            for which in range(2):
                first = sub * PAIR + which * TILE
                there = pl.ds(
                    pl.multiple_of(which * dst_dev + (block * (WIDE // PAIR) + sub) * TILE, TILE), TILE
                )
                high_ref[there, :] = high[first : first + TILE]
                low_ref[there, :] = low[first : first + TILE]
                count_high_ref[which, here, :] = counts[first : first + TILE]
        return 0

    lax.fori_loop(0, 2 * dst_dev // WIDE, relate_block, 0, unroll=True)

    def mix_block(block, _):
        here = rows_at(block, WIDE)
        parts = []
        for which in range(2):
            there = pl.ds(pl.multiple_of(which * dst_dev + block * WIDE, WIDE), WIDE)
            parts.append(dot_split((high_ref[there, :], low_ref[there, :]), weight[which]))
        mixed_ref[here, :] += parts[0] + parts[1]
        return 0

    lax.fori_loop(0, dst_dev // WIDE, mix_block, 0, unroll=True)

    turned = turned_ref[...]
    grad_rel = jnp.zeros((D, RELS_PAD), F32)
    met = [dot(turned, count_high_ref[which]) for which in range(2)]
    for which in range(2):
        there = pl.ds(which * dst_dev, dst_dev)
        product = dot(turned, high_ref[there, :]) + dot(turned, low_ref[there, :])
        sums_ref[pl.ds(which * D, D), :] = product.T
        grad_rel -= dot_split(weight[which], split(met[which]))
    sums_ref[pl.ds(3 * D, RELS_PAD), :] = grad_rel.T

    @pl.when(large)
    def _():
        def low_block(block, _):
            cot = cot_ref[rows_at(block, TILE), :]
            counts = counts_ref[rows_at(block, PAIR), :]
            for which in range(2):
                low = split(counts[which * TILE : (which + 1) * TILE])[1]
                part = split(dot(low, cot, TN))
                sums_ref[pl.ds(3 * D, RELS_PAD), :] -= dot_split(part, weight[which], NT)
            return 0

        lax.fori_loop(0, blocks, low_block, 0)

    sums_ref[pl.ds(3 * D + rels_all - 1, 1), :] -= jnp.sum(self_rel_ref[...], axis=0, keepdims=True)

    for copy in stores:
        copy.wait()


def tiles_call(rows, cols, rel, weights, sources, cot, forward, backward, counted):
    dst_dev, src_dev = cot.shape[0], sources.shape[0]
    smem = pl.BlockSpec(memory_space=pltpu.SMEM)
    vmem = pl.BlockSpec(memory_space=pltpu.VMEM)
    anywhere = pl.BlockSpec(memory_space=pl.ANY)
    return pl.pallas_call(
        tiles_kernel,
        out_shape=[
            jax.ShapeDtypeStruct((src_dev, D), F32),
            jax.ShapeDtypeStruct((dst_dev, D), F32),
            jax.ShapeDtypeStruct((3 * D + RELS_PAD, D), F32),
        ],
        in_specs=[smem] * 2 + [vmem] * 2 + [anywhere] * 5,
        out_specs=[anywhere, vmem, vmem],
        scratch_shapes=[
            pltpu.VMEM(forward.shape, BF16),
            pltpu.VMEM(backward.shape, BF16),
            pltpu.VMEM(counted.shape, BF16),
            pltpu.VMEM((src_dev, D), BF16),
            pltpu.VMEM((dst_dev, D), BF16),
            pltpu.VMEM((D, dst_dev), BF16),
            pltpu.VMEM((RELS_PAD, D), F32),
            pltpu.VMEM((2 * dst_dev, D), F32),
            pltpu.VMEM((2 * dst_dev, RELS_PAD), F32),
            pltpu.VMEM((2 * dst_dev, D), BF16),
            pltpu.VMEM((2 * dst_dev, D), BF16),
            pltpu.VMEM((2, dst_dev, RELS_PAD), BF16),
            pltpu.VMEM((src_dev, D), F32),
            pltpu.VMEM((8, D), F32),
            pltpu.VMEM((8, D), F32),
            pltpu.SemaphoreType.DMA((6 + 3 * CHUNKS,)),
        ],
        compiler_params=pltpu.CompilerParams(vmem_limit_bytes=TILES_VMEM),
        name="tiles",
    )(rows, cols, rel, weights, sources, cot, forward, backward, counted)


MESH = pl.DeviceIdType.MESH
RING = 4
HALF = TILE


class Copies:
    def __init__(self, send_sems):
        self.send_sems, self.started = send_sems, []

    def start(self, src, dst, recv, peer):
        copy = pltpu.make_async_remote_copy(
            src_ref=src,
            dst_ref=dst,
            send_sem=self.send_sems.at[len(self.started)],
            recv_sem=recv,
            device_id=peer,
            device_id_type=MESH,
        )
        copy.start()
        self.started.append(copy)

    def received(self, dst, recv):
        pltpu.make_async_remote_copy(
            src_ref=dst,
            dst_ref=dst,
            send_sem=self.send_sems.at[0],
            recv_sem=recv,
            device_id=self.any_peer,
            device_id_type=MESH,
        ).wait_recv()

    def finish(self):
        for copy in self.started:
            copy.wait_send()


class Place:
    def __init__(self):
        self.row = lax.axis_index("row")
        self.col = lax.axis_index("col")
        self.core = self.col % 2
        self.stride1 = 8 - 6 * self.core
        self.stride2 = 10 - self.stride1
        self.p1 = self.col // self.stride1 % RING
        self.p2 = self.col // self.stride2 % RING

    def col_at(self, k1, k2):
        return (self.p1 + k1) % RING * self.stride1 + (self.p2 + k2) % RING * self.stride2 + self.core

    def peer(self, k1, k2):
        return (self.row, self.col_at(k1, k2))

    def partner(self):
        return (self.row, self.col + 1 - 2 * self.core)

    def along_row(self, k, rows):
        return ((self.row + k) % rows, self.col)

    def greet(self, peers):
        barrier = pltpu.get_barrier_semaphore()
        for peer in peers:
            pl.semaphore_signal(barrier, inc=1, device_id=peer, device_id_type=MESH)
        pl.semaphore_wait(barrier, len(peers))


def run_in_order(pipes, order):
    for name in order:
        next(pipes[name], None)
    for pipe in pipes.values():
        for _ in pipe:
            pass


def gather_kernel(
    rows,
    live_ref,
    count_ref,
    ends_ref,
    relation_ref,
    dir_ref,
    feats_ref,
    cot_ref,
    sources_ref,
    targets_ref,
    forward_any,
    backward_any,
    counted_any,
    forward_ref,
    backward_ref,
    counted_ref,
    send_sems,
    shard_sems,
    row_sems,
    own_sems,
    tile_sems,
):
    place = Place()
    copies = Copies(send_sems)
    copies.any_peer = place.partner()
    own_copies = [
        pltpu.make_async_copy(feats_ref, sources_ref.at[place.col], own_sems.at[0]),
        pltpu.make_async_copy(cot_ref, targets_ref.at[place.row], own_sems.at[1]),
    ]
    for copy in own_copies:
        copy.start()
    place.greet(
        [place.partner()]
        + [place.peer(k, 0) for k in (1, 3)]
        + [place.peer(0, k) for k in (1, 3)]
        + [place.along_row(k, rows) for k in (1, rows - 1)]
    )
    parts = [pl.ds(0, HALF), pl.ds(HALF, HALF)]

    def send(array, sems, count, index, peer, half=None, src=None):
        here = array.at[index] if half is None else array.at[index, parts[half]]
        sem = sems.at[2 * count + index] if half is None else sems.at[2 * index + half]
        copies.start(here if src is None else src, here, sem, peer)

    def got(array, sems, count, index, halves=False):
        if halves:
            for half in range(2):
                copies.received(array.at[index, parts[half]], sems.at[2 * index + half])
        else:
            copies.received(array.at[index], sems.at[2 * count + index])

    send_shard = functools.partial(send, sources_ref, shard_sems, 2 * RING * RING)
    got_shard = functools.partial(got, sources_ref, shard_sems, 2 * RING * RING)
    send_row = functools.partial(send, targets_ref, row_sems, rows)
    got_row = functools.partial(got, targets_ref, row_sems, rows)

    def feats_pipe():
        for peer in (place.peer(1, 0), place.peer(3, 0), place.peer(0, 1), place.peer(0, 3), place.partner()):
            send_shard(place.col, peer, src=feats_ref)
        yield

        def spread(b):
            for peer in (place.peer(0, 1), place.peer(0, 3), place.partner()):
                send_shard(b, peer)

        left, right, far = place.col_at(3, 0), place.col_at(1, 0), place.col_at(2, 0)
        got_shard(left)
        send_shard(left, place.peer(1, 0), 0)
        spread(left)
        got_shard(right)
        send_shard(right, place.peer(3, 0), 1)
        spread(right)
        yield

        def second(k1):
            below, above = place.col_at(k1, 3), place.col_at(k1, 1)
            got_shard(below)
            send_shard(below, place.peer(0, 1), 0)
            got_shard(above)
            send_shard(above, place.peer(0, 3), 1)
            send_shard(below, place.partner())
            send_shard(above, place.partner())

        second(0)
        yield
        got_shard(far, halves=True)
        spread(far)
        yield
        second(3)
        yield
        second(1)
        yield
        second(2)
        yield
        for k1 in (0, 3, 1, 2):
            b = place.col_at(k1, 2)
            got_shard(b, halves=True)
            send_shard(b, place.partner())
        yield
        for k1 in range(RING):
            for k2 in range(RING):
                got_shard(place.col_at(k1, k2) + 1 - 2 * place.core)

    def cot_pipe():
        after, before = place.along_row(1, rows), place.along_row(rows - 1, rows)
        send_row(place.row, after, src=cot_ref)
        send_row(place.row, before, src=cot_ref)
        yield
        for k in range(1, rows // 2):
            last = k == rows // 2 - 1
            low, high = (place.row + rows - k) % rows, (place.row + k) % rows
            got_row(low)
            send_row(low, after, 0 if last else None)
            got_row(high)
            send_row(high, before, 1 if last else None)
            yield
        got_row((place.row + rows // 2) % rows, halves=True)

    pair_iota = lax.broadcasted_iota(jnp.int32, (PAIR, EDGE_TILE), 0)
    tile_iota = lax.broadcasted_iota(jnp.int32, (TILE, EDGE_TILE), 0)
    edge_iota = lax.broadcasted_iota(jnp.int32, (1, EDGE_TILE), 1)
    tile_copies = []

    def tile(slot, _):
        at = pl.ds(slot, 1)
        edges = jnp.where(slot < live_ref[0], count_ref[slot], 0)
        ends = ends_ref[at, :]
        key = dir_ref[at, :] * TILE + lax.shift_right_logical(ends, 7)
        hot_dst = hot(pair_iota, jnp.where(edge_iota < edges, key, NONE))
        hot_src = hot(tile_iota, ends & (TILE - 1))
        hot_rel = hot(pair_iota, relation_ref[at, :])
        forward_ref[slot] = dot(hot_dst, hot_src, NT).astype(BF16)
        backward_ref[slot] = dot(hot_src, hot_dst, NT).astype(BF16)
        counted_ref[slot] = dot(hot_dst, hot_rel, NT).astype(BF16)
        return 0

    def tiles_pipe():
        chunk = ends_ref.shape[0] // PREPARED
        for part in range(PREPARED):
            lax.fori_loop(part * chunk, (part + 1) * chunk, tile, 0, unroll=2)
            here = pl.ds(part * chunk, chunk)
            for which, (src, dst) in enumerate(
                ((forward_ref, forward_any), (backward_ref, backward_any), (counted_ref, counted_any))
            ):
                copy = pltpu.make_async_copy(src.at[here], dst.at[here], tile_sems.at[3 * part + which])
                copy.start()
                tile_copies.append(copy)
            yield

    run_in_order({"f": feats_pipe(), "c": cot_pipe(), "p": tiles_pipe()}, "fcppppfpfcpfppcfppfpcfpppfppcff")
    for copy in tile_copies:
        copy.wait()
    for copy in own_copies:
        copy.wait()
    copies.finish()


def gather_call(live, counts, ends, relation, direction, feats, cot, rows, cols):
    anywhere = pl.BlockSpec(memory_space=pl.ANY)
    smem = pl.BlockSpec(memory_space=pltpu.SMEM)
    vmem = pl.BlockSpec(memory_space=pltpu.VMEM)
    slots = ends.shape[0]
    shapes = [(slots, PAIR, TILE), (slots, TILE, PAIR), (slots, PAIR, RELS_PAD)]
    sources, targets, *tiles = pl.pallas_call(
        functools.partial(gather_kernel, rows),
        out_shape=[
            jax.ShapeDtypeStruct((cols,) + feats.shape, feats.dtype),
            jax.ShapeDtypeStruct((rows,) + cot.shape, cot.dtype),
        ]
        + [jax.ShapeDtypeStruct(shape, BF16) for shape in shapes],
        in_specs=[smem] * 2 + [vmem] * 3 + [anywhere] * 2,
        out_specs=[anywhere] * 5,
        scratch_shapes=[pltpu.VMEM(shape, BF16) for shape in shapes]
        + [
            pltpu.SemaphoreType.DMA((64,)),
            pltpu.SemaphoreType.DMA((3 * cols,)),
            pltpu.SemaphoreType.DMA((3 * rows,)),
            pltpu.SemaphoreType.DMA((2,)),
            pltpu.SemaphoreType.DMA((3 * PREPARED,)),
        ],
        compiler_params=pltpu.CompilerParams(
            collective_id=0, has_side_effects=True, vmem_limit_bytes=GATHER_VMEM
        ),
        name="gather",
    )(live, counts, ends, relation, direction, feats, cot)
    return [sources.reshape(-1, D), targets.reshape(-1, D)] + tiles


def reduce_kernel(
    rows,
    grad_any,
    mixed_any,
    sums_any,
    grad_out,
    mixed_out,
    sums_out,
    grad_acc,
    mixed_in,
    sums_in,
    pair_in,
    relay1,
    ring1,
    relay2,
    ring2,
    row_up,
    row_down,
    sum_pair,
    sum_first,
    sum_second,
    sum_rows,
    sum_tiles,
    send_sems,
    own_sems,
    pair_sems,
    ring_sems,
    row_sems,
    sum_sems,
    spread_sems,
):
    place = Place()
    copies = Copies(send_sems)
    copies.any_peer = place.partner()
    partner = place.partner()
    core = place.core
    order1 = (2, 1, 3, 0)
    load_sums = pltpu.make_async_copy(sums_any.at[core], sums_in, own_sems.at[16])
    load_mixed = pltpu.make_async_copy(mixed_any, mixed_in, own_sems.at[17])
    load_sums.start()
    load_mixed.start()
    own_copies = {}
    for k in order1:
        for r in (2, 1, 3, 0):
            block = place.col_at(k, r) // 2
            copy = pltpu.make_async_copy(grad_any.at[block, core], grad_acc.at[k, r], own_sems.at[4 * k + r])
            copy.start()
            own_copies[k, r] = copy
    place.greet(
        [partner]
        + [place.peer(k, 0) for k in (1, 2, 3)]
        + [place.peer(0, k) for k in (1, 2, 3)]
        + [place.along_row(k, rows) for k in range(1, rows)]
    )
    low, high = pl.ds(0, HALF), pl.ds(HALF, HALF)

    def grad_pipe():
        for k in order1:
            for r in (2, 1, 3, 0):
                block = ((place.p2 + k) % RING * place.stride2 + (place.p1 + r) % RING * place.stride1) // 2
                copies.start(grad_any.at[block, 1 - core], pair_in.at[k, r], pair_sems.at[4 * k + r], partner)
        yield

        def pair_sum(k, r):
            own_copies[k, r].wait()
            copies.received(pair_in.at[k, r], pair_sems.at[4 * k + r])
            grad_acc[k, r] += pair_in[k, r]

        right, left = place.peer(1, 0), place.peer(3, 0)
        for r in range(RING):
            pair_sum(2, r)
        copies.start(grad_acc.at[2, pl.ds(0, 2)], relay1.at[0], ring_sems.at[0], right)
        copies.start(grad_acc.at[2, pl.ds(2, 2)], relay1.at[1], ring_sems.at[1], left)
        yield
        for r in (2, 3):
            pair_sum(1, r)
        copies.start(grad_acc.at[1, pl.ds(2, 2)], ring1.at[0, pl.ds(2, 2)], ring_sems.at[3], right)
        for r in (0, 1):
            pair_sum(3, r)
        copies.start(grad_acc.at[3, pl.ds(0, 2)], ring1.at[1, pl.ds(0, 2)], ring_sems.at[4], left)
        yield
        for r in (0, 1):
            pair_sum(1, r)
        for r in (2, 3):
            pair_sum(3, r)
        for r in range(RING):
            pair_sum(0, r)
        yield
        copies.received(relay1.at[0], ring_sems.at[0])
        for r in (0, 1):
            grad_acc[1, r] += relay1[0, r]
        copies.start(grad_acc.at[1, pl.ds(0, 2)], ring1.at[0, pl.ds(0, 2)], ring_sems.at[2], right)
        copies.received(relay1.at[1], ring_sems.at[1])
        for r in (0, 1):
            grad_acc[3, 2 + r] += relay1[1, r]
        copies.start(grad_acc.at[3, pl.ds(2, 2)], ring1.at[1, pl.ds(2, 2)], ring_sems.at[5], left)
        yield
        copies.received(ring1.at[0, pl.ds(2, 2)], ring_sems.at[3])
        copies.received(ring1.at[1, pl.ds(0, 2)], ring_sems.at[4])
        for r in (2, 3):
            grad_acc[0, r] += ring1[0, r]
        for r in (0, 1):
            grad_acc[0, r] += ring1[1, r]
        yield
        up, down = place.peer(0, 1), place.peer(0, 3)
        copies.received(ring1.at[1, pl.ds(2, 2)], ring_sems.at[5])
        grad_acc[0, 2] += ring1[1, 2]
        copies.start(grad_acc.at[0, 2, low], relay2.at[0], ring_sems.at[6], up)
        copies.start(grad_acc.at[0, 2, high], relay2.at[1], ring_sems.at[7], down)
        grad_acc[0, 3] += ring1[1, 3]
        copies.start(grad_acc.at[0, 3, low], ring2.at[1, low], ring_sems.at[10], down)
        copies.received(ring1.at[0, pl.ds(0, 2)], ring_sems.at[2])
        grad_acc[0, 1] += ring1[0, 1]
        copies.start(grad_acc.at[0, 1, high], ring2.at[0, high], ring_sems.at[9], up)
        grad_acc[0, 0] += ring1[0, 0]
        yield
        copies.received(relay2.at[0], ring_sems.at[6])
        grad_acc[0, 1, low] += relay2[0]
        copies.start(grad_acc.at[0, 1, low], ring2.at[0, low], ring_sems.at[8], up)
        copies.received(relay2.at[1], ring_sems.at[7])
        grad_acc[0, 3, high] += relay2[1]
        copies.start(grad_acc.at[0, 3, high], ring2.at[1, high], ring_sems.at[11], down)
        yield
        copies.received(ring2.at[0, high], ring_sems.at[9])
        copies.received(ring2.at[1, low], ring_sems.at[10])
        copies.received(ring2.at[0, low], ring_sems.at[8])
        copies.received(ring2.at[1, high], ring_sems.at[11])
        grad_out[...] = grad_acc[0, 0] + ring2[0] + ring2[1]

    def mixed_pipe():
        after, before = place.along_row(1, rows), place.along_row(rows - 1, rows)
        copies.start(mixed_any.at[(place.row + rows - 1) % rows, low], row_up.at[0], row_sems.at[0], after)
        copies.start(mixed_any.at[(place.row + 1) % rows, high], row_down.at[0], row_sems.at[rows], before)
        yield
        load_mixed.wait()
        for step in range(1, rows):
            copies.received(row_up.at[step - 1], row_sems.at[step - 1])
            row_up[step - 1] += mixed_in[(place.row + 2 * rows - 1 - step) % rows, low]
            if step < rows - 1:
                copies.start(row_up.at[step - 1], row_up.at[step], row_sems.at[step], after)
            copies.received(row_down.at[step - 1], row_sems.at[rows + step - 1])
            row_down[step - 1] += mixed_in[(place.row + 1 + step) % rows, high]
            if step < rows - 1:
                copies.start(row_down.at[step - 1], row_down.at[step], row_sems.at[rows + step], before)
            yield
        mixed_out[low] = row_up[rows - 2]
        mixed_out[high] = row_down[rows - 2]

    def sums_pipe():
        copies.start(sums_any.at[1 - core], sum_pair, sum_sems.at[0], partner)
        yield
        load_sums.wait()
        copies.received(sum_pair, sum_sems.at[0])
        for q in range(RING):
            sum_pair[q] += sums_in[q]
        for k in (2, 1, 3):
            copies.start(sum_pair.at[(place.p1 + k) % RING], sum_first.at[k], sum_sems.at[k], place.peer(k, 0))
        sum_first[0] = sum_pair[place.p1]
        yield
        for k in (1, 3, 2):
            copies.received(sum_first.at[k], sum_sems.at[k])
            sum_first[0] += sum_first[k]
        for k in (2, 1, 3):
            copies.start(sum_first.at[0, (place.p2 + k) % RING], sum_second.at[k], sum_sems.at[3 + k], place.peer(0, k))
        sum_second[0] = sum_first[0, place.p2]
        yield
        for k in (1, 3, 2):
            copies.received(sum_second.at[k], sum_sems.at[3 + k])
            sum_second[0] += sum_second[k]
        for quarter in range(RING):
            for side in range(2):
                sum_tiles[2 * quarter + side] = sum_second[0, pl.ds(8 * quarter, 8), pl.ds(TILE * side, TILE)]
        for k in (4, 3, 5, 2, 6, 1, 7):
            copies.start(
                sum_tiles.at[(place.row + k) % rows], sum_rows.at[k], sum_sems.at[6 + k], place.along_row(k, rows)
            )
        sum_rows[0] = sum_tiles[place.row]
        yield
        for k in (1, 7, 2, 6, 3, 5, 4):
            copies.received(sum_rows.at[k], sum_sems.at[6 + k])
            sum_rows[0] += sum_rows[k]
        for k in (4, 3, 5, 2, 6, 1, 7):
            copies.start(
                sum_rows.at[0], sum_tiles.at[rows + place.row], sum_sems.at[13 + k], place.along_row(k, rows)
            )
        sum_tiles[rows + place.row] = sum_rows[0]
        yield
        for k in (1, 7, 2, 6, 3, 5, 4):
            copies.received(sum_tiles.at[rows + (place.row + rows - k) % rows], sum_sems.at[13 + k])
        own = sums_out.at[core, place.p1, place.p2]
        for quarter in range(RING):
            for side in range(2):
                own[pl.ds(8 * quarter, 8), pl.ds(TILE * side, TILE)] = sum_tiles[rows + 2 * quarter + side]
        for k in (2, 1, 3):
            copies.start(own, own, spread_sems.at[k], place.peer(0, k))
        yield
        for k in (1, 3, 2):
            copies.received(sums_out.at[core, place.p1, (place.p2 + RING - k) % RING], spread_sems.at[k])
        line = sums_out.at[core, place.p1]
        for k in (2, 1, 3):
            copies.start(line, line, spread_sems.at[3 + k], place.peer(k, 0))
        yield
        copies.start(line, line, spread_sems.at[7], partner)
        for k in (1, 3, 2):
            there = sums_out.at[core, (place.p1 + RING - k) % RING]
            copies.received(there, spread_sems.at[3 + k])
            copies.start(there, there, spread_sems.at[7 + k], partner)
        yield
        copies.received(sums_out.at[1 - core, place.p2], spread_sems.at[7])
        for k in (1, 3, 2):
            copies.received(sums_out.at[1 - core, (place.p2 + RING - k) % RING], spread_sems.at[7 + k])

    run_in_order(
        {"s": sums_pipe(), "m": mixed_pipe(), "g": grad_pipe()},
        "sgmsgmsgmsgmsgmsgmsgmsgmgg",
    )
    copies.finish()


def reduce_call(grad, mixed, sums, rows, cols):
    anywhere = pl.BlockSpec(memory_space=pl.ANY)
    vmem = pl.BlockSpec(memory_space=pltpu.VMEM)
    ent_dev = grad.shape[0] // cols
    block = (ent_dev, D)
    share = sums.shape[0] // cols
    grad_out, mixed_out, sums_out = pl.pallas_call(
        functools.partial(reduce_kernel, rows),
        out_shape=[
            jax.ShapeDtypeStruct(block, F32),
            jax.ShapeDtypeStruct(block, F32),
            jax.ShapeDtypeStruct((2, RING, RING, share, D), F32),
        ],
        in_specs=[anywhere] * 3,
        out_specs=[vmem] * 3,
        scratch_shapes=[
            pltpu.VMEM((RING, RING) + block, F32),
            pltpu.VMEM((rows,) + block, F32),
            pltpu.VMEM((RING, RING, share, D), F32),
            pltpu.VMEM((RING, RING) + block, F32),
            pltpu.VMEM((2, 2) + block, F32),
            pltpu.VMEM((2, RING) + block, F32),
            pltpu.VMEM((2, HALF, D), F32),
            pltpu.VMEM((2,) + block, F32),
            pltpu.VMEM((rows - 1, HALF, D), F32),
            pltpu.VMEM((rows - 1, HALF, D), F32),
            pltpu.VMEM((RING, RING, share, D), F32),
            pltpu.VMEM((RING, RING, share, D), F32),
            pltpu.VMEM((RING, share, D), F32),
            pltpu.VMEM((rows, 8, TILE), F32),
            pltpu.VMEM((2 * rows, 8, TILE), F32),
            pltpu.SemaphoreType.DMA((96,)),
            pltpu.SemaphoreType.DMA((18,)),
            pltpu.SemaphoreType.DMA((16,)),
            pltpu.SemaphoreType.DMA((12,)),
            pltpu.SemaphoreType.DMA((2 * rows,)),
            pltpu.SemaphoreType.DMA((24,)),
            pltpu.SemaphoreType.DMA((16,)),
        ],
        compiler_params=pltpu.CompilerParams(
            collective_id=1, has_side_effects=True, vmem_limit_bytes=REDUCE_VMEM
        ),
        name="reduce",
    )(
        grad.reshape((cols // 2, 2) + block),
        mixed.reshape((rows,) + block),
        sums.reshape(2, RING, RING, share, D),
    )
    return grad_out, mixed_out, sums_out.reshape(-1, D)


def place_kernel(grad_in, mixed_in, sums_in, mixed_out, grad_out, grad_rel_out, grad_weights_out, rel_ref, sems):
    rels_all = grad_rel_out.shape[0]
    pairs = [(sums_in.at[pl.ds(3 * D, RELS_PAD)], rel_ref), (mixed_in, mixed_out), (grad_in, grad_out)]
    pairs += [(sums_in.at[pl.ds(which * D, D)], grad_weights_out.at[which]) for which in range(3)]
    started = [pltpu.make_async_copy(src, dst, sems.at[index]) for index, (src, dst) in enumerate(pairs)]
    for copy in started:
        copy.start()
    started[0].wait()
    grad_rel_out[...] = rel_ref[pl.ds(0, rels_all), :]
    for copy in started[1:]:
        copy.wait()


def place_call(grad, mixed, sums, rels_all):
    anywhere = pl.BlockSpec(memory_space=pl.ANY)
    return pl.pallas_call(
        place_kernel,
        out_shape=[
            jax.ShapeDtypeStruct(mixed.shape, F32),
            jax.ShapeDtypeStruct(grad.shape, F32),
            jax.ShapeDtypeStruct((rels_all, D), F32),
            jax.ShapeDtypeStruct((3, D, D), F32),
        ],
        in_specs=[anywhere] * 3,
        out_specs=[anywhere, anywhere, pl.BlockSpec(memory_space=pltpu.VMEM), anywhere],
        scratch_shapes=[pltpu.VMEM((RELS_PAD, D), F32), pltpu.SemaphoreType.DMA((6,))],
        compiler_params=pltpu.CompilerParams(vmem_limit_bytes=REDUCE_VMEM),
        name="place",
    )(grad, mixed, sums)


def shards(
    feats,
    rel_embed,
    weights,
    cot,
    tile_row,
    tile_col,
    tile_live,
    edge_ends,
    edge_relation,
    edge_dir,
    edge_count,
):
    rows_n, cols_n = lax.axis_size("row"), lax.axis_size("col")
    sources, targets, *tiles = gather_call(
        tile_live, edge_count, edge_ends, edge_relation, edge_dir, feats, cot, rows_n, cols_n
    )
    grad, mixed, sums = tiles_call(tile_row, tile_col, rel_embed, weights, sources, targets, *tiles)
    grad_feats, mixed, sums = reduce_call(grad, mixed, sums, rows_n, cols_n)
    return place_call(grad_feats, mixed, sums, rel_embed.shape[0])


def solution(mesh):
    return jax.shard_map(
        shards,
        mesh=mesh,
        in_specs=(
            P(("row", "col"), None),
            P(),
            P(),
            P(("col", "row"), None),
            P(("row", "col")),
            P(("row", "col")),
            P(("row", "col")),
            P(("row", "col"), None),
            P(("row", "col"), None),
            P(("row", "col"), None),
            P(("row", "col")),
        ),
        out_specs=(P(("col", "row"), None), P(("row", "col"), None), P(), P()),
        check_vma=False,
    )
```
